32 devices in a mesh: seq: 8 (over y, x, core), res: 4 (over z).
Axes of the slice: x: 2, y: 2, z: 4, core: 2. Of those that a mesh axis runs over, the one named last changes fastest.
Arguments:
- coupled_embedding: float32 [192, 192, 128], P(('res', 'seq')), may hold values from -6 to 6
- aligned_embedding: float32 [16, 192, 256], P('seq', 'res'), may hold values from -6 to 6
- coupled_change_adjoint: float32 [192, 192, 128], P(('res', 'seq')), may hold values from -6 to 6
- aligned_change_adjoint: float32 [16, 192, 256], P('seq', 'res'), may hold values from -6 to 6
- coupled_scaler: float32 [128], replicated, may hold values from 0.25 to 1.75
- coupled_asking_matrix: float32 [128, 128], replicated, may hold values from -24 to 24
- coupled_lookup_matrix: float32 [128, 128], replicated, may hold values from -1 to 1
- coupled_content_matrix: float32 [128, 128], replicated, may hold values from -0.5 to 0.5
- coupled_sigmoid_matrix: float32 [128, 128], replicated, may hold values from -0.5 to 0.5
- coupled_offset_matrix: float32 [128, 4], replicated, may hold values from -1 to 1
- coupled_result_matrix: float32 [128, 128], replicated, may hold values from -0.5 to 0.5
- aligned_scaler: float32 [256], replicated, may hold values from 0.25 to 1.75
- coupled_scaler_for_offset: float32 [128], replicated, may hold values from 0.25 to 1.75
- aligned_asking_matrix: float32 [256, 256], replicated, may hold values from -24 to 24
- aligned_lookup_matrix: float32 [256, 256], replicated, may hold values from -1 to 1
- aligned_content_matrix: float32 [256, 256], replicated, may hold values from -0.375 to 0.375
- aligned_sigmoid_matrix: float32 [256, 256], replicated, may hold values from -0.375 to 0.375
- aligned_offset_matrix: float32 [128, 8], replicated, may hold values from -1 to 1
- aligned_result_matrix: float32 [256, 256], replicated, may hold values from -0.375 to 0.375
Outputs:
- coupled_embedding_sensitivity: float32 [192, 192, 128], P(('res', 'seq'))
- aligned_embedding_sensitivity: float32 [16, 192, 256], P('seq', 'res')
The draws below stay inside these ranges and needn't reach their ends.
All inputs are finite; a program needn't handle non-finite values.
Results may differ from the reference program's by a relative error of at most 0.0003.
Values sent between devices are 32-bit elements; how exact they have to be, the bound alone decides.
No kernel may reach another device: no remote copies, remote signals or barrier semaphores. Data moves between devices by JAX's collectives and lax.ppermute only.
A program may use at most 192 MiB of HBM per device.

```python
import math
import jax
import jax.numpy as jnp
from jax import lax

COUPLED_FEATURES = 128
ALIGNED_FEATURES = 256
HP = 4
ALIGNED_SPLITS = 8
SUBSPACE_WIDTH = 32
CHAIN_LENGTH = 192
ALIGNED_DEPTH = 16


def lookup_matrix(key, fan_in, columns):
    return jax.random.normal(jax.random.fold_in(key, 7), (fan_in, columns), jnp.float32) / math.sqrt(fan_in)


def asking_matrix(key, fan_in, columns):
    fresh = jax.random.normal(jax.random.fold_in(key, 9), (fan_in, columns), jnp.float32) / math.sqrt(fan_in)
    return fresh


def draw_coupled_lookup_matrix(key, part):
    return lookup_matrix(key, COUPLED_FEATURES, HP * SUBSPACE_WIDTH)


def draw_coupled_asking_matrix(key, part):
    return asking_matrix(key, COUPLED_FEATURES, HP * SUBSPACE_WIDTH)


def draw_aligned_lookup_matrix(key, part):
    return lookup_matrix(key, ALIGNED_FEATURES, ALIGNED_SPLITS * SUBSPACE_WIDTH)


def draw_aligned_asking_matrix(key, part):
    return asking_matrix(key, ALIGNED_FEATURES, ALIGNED_SPLITS * SUBSPACE_WIDTH)


def block_levels(key, extent, cuts, smallest, high):
    loudness = 1.0
    for dim, parts in cuts:
        draws = jax.random.uniform(jax.random.fold_in(jax.random.fold_in(key, 6), dim), (parts,), jnp.float32, smallest / len(cuts), high / len(cuts))
        loudness = loudness * jnp.repeat(jnp.exp(draws), extent[dim] // parts).reshape((-1,) + (1,) * (len(extent) - 1 - dim))
    return loudness


def scatter_about(stream_key, shape, deviation, reach, shards=(), kind=jnp.bfloat16):
    result = jax.random.normal(stream_key, shape, jnp.float32) * deviation
    if len(shards) > 0:
        result = block_levels(stream_key, shape, shards, -0.22, 0.18) * result
    return jnp.clip(result, min=-reach, max=reach).astype(kind)


def setup_inputs(seed: int = 0) -> dict:
    streams_of = jax.random.split(jax.random.key(seed), 20)
    return {
        "coupled_embedding": scatter_about(streams_of[0], (CHAIN_LENGTH, CHAIN_LENGTH, COUPLED_FEATURES), 1.0, 6.0, ((0, 32),), jnp.float32),
        "aligned_embedding": scatter_about(streams_of[1], (ALIGNED_DEPTH, CHAIN_LENGTH, ALIGNED_FEATURES), 1.0, 6.0, ((0, 8), (1, 4)), jnp.float32),
        "coupled_change_adjoint": scatter_about(streams_of[2], (CHAIN_LENGTH, CHAIN_LENGTH, COUPLED_FEATURES), 1.0, 6.0, ((0, 32),), jnp.float32),
        "aligned_change_adjoint": scatter_about(streams_of[3], (ALIGNED_DEPTH, CHAIN_LENGTH, ALIGNED_FEATURES), 1.0, 6.0, ((0, 8), (1, 4)), jnp.float32),
        "coupled_scaler": jnp.clip(1.0 + 0.15 * jax.random.normal(streams_of[4], (COUPLED_FEATURES,), jnp.float32), 0.25, 1.75),
        "coupled_asking_matrix": draw_coupled_asking_matrix(jax.random.fold_in(streams_of[19], 71), 0),
        "coupled_lookup_matrix": draw_coupled_lookup_matrix(jax.random.fold_in(streams_of[19], 71), 0),
        "coupled_content_matrix": scatter_about(streams_of[7], (COUPLED_FEATURES, HP * SUBSPACE_WIDTH), COUPLED_FEATURES ** -0.5, 0.5, (), jnp.float32),
        "coupled_sigmoid_matrix": scatter_about(streams_of[8], (COUPLED_FEATURES, HP * SUBSPACE_WIDTH), COUPLED_FEATURES ** -0.5, 0.5, (), jnp.float32),
        "coupled_offset_matrix": scatter_about(streams_of[9], (COUPLED_FEATURES, HP), (COUPLED_FEATURES // 4) ** -0.5, 1.0, (), jnp.float32),
        "coupled_result_matrix": scatter_about(streams_of[10], (HP * SUBSPACE_WIDTH, COUPLED_FEATURES), (HP * SUBSPACE_WIDTH) ** -0.5, 0.5, (), jnp.float32),
        "aligned_scaler": jnp.clip(1.0 + 0.15 * jax.random.normal(streams_of[11], (ALIGNED_FEATURES,), jnp.float32), 0.25, 1.75),
        "coupled_scaler_for_offset": jnp.clip(1.0 + 0.15 * jax.random.normal(streams_of[12], (COUPLED_FEATURES,), jnp.float32), 0.25, 1.75),
        "aligned_asking_matrix": draw_aligned_asking_matrix(jax.random.fold_in(streams_of[19], 71), 0),
        "aligned_lookup_matrix": draw_aligned_lookup_matrix(jax.random.fold_in(streams_of[19], 71), 0),
        "aligned_content_matrix": scatter_about(streams_of[15], (ALIGNED_FEATURES, ALIGNED_SPLITS * SUBSPACE_WIDTH), ALIGNED_FEATURES ** -0.5, 0.375, (), jnp.float32),
        "aligned_sigmoid_matrix": scatter_about(streams_of[16], (ALIGNED_FEATURES, ALIGNED_SPLITS * SUBSPACE_WIDTH), ALIGNED_FEATURES ** -0.5, 0.375, (), jnp.float32),
        "aligned_offset_matrix": scatter_about(streams_of[17], (COUPLED_FEATURES, ALIGNED_SPLITS), (COUPLED_FEATURES // 4) ** -0.5, 1.0, (), jnp.float32),
        "aligned_result_matrix": scatter_about(streams_of[18], (ALIGNED_SPLITS * SUBSPACE_WIDTH, ALIGNED_FEATURES), (ALIGNED_SPLITS * SUBSPACE_WIDTH) ** -0.5, 0.375, (), jnp.float32),
    }


EXACT_MATMUL = lax.Precision.HIGHEST
EPSILON = 1e-05

def standardize_features(values, norm_gain):
    center = values - lax.optimization_barrier(jnp.mean(values, axis=-1, keepdims=True))
    spread = lax.optimization_barrier(jnp.mean(center * center, axis=-1, keepdims=True))
    return center * lax.rsqrt(spread + EPSILON) * norm_gain

def affine_map(values, weight):
    return jnp.einsum('...c,ce->...e', values, weight, precision=EXACT_MATMUL)

def sigmoid_mixing(query_vectors, key_rows, value_rows, gate_preact, softmax_offset, head_count):
    query_shape = query_vectors.shape
    head_width = query_shape[-1] // head_count
    query_heads = query_vectors.reshape(query_shape[:-1] + (head_count, head_width))
    key_heads = key_rows.reshape(key_rows.shape[:-1] + (head_count, head_width))
    value_heads = value_rows.reshape(value_rows.shape[:-1] + (head_count, head_width))
    logits = jnp.einsum('...qhd,...khd->...qhk', query_heads, key_heads, precision=EXACT_MATMUL) / math.sqrt(head_width) + softmax_offset
    largest = lax.stop_gradient(lax.optimization_barrier(jnp.max(logits, axis=-1, keepdims=True)))
    weights = jnp.exp(logits - largest)
    weights = weights / lax.optimization_barrier(jnp.sum(weights, axis=-1, keepdims=True))
    mixed_contents = jnp.einsum('...qhk,...khd->...qhd', weights, value_heads, precision=EXACT_MATMUL)
    return mixed_contents.reshape(query_shape) * jax.nn.sigmoid(gate_preact)

def reference(coupled_embedding, aligned_embedding, coupled_change_adjoint, aligned_change_adjoint, coupled_scaler, coupled_asking_matrix, coupled_lookup_matrix, coupled_content_matrix, coupled_sigmoid_matrix, coupled_offset_matrix, coupled_result_matrix, aligned_scaler, coupled_scaler_for_offset, aligned_asking_matrix, aligned_lookup_matrix, aligned_content_matrix, aligned_sigmoid_matrix, aligned_offset_matrix, aligned_result_matrix):

    def coupled_mixing_apply(present_carry):
        standardized_source = standardize_features(present_carry, coupled_scaler)
        softmax_offset = jnp.einsum('jkc,ch->jhk', standardized_source, coupled_offset_matrix, precision=EXACT_MATMUL)

        def one_row(row_normed):
            mixed_contents = sigmoid_mixing(affine_map(row_normed, coupled_asking_matrix), affine_map(row_normed, coupled_lookup_matrix), affine_map(row_normed, coupled_content_matrix), affine_map(row_normed, coupled_sigmoid_matrix), softmax_offset, HP)
            return affine_map(mixed_contents, coupled_result_matrix)
        return lax.map(jax.checkpoint(one_row), standardized_source)

    def aligned_mixing_apply(present_carry, entering_lines):
        standardized_source = standardize_features(entering_lines, aligned_scaler)
        softmax_offset = jnp.einsum('gys,sj->gjy', standardize_features(present_carry, coupled_scaler_for_offset), aligned_offset_matrix, precision=EXACT_MATMUL)

        def one_sequence(aligned_standardized):
            mixed_contents = sigmoid_mixing(affine_map(aligned_standardized, aligned_asking_matrix), affine_map(aligned_standardized, aligned_lookup_matrix), affine_map(aligned_standardized, aligned_content_matrix), affine_map(aligned_standardized, aligned_sigmoid_matrix), softmax_offset, ALIGNED_SPLITS)
            return affine_map(mixed_contents, aligned_result_matrix)
        return lax.map(jax.checkpoint(one_sequence), standardized_source)

    def combined_sensitivity(present_carry, entering_lines):
        return (coupled_mixing_apply(present_carry), aligned_mixing_apply(present_carry, entering_lines))
    discarded_entry, trunk_reverse_sweep = jax.vjp(combined_sensitivity, coupled_embedding, aligned_embedding)
    coupled_embedding_sensitivity, aligned_embedding_sensitivity = trunk_reverse_sweep((coupled_change_adjoint, aligned_change_adjoint))
    return (coupled_embedding_sensitivity, aligned_embedding_sensitivity)
```

```python
import functools
import math

import jax
import jax.numpy as jnp
from jax import lax
from jax.experimental import pallas as pl
from jax.experimental.pallas import tpu as pltpu
from jax.sharding import PartitionSpec as P

HP = 4
ALIGNED_SPLITS = 8


EXACT_MATMUL = lax.Precision.HIGHEST
EPSILON = 1e-05


def standardize_features(values, norm_gain):
    center = values - jnp.mean(values, axis=-1, keepdims=True)
    spread = jnp.mean(center * center, axis=-1, keepdims=True)
    return center * lax.rsqrt(spread + EPSILON) * norm_gain


def affine_map(values, weight):
    return jnp.einsum("...c,ce->...e", values, weight, precision=EXACT_MATMUL)


def sigmoid_mixing(query_vectors, key_rows, value_rows, gate_preact, softmax_offset, head_count):
    query_shape = query_vectors.shape
    head_width = query_shape[-1] // head_count
    query_heads = query_vectors.reshape(query_shape[:-1] + (head_count, head_width))
    key_heads = key_rows.reshape(key_rows.shape[:-1] + (head_count, head_width))
    value_heads = value_rows.reshape(value_rows.shape[:-1] + (head_count, head_width))
    logits = (
        jnp.einsum("...qhd,...khd->...qhk", query_heads, key_heads, precision=EXACT_MATMUL)
        / math.sqrt(head_width)
        + softmax_offset
    )
    largest = lax.stop_gradient(jnp.max(logits, axis=-1, keepdims=True))
    weights = jnp.exp(logits - largest)
    weights = weights / jnp.sum(weights, axis=-1, keepdims=True)
    mixed_contents = jnp.einsum(
        "...qhk,...khd->...qhd", weights, value_heads, precision=EXACT_MATMUL
    )
    return mixed_contents.reshape(query_shape) * jax.nn.sigmoid(gate_preact)


def scanned_on_device(
    coupled_embedding,
    aligned_embedding,
    coupled_change_adjoint,
    aligned_change_adjoint,
    coupled_scaler,
    coupled_asking_matrix,
    coupled_lookup_matrix,
    coupled_content_matrix,
    coupled_sigmoid_matrix,
    coupled_offset_matrix,
    coupled_result_matrix,
    aligned_scaler,
    coupled_scaler_for_offset,
    aligned_asking_matrix,
    aligned_lookup_matrix,
    aligned_content_matrix,
    aligned_sigmoid_matrix,
    aligned_offset_matrix,
    aligned_result_matrix,
):

    def pair_local(entering_lines):
        standardized_source = standardize_features(entering_lines, coupled_scaler)
        return (
            affine_map(standardized_source, coupled_asking_matrix),
            affine_map(standardized_source, coupled_lookup_matrix),
            affine_map(standardized_source, coupled_content_matrix),
            affine_map(standardized_source, coupled_sigmoid_matrix),
            jnp.einsum(
                "jkc,ch->jhk", standardized_source, coupled_offset_matrix, precision=EXACT_MATMUL
            ),
        )

    (row_queries, row_keys, row_values, row_gates, bias_rows), pair_back = jax.vjp(
        pair_local, coupled_embedding
    )
    by_seq = lax.all_gather(bias_rows, "seq", axis=0, tiled=True)
    full_bias = lax.all_gather(by_seq, "res", axis=0, tiled=True)

    def row_output(one_query, one_key, one_value, one_gate, softmax_offset):
        return affine_map(
            sigmoid_mixing(one_query, one_key, one_value, one_gate, softmax_offset, HP),
            coupled_result_matrix,
        )

    def row_step(bias_sum, row_items):
        one_query, one_key, one_value, one_gate, one_cotan = row_items
        discarded_entry, row_back = jax.vjp(
            row_output, one_query, one_key, one_value, one_gate, full_bias
        )
        grad_query, grad_key, grad_value, grad_gate, grad_bias = row_back(one_cotan)
        return (bias_sum + grad_bias, (grad_query, grad_key, grad_value, grad_gate))

    bias_total, row_grads = lax.scan(
        row_step,
        jnp.zeros_like(full_bias),
        (row_queries, row_keys, row_values, row_gates, coupled_change_adjoint),
    )
    by_res = lax.psum_scatter(bias_total, "res", scatter_dimension=0, tiled=True)
    bias_grad_rows = lax.psum_scatter(by_res, "seq", scatter_dimension=0, tiled=True)
    (mixed_result_sensitivity,) = pair_back(row_grads + (bias_grad_rows,))

    def aligned_offset_portion(entering_lines):
        return jnp.einsum(
            "gys,sj->gjy",
            standardize_features(entering_lines, coupled_scaler_for_offset),
            aligned_offset_matrix,
            precision=EXACT_MATMUL,
        )

    aligned_offset_part, aligned_offset_reverse = jax.vjp(aligned_offset_portion, coupled_embedding)
    tile_softmax_offset = lax.all_gather(aligned_offset_part, "seq", axis=0, tiled=True)

    def sequence_output(query_vectors, full_key_rows, full_value_rows, gate_preact, softmax_offset):
        return affine_map(
            sigmoid_mixing(
                query_vectors,
                full_key_rows,
                full_value_rows,
                gate_preact,
                softmax_offset,
                ALIGNED_SPLITS,
            ),
            aligned_result_matrix,
        )

    state_all = lax.all_gather(aligned_embedding, "res", axis=1, tiled=True)

    def near_local(carry_pile):
        standardized_source = standardize_features(carry_pile, aligned_scaler)
        return (
            affine_map(standardized_source, aligned_asking_matrix),
            affine_map(standardized_source, aligned_sigmoid_matrix),
        )

    def keys_local(carry_pile):
        standardized_source = standardize_features(carry_pile, aligned_scaler)
        return (
            affine_map(standardized_source, aligned_lookup_matrix),
            affine_map(standardized_source, aligned_content_matrix),
        )

    (aligned_asking_lines, aligned_sigmoid_factors), near_back = jax.vjp(
        near_local, aligned_embedding
    )
    (full_key_rows, full_value_rows), keys_back = jax.vjp(keys_local, state_all)
    discarded_entry, sigmoid_mixing_reverse = jax.vjp(
        sequence_output,
        aligned_asking_lines,
        full_key_rows,
        full_value_rows,
        aligned_sigmoid_factors,
        tile_softmax_offset,
    )
    query_gradient, full_key_gradient, full_value_gradient, gate_gradient, block_bias_gradient = (
        sigmoid_mixing_reverse(aligned_change_adjoint)
    )
    (state_term,) = keys_back((full_key_gradient, full_value_gradient))
    spread_grad = lax.psum_scatter(state_term, "res", scatter_dimension=1, tiled=True)
    (near_grad,) = near_back((query_gradient, gate_gradient))
    aligned_embedding_sensitivity = near_grad + spread_grad
    offset_line_sensitivity = lax.psum_scatter(
        block_bias_gradient, "seq", scatter_dimension=0, tiled=True
    )
    (coupled_sensitivity_via_offset,) = aligned_offset_reverse(offset_line_sensitivity)
    return (
        mixed_result_sensitivity + coupled_sensitivity_via_offset,
        aligned_embedding_sensitivity,
    )


F32 = jnp.float32
BF16 = jnp.bfloat16
HEAD = 32
LANES = 128


def split2(a):
    top = a.astype(BF16)
    return top, (a - top.astype(F32)).astype(BF16)


def split3(a):
    top = a.astype(BF16)
    rest = a - top.astype(F32)
    mid = rest.astype(BF16)
    return top, mid, (rest - mid.astype(F32)).astype(BF16)


def left6(parts):
    a, b, c = parts
    return [a, a, b, b, a, c]


def right6(parts):
    a, b, c = parts
    return [a, b, a, b, c, a]


def left3(parts):
    return [parts[0], parts[0], parts[1]]


def right3(parts):
    return [parts[0], parts[1], parts[0]]


def nn(a, b):
    return lax.dot_general(a, b, (((1,), (0,)), ((), ())), preferred_element_type=F32)


def nt(a, b):
    return lax.dot_general(a, b, (((1,), (1,)), ((), ())), preferred_element_type=F32)


def cat(parts, axis):
    return jnp.concatenate(parts, axis=axis)


def normed(v):
    center = v - jnp.mean(v, axis=-1, keepdims=True)
    spread = jnp.mean(center * center, axis=-1, keepdims=True)
    scale = lax.rsqrt(spread + EPSILON)
    return center * scale, scale


def normed_back(n, scale, dn):
    return scale * (
        dn - jnp.mean(dn, axis=-1, keepdims=True) - n * jnp.mean(dn * n, axis=-1, keepdims=True)
    )


def head_mask(h, dtype):
    lane = lax.broadcasted_iota(jnp.int32, (1, LANES), 1)
    return jnp.where((lane // HEAD) == h, 1.0, 0.0).astype(dtype)


def bias_kernel(rows, x_ref, g_ref, wp_ref, g2_ref, wm_ref, bp_ref, bm_ref):
    hp, hm = wp_ref.shape[0], wm_ref.shape[0]
    w = cat([wp_ref[...] * g_ref[...], wm_ref[...] * g2_ref[...]], 0)
    wcat = cat(left6(split3(w)), 1)
    for j in range(rows):
        n, _ = normed(x_ref[j])
        res = nt(wcat, cat(right6(split3(n)), 1))
        for h in range(hp):
            bp_ref[h * rows + j : h * rows + j + 1, :] = res[h : h + 1]
        for h in range(hm):
            bm_ref[h * rows + j : h * rows + j + 1, :] = res[hp + h : hp + h + 1]


def place(axis_sizes):
    seq_n, res_n = axis_sizes
    return lax.axis_index("seq"), lax.axis_index("res")


def pair_kernel(
    dims,
    x_ref, adj_ref, own_ref, other_ref,
    g_ref, wq_ref, wk_ref, wv_ref, wg_ref, wo_ref,
    dn_ref, near_ref, far_ref,
    bt, dbt, w6, w3, wo3, wb,
):
    rows, heads, seq_n, res_n = dims
    step = pl.program_id(0)
    seq, res = lax.axis_index("seq"), lax.axis_index("res")
    core, chip = lax.rem(seq, 2), lax.div(seq, 2)
    n_keys = x_ref.shape[1]

    @pl.when(step == 0)
    def _():
        g = g_ref[...]
        wq = wq_ref[...] * g * (1.0 / math.sqrt(HEAD))
        wk = wk_ref[...] * g
        wv = wv_ref[...] * g
        wg = wg_ref[...] * g
        w6[...] = cat(right6(split3(cat([wq, wk], 1))), 0)
        w3[...] = cat(right3(split2(cat([wv, wg], 1))), 0)
        wo3[...] = cat(right3(split2(wo_ref[...])), 1)
        top, low = split2(cat([wq, wk, wv, wg], 1))
        wb[0] = top
        wb[1] = low
        for z in range(res_n):
            zi = lax.bitwise_xor(res, z)
            for s in range(seq_n):
                ci = lax.bitwise_xor(chip, s // 2)
                block = jnp.where(core == s % 2, own_ref[ci, zi], other_ref[ci, zi])
                d = z * seq_n + s
                for h in range(heads):
                    dbt[h, d * rows : (d + 1) * rows, :] = block[h * rows : (h + 1) * rows]
        for h in range(heads):
            bt[h] = dbt[h].T
        dbt[...] = jnp.zeros_like(dbt)

    n, _ = normed(x_ref[0])
    parts = split3(n)
    qk = nn(cat(left6(parts), 1), w6[...])
    vg = nn(cat(left3(parts), 1), w3[...])
    q, k, v, gate = qk[:, :LANES], qk[:, LANES:], vg[:, :LANES], vg[:, LANES:]
    d_out = nt(cat(left3(split2(adj_ref[0])), 1), wo3[...])
    sig = jax.nn.sigmoid(gate)
    d_mix = d_out * sig
    q1, q2, q3 = split3(q)
    ks = split3(k)
    kcat = cat(left6(ks), 1)
    vs = split2(v)
    vcat = cat(left3(vs), 1)
    kt1, kt2 = split2(k.T)
    vt1, vt2 = split2(v.T)
    m1, m2 = split2(d_mix)
    mixed, dq = [], []
    dk = jnp.zeros((n_keys, LANES), F32)
    dv = jnp.zeros((n_keys, LANES), F32)
    for h in range(heads):
        mask = head_mask(h, BF16)
        qh = (q1 * mask, q2 * mask, q3 * mask)
        mh = (m1 * mask, m2 * mask)
        band = slice(h * HEAD, (h + 1) * HEAD)
        s = nt(kcat, cat(right6(qh), 1)) + bt[h]
        e = jnp.exp(s - jnp.max(s, axis=0, keepdims=True))
        p = e * (1.0 / jnp.sum(e, axis=0, keepdims=True))
        p1, p2 = split2(p)
        both = nn(cat([vt1[band], vt2[band]], 0), p1)
        mixed.append(both[:HEAD] + both[HEAD:] + nn(vt1[band], p2))
        dp = nt(vcat, cat(right3(mh), 1))
        ds = p * (dp - jnp.sum(p * dp, axis=0, keepdims=True))
        dbt[h] = dbt[h] + ds
        s1, s2 = split2(ds)
        both = nn(cat([kt1[band], kt2[band]], 0), s1)
        dq.append(both[:HEAD] + both[HEAD:] + nn(kt1[band], s2))
        both = nn(s1, cat(qh[:2], 1))
        dk = dk + both[:, :LANES] + both[:, LANES:] + nn(s2, qh[0])
        both = nn(p1, cat(mh, 1))
        dv = dv + both[:, :LANES] + both[:, LANES:] + nn(p2, mh[0])
    o = cat(mixed, 0).T
    d_gate = d_out * o * sig * (1.0 - sig)
    t1, t2 = split2(cat([cat(dq, 0).T, dk, dv, d_gate], 1))
    dn_ref[0] = nt(t1, wb[0]) + nt(t1, wb[1]) + nt(t2, wb[0])

    @pl.when(step == rows - 1)
    def _():
        for h in range(heads):
            bt[h] = dbt[h].T
        for z in range(res_n):
            zi = lax.bitwise_xor(res, z)
            for s in range(seq_n):
                ci = lax.bitwise_xor(chip, s // 2)
                d = z * seq_n + s
                block = cat([bt[h, d * rows : (d + 1) * rows, :] for h in range(heads)], 0)

                @pl.when(core == s % 2)
                def _():
                    near_ref[ci, zi] = block

                @pl.when(core != s % 2)
                def _():
                    far_ref[ci, zi] = block


def msa_kernel(
    dims,
    y0_ref, y1_ref, y2_ref, y3_ref, adj_ref, own_ref, other_ref,
    g_ref, wq_ref, wk_ref, wv_ref, wg_ref, wo_ref,
    dy_ref, r0_ref, r1_ref, r2_ref, r3_ref, near_ref, far_ref,
    bias, dbias, yall, dyall,
):
    rows, heads, seq_n, res_n = dims
    seq, res = lax.axis_index("seq"), lax.axis_index("res")
    core, chip = lax.rem(seq, 2), lax.div(seq, 2)
    n_seqs, own, feats = y0_ref.shape
    n_keys = own * res_n
    tiles = feats // LANES
    g = g_ref[...]
    wq = wq_ref[...] * g * (1.0 / math.sqrt(HEAD))
    wk = wk_ref[...] * g
    wv = wv_ref[...] * g
    wg = wg_ref[...] * g

    for t, ref in enumerate((y0_ref, y1_ref, y2_ref, y3_ref)):
        at = pl.multiple_of(lax.bitwise_xor(res, t) * own, own)
        for b in range(n_seqs):
            yall[b, pl.ds(at, own), :] = ref[b]
    for s in range(seq_n):
        ci = lax.bitwise_xor(chip, s // 2)
        block = jnp.where(core == s % 2, own_ref[ci], other_ref[ci])
        for h in range(heads):
            bias[h, s * rows : (s + 1) * rows, :] = block[h * rows : (h + 1) * rows]

    n_own, _ = normed(y0_ref[...].reshape(n_seqs * own, feats))
    n_all, _ = normed(yall[...].reshape(n_seqs * n_keys, feats))
    own_parts, all_parts = split3(n_own), split3(n_all)
    q = nn(cat(left6(own_parts), 1), cat(right6(split3(wq)), 0))
    gate = nn(cat(left3(own_parts), 1), cat(right3(split2(wg)), 0))
    k = nn(cat(left6(all_parts), 1), cat(right6(split3(wk)), 0))
    v = nn(cat(left3(all_parts), 1), cat(right3(split2(wv)), 0))
    adj = adj_ref[...].reshape(n_seqs * own, feats)
    d_out = nt(cat(left3(split2(adj)), 1), cat(right3(split2(wo_ref[...])), 1))
    sig = jax.nn.sigmoid(gate)
    d_mix = d_out * sig
    mixes, dqs = [], []
    for b in range(n_seqs):
        near = slice(b * own, (b + 1) * own)
        wide = slice(b * n_keys, (b + 1) * n_keys)
        mix_tiles, dq_tiles, dkt, dvt = [], [], [], []
        for t in range(tiles):
            cols = slice(t * LANES, (t + 1) * LANES)
            q_t, k_t, v_t, m_t = q[near, cols], k[wide, cols], v[wide, cols], d_mix[near, cols]
            qp = split3(q_t)
            kp = split3(k_t)
            vp = split2(v_t)
            mp = split2(m_t)
            qt1, qt2 = split2(q_t.T)
            mt1, mt2 = split2(m_t.T)
            kcat = cat(right6(kp), 1)
            vcat = cat(right3(vp), 1)
            mix = jnp.zeros((own, LANES), F32)
            dq = jnp.zeros((own, LANES), F32)
            for u in range(LANES // HEAD):
                h = t * (LANES // HEAD) + u
                mask = head_mask(u, BF16)
                fmask = head_mask(u, F32)
                band = slice(u * HEAD, (u + 1) * HEAD)
                s = nt(cat(left6([a * mask for a in qp]), 1), kcat) + bias[h]
                e = jnp.exp(s - jnp.max(s, axis=1, keepdims=True))
                p = e * (1.0 / jnp.sum(e, axis=1, keepdims=True))
                p1, p2 = split2(p)
                both = nn(p1, cat(vp, 1))
                mix = mix + fmask * (both[:, :LANES] + both[:, LANES:] + nn(p2, vp[0]))
                dp = nt(cat(left3([a * mask for a in mp]), 1), vcat)
                ds = p * (dp - jnp.sum(p * dp, axis=1, keepdims=True))
                dbias[h] = ds if b == 0 else dbias[h] + ds
                s1, s2 = split2(ds)
                both = nn(s1, cat(kp[:2], 1))
                dq = dq + fmask * (both[:, :LANES] + both[:, LANES:] + nn(s2, kp[0]))
                both = nn(cat([qt1[band], qt2[band]], 0), s1)
                dkt.append(both[:HEAD] + both[HEAD:] + nn(qt1[band], s2))
                both = nn(cat([mt1[band], mt2[band]], 0), p1)
                dvt.append(both[:HEAD] + both[HEAD:] + nn(mt1[band], p2))
            mix_tiles.append(mix)
            dq_tiles.append(dq)
        mixes.append(cat(mix_tiles, 1))
        dqs.append(cat(dq_tiles, 1))
        t1, t2 = split2(cat([cat(dkt, 0).T, cat(dvt, 0).T], 1))
        b1, b2 = split2(cat([wk, wv], 1))
        dyall[b] = nt(t1, b1) + nt(t1, b2) + nt(t2, b1)
    o = cat(mixes, 0)
    d_gate = d_out * o * sig * (1.0 - sig)
    t1, t2 = split2(cat([cat(dqs, 0), d_gate], 1))
    b1, b2 = split2(cat([wq, wg], 1))
    dy_ref[...] = (nt(t1, b1) + nt(t1, b2) + nt(t2, b1)).reshape(n_seqs, own, feats)
    for t, ref in enumerate((r0_ref, r1_ref, r2_ref, r3_ref)):
        at = pl.multiple_of(lax.bitwise_xor(res, t) * own, own)
        for b in range(n_seqs):
            ref[b] = dyall[b, pl.ds(at, own), :]
    for s in range(seq_n):
        ci = lax.bitwise_xor(chip, s // 2)
        block = cat([dbias[h, s * rows : (s + 1) * rows, :] for h in range(heads)], 0)

        @pl.when(core == s % 2)
        def _():
            near_ref[ci] = block

        @pl.when(core != s % 2)
        def _():
            far_ref[ci] = block


def aligned_end_kernel(y_ref, dy_ref, r0_ref, r1_ref, r2_ref, r3_ref, out_ref):
    n, scale = normed(y_ref[...])
    dn = dy_ref[...] + r0_ref[...] + r1_ref[...] + r2_ref[...] + r3_ref[...]
    out_ref[...] = normed_back(n, scale, dn)


def pair_end_kernel(
    rows,
    x_ref, dn_ref, p0_ref, p1_ref, p2_ref, p3_ref, m0_ref, m1_ref, m2_ref, m3_ref,
    g_ref, wp_ref, g2_ref, wm_ref, out_ref,
):
    hp, hm = wp_ref.shape[0], wm_ref.shape[0]
    w = cat([wp_ref[...] * g_ref[...], wm_ref[...] * g2_ref[...]], 0)
    w = cat([w, jnp.zeros((16 - hp - hm, w.shape[1]), F32)], 0)
    wcat = cat(right3(split2(w)), 0)
    pair = p0_ref[...] + p1_ref[...] + p2_ref[...] + p3_ref[...]
    msa = m0_ref[...] + m1_ref[...] + m2_ref[...] + m3_ref[...]
    for j in range(rows):
        lines = [pair[h * rows + j : h * rows + j + 1] for h in range(hp)]
        lines += [msa[h * rows + j : h * rows + j + 1] for h in range(hm)]
        lines += [jnp.zeros((16 - hp - hm, pair.shape[1]), F32)]
        b = cat(lines, 0).T
        dn = dn_ref[j] + nn(cat(left3(split2(b)), 1), wcat)
        n, scale = normed(x_ref[j])
        out_ref[j] = normed_back(n, scale, dn)


MIB = 1 << 20


def params(mib, **more):
    return pltpu.CompilerParams(vmem_limit_bytes=mib * MIB, **more)


def swap(values, axis, size, offset):
    return lax.ppermute(values, axis, [(i, i ^ offset) for i in range(size)])


def fused_on_device(
    seq_n,
    res_n,
    coupled_embedding,
    aligned_embedding,
    coupled_change_adjoint,
    aligned_change_adjoint,
    coupled_scaler,
    coupled_asking_matrix,
    coupled_lookup_matrix,
    coupled_content_matrix,
    coupled_sigmoid_matrix,
    coupled_offset_matrix,
    coupled_result_matrix,
    aligned_scaler,
    coupled_scaler_for_offset,
    aligned_asking_matrix,
    aligned_lookup_matrix,
    aligned_content_matrix,
    aligned_sigmoid_matrix,
    aligned_offset_matrix,
    aligned_result_matrix,
):
    rows, length, feats = coupled_embedding.shape
    n_seqs, own, wide = aligned_embedding.shape
    hp, hm = HP, ALIGNED_SPLITS
    chips = seq_n // 2
    shape = lambda *s: jax.ShapeDtypeStruct(s, F32)
    wp_t, wm_t = coupled_offset_matrix.T, aligned_offset_matrix.T
    gain = coupled_scaler.reshape(1, feats)
    gain2 = coupled_scaler_for_offset.reshape(1, feats)

    others = [swap(aligned_embedding, "res", res_n, t) for t in range(1, res_n)]
    pair_rows, msa_rows = pl.pallas_call(
        functools.partial(bias_kernel, rows),
        out_shape=(shape(hp * rows, length), shape(hm * rows, length)),
        compiler_params=params(16),
        name="bias_rows",
    )(coupled_embedding, gain, wp_t, gain2, wm_t)
    column = jnp.stack([pair_rows] + [swap(pair_rows, "res", res_n, t) for t in range(1, res_n)])
    own_pair = jnp.stack([column] + [swap(column, "seq", seq_n, 2 * t) for t in range(1, chips)])
    own_msa = jnp.stack([msa_rows] + [swap(msa_rows, "seq", seq_n, 2 * t) for t in range(1, chips)])
    other_pair = swap(own_pair, "seq", seq_n, 1)
    other_msa = swap(own_msa, "seq", seq_n, 1)

    msa = pl.pallas_call(
        functools.partial(msa_kernel, (rows, hm, seq_n, res_n)),
        out_shape=(shape(n_seqs, own, wide),) * 5 + (shape(chips, hm * rows, length),) * 2,
        scratch_shapes=[
            pltpu.VMEM((hm, own, length), F32),
            pltpu.VMEM((hm, own, length), F32),
            pltpu.VMEM((n_seqs, length, wide), F32),
            pltpu.VMEM((n_seqs, length, wide), F32),
        ],
        compiler_params=params(48),
        name="msa_attention",
        cost_estimate=pl.CostEstimate(flops=2 * 10**9, bytes_accessed=4 * 10**6, transcendentals=0),
    )(
        aligned_embedding, *others, aligned_change_adjoint, own_msa, other_msa,
        aligned_scaler.reshape(wide, 1), aligned_asking_matrix, aligned_lookup_matrix,
        aligned_content_matrix, aligned_sigmoid_matrix, aligned_result_matrix,
    )
    dy, kept, sent, msa_near, msa_far = msa[0], msa[1], msa[2:5], msa[5], msa[6]
    arrived = [swap(a, "res", res_n, t + 1) for t, a in enumerate(sent)]
    msa_half = msa_near + swap(msa_far, "seq", seq_n, 1)
    msa_parts = [msa_half[0]] + [swap(msa_half[t], "seq", seq_n, 2 * t) for t in range(1, chips)]

    whole = lambda *s: pl.BlockSpec(s, lambda i: (0,) * len(s))
    row = pl.BlockSpec((1, length, feats), lambda i: (i, 0, 0))
    quarter = (chips, res_n, hp * rows, length)
    dn, near, far = pl.pallas_call(
        functools.partial(pair_kernel, (rows, hp, seq_n, res_n)),
        grid=(rows,),
        in_specs=[row, row, whole(*quarter), whole(*quarter), whole(feats, 1)]
        + [whole(feats, feats)] * 5,
        out_specs=(row, whole(*quarter), whole(*quarter)),
        out_shape=(shape(rows, length, feats), shape(*quarter), shape(*quarter)),
        scratch_shapes=[
            pltpu.VMEM((hp, length, length), F32),
            pltpu.VMEM((hp, length, length), F32),
            pltpu.VMEM((6 * feats, 2 * feats), BF16),
            pltpu.VMEM((3 * feats, 2 * feats), BF16),
            pltpu.VMEM((feats, 3 * feats), BF16),
            pltpu.VMEM((2, feats, 4 * feats), BF16),
        ],
        compiler_params=params(48),
        name="pair_attention",
        cost_estimate=pl.CostEstimate(flops=2 * 10**10, bytes_accessed=6 * 10**6, transcendentals=0),
    )(
        coupled_embedding, coupled_change_adjoint, own_pair, other_pair,
        coupled_scaler.reshape(feats, 1), coupled_asking_matrix, coupled_lookup_matrix,
        coupled_content_matrix, coupled_sigmoid_matrix, coupled_result_matrix,
    )
    half = near + swap(far, "seq", seq_n, 1)
    column = half[0]
    for t in range(1, chips):
        column = column + swap(half[t], "seq", seq_n, 2 * t)
    parts = [column[0]] + [swap(column[t], "res", res_n, t) for t in range(1, res_n)]

    aligned_out = pl.pallas_call(
        aligned_end_kernel,
        out_shape=shape(n_seqs, own, wide),
        compiler_params=params(16),
        name="aligned_end",
    )(aligned_embedding, dy, kept, *arrived)
    coupled_out = pl.pallas_call(
        functools.partial(pair_end_kernel, rows),
        out_shape=shape(rows, length, feats),
        compiler_params=params(16),
        name="pair_end",
    )(coupled_embedding, dn, *parts, *msa_parts, gain, wp_t, gain2, wm_t)
    return coupled_out, aligned_out


def on_device(seq_n, res_n, *arrays):
    length = arrays[0].shape[1]
    if length <= 2 * LANES and seq_n == 8 and res_n == 4:
        return fused_on_device(seq_n, res_n, *arrays)
    return scanned_on_device(*arrays)


def solution(mesh):
    in_specs = (
        P(("res", "seq"), None, None),
        P("seq", "res", None),
        P(("res", "seq"), None, None),
        P("seq", "res", None),
        P(),
        P(),
        P(),
        P(),
        P(),
        P(),
        P(),
        P(),
        P(),
        P(),
        P(),
        P(),
        P(),
        P(),
        P(),
    )
    out_specs = (P(("res", "seq"), None, None), P("seq", "res", None))
    return jax.shard_map(
        functools.partial(on_device, mesh.shape["seq"], mesh.shape["res"]),
        mesh=mesh, in_specs=in_specs, out_specs=out_specs, check_vma=False
    )
```

```python
import functools
import math

import jax
import jax.numpy as jnp
from jax import lax
from jax.experimental import pallas as pl
from jax.experimental.pallas import tpu as pltpu
from jax.sharding import PartitionSpec as P

HP = 4
ALIGNED_SPLITS = 8


EXACT_MATMUL = lax.Precision.HIGHEST
EPSILON = 1e-05


def standardize_features(values, norm_gain):
    center = values - jnp.mean(values, axis=-1, keepdims=True)
    spread = jnp.mean(center * center, axis=-1, keepdims=True)
    return center * lax.rsqrt(spread + EPSILON) * norm_gain


def affine_map(values, weight):
    return jnp.einsum("...c,ce->...e", values, weight, precision=EXACT_MATMUL)


def sigmoid_mixing(query_vectors, key_rows, value_rows, gate_preact, softmax_offset, head_count):
    query_shape = query_vectors.shape
    head_width = query_shape[-1] // head_count
    query_heads = query_vectors.reshape(query_shape[:-1] + (head_count, head_width))
    key_heads = key_rows.reshape(key_rows.shape[:-1] + (head_count, head_width))
    value_heads = value_rows.reshape(value_rows.shape[:-1] + (head_count, head_width))
    logits = (
        jnp.einsum("...qhd,...khd->...qhk", query_heads, key_heads, precision=EXACT_MATMUL)
        / math.sqrt(head_width)
        + softmax_offset
    )
    largest = lax.stop_gradient(jnp.max(logits, axis=-1, keepdims=True))
    weights = jnp.exp(logits - largest)
    weights = weights / jnp.sum(weights, axis=-1, keepdims=True)
    mixed_contents = jnp.einsum(
        "...qhk,...khd->...qhd", weights, value_heads, precision=EXACT_MATMUL
    )
    return mixed_contents.reshape(query_shape) * jax.nn.sigmoid(gate_preact)


def scanned_on_device(
    coupled_embedding,
    aligned_embedding,
    coupled_change_adjoint,
    aligned_change_adjoint,
    coupled_scaler,
    coupled_asking_matrix,
    coupled_lookup_matrix,
    coupled_content_matrix,
    coupled_sigmoid_matrix,
    coupled_offset_matrix,
    coupled_result_matrix,
    aligned_scaler,
    coupled_scaler_for_offset,
    aligned_asking_matrix,
    aligned_lookup_matrix,
    aligned_content_matrix,
    aligned_sigmoid_matrix,
    aligned_offset_matrix,
    aligned_result_matrix,
):

    def pair_local(entering_lines):
        standardized_source = standardize_features(entering_lines, coupled_scaler)
        return (
            affine_map(standardized_source, coupled_asking_matrix),
            affine_map(standardized_source, coupled_lookup_matrix),
            affine_map(standardized_source, coupled_content_matrix),
            affine_map(standardized_source, coupled_sigmoid_matrix),
            jnp.einsum(
                "jkc,ch->jhk", standardized_source, coupled_offset_matrix, precision=EXACT_MATMUL
            ),
        )

    (row_queries, row_keys, row_values, row_gates, bias_rows), pair_back = jax.vjp(
        pair_local, coupled_embedding
    )
    by_seq = lax.all_gather(bias_rows, "seq", axis=0, tiled=True)
    full_bias = lax.all_gather(by_seq, "res", axis=0, tiled=True)

    def row_output(one_query, one_key, one_value, one_gate, softmax_offset):
        return affine_map(
            sigmoid_mixing(one_query, one_key, one_value, one_gate, softmax_offset, HP),
            coupled_result_matrix,
        )

    def row_step(bias_sum, row_items):
        one_query, one_key, one_value, one_gate, one_cotan = row_items
        discarded_entry, row_back = jax.vjp(
            row_output, one_query, one_key, one_value, one_gate, full_bias
        )
        grad_query, grad_key, grad_value, grad_gate, grad_bias = row_back(one_cotan)
        return (bias_sum + grad_bias, (grad_query, grad_key, grad_value, grad_gate))

    bias_total, row_grads = lax.scan(
        row_step,
        jnp.zeros_like(full_bias),
        (row_queries, row_keys, row_values, row_gates, coupled_change_adjoint),
    )
    by_res = lax.psum_scatter(bias_total, "res", scatter_dimension=0, tiled=True)
    bias_grad_rows = lax.psum_scatter(by_res, "seq", scatter_dimension=0, tiled=True)
    (mixed_result_sensitivity,) = pair_back(row_grads + (bias_grad_rows,))

    def aligned_offset_portion(entering_lines):
        return jnp.einsum(
            "gys,sj->gjy",
            standardize_features(entering_lines, coupled_scaler_for_offset),
            aligned_offset_matrix,
            precision=EXACT_MATMUL,
        )

    aligned_offset_part, aligned_offset_reverse = jax.vjp(aligned_offset_portion, coupled_embedding)
    tile_softmax_offset = lax.all_gather(aligned_offset_part, "seq", axis=0, tiled=True)

    def sequence_output(query_vectors, full_key_rows, full_value_rows, gate_preact, softmax_offset):
        return affine_map(
            sigmoid_mixing(
                query_vectors,
                full_key_rows,
                full_value_rows,
                gate_preact,
                softmax_offset,
                ALIGNED_SPLITS,
            ),
            aligned_result_matrix,
        )

    state_all = lax.all_gather(aligned_embedding, "res", axis=1, tiled=True)

    def near_local(carry_pile):
        standardized_source = standardize_features(carry_pile, aligned_scaler)
        return (
            affine_map(standardized_source, aligned_asking_matrix),
            affine_map(standardized_source, aligned_sigmoid_matrix),
        )

    def keys_local(carry_pile):
        standardized_source = standardize_features(carry_pile, aligned_scaler)
        return (
            affine_map(standardized_source, aligned_lookup_matrix),
            affine_map(standardized_source, aligned_content_matrix),
        )

    (aligned_asking_lines, aligned_sigmoid_factors), near_back = jax.vjp(
        near_local, aligned_embedding
    )
    (full_key_rows, full_value_rows), keys_back = jax.vjp(keys_local, state_all)
    discarded_entry, sigmoid_mixing_reverse = jax.vjp(
        sequence_output,
        aligned_asking_lines,
        full_key_rows,
        full_value_rows,
        aligned_sigmoid_factors,
        tile_softmax_offset,
    )
    query_gradient, full_key_gradient, full_value_gradient, gate_gradient, block_bias_gradient = (
        sigmoid_mixing_reverse(aligned_change_adjoint)
    )
    (state_term,) = keys_back((full_key_gradient, full_value_gradient))
    spread_grad = lax.psum_scatter(state_term, "res", scatter_dimension=1, tiled=True)
    (near_grad,) = near_back((query_gradient, gate_gradient))
    aligned_embedding_sensitivity = near_grad + spread_grad
    offset_line_sensitivity = lax.psum_scatter(
        block_bias_gradient, "seq", scatter_dimension=0, tiled=True
    )
    (coupled_sensitivity_via_offset,) = aligned_offset_reverse(offset_line_sensitivity)
    return (
        mixed_result_sensitivity + coupled_sensitivity_via_offset,
        aligned_embedding_sensitivity,
    )


F32 = jnp.float32
BF16 = jnp.bfloat16
HEAD = 32
LANES = 128
TILE = 256


def split2(a):
    top = a.astype(BF16)
    return top, (a - top.astype(F32)).astype(BF16)


def split3(a):
    top = a.astype(BF16)
    rest = a - top.astype(F32)
    mid = rest.astype(BF16)
    return top, mid, (rest - mid.astype(F32)).astype(BF16)


def left6(parts):
    a, b, c = parts
    return [a, a, b, b, a, c]


def right6(parts):
    a, b, c = parts
    return [a, b, a, b, c, a]


def left3(parts):
    return [parts[0], parts[0], parts[1]]


def right3(parts):
    return [parts[0], parts[1], parts[0]]


def nn(a, b):
    return lax.dot_general(a, b, (((1,), (0,)), ((), ())), preferred_element_type=F32)


def nt(a, b):
    return lax.dot_general(a, b, (((1,), (1,)), ((), ())), preferred_element_type=F32)


def cat(parts, axis):
    return jnp.concatenate(parts, axis=axis)


def normed(v):
    center = v - jnp.mean(v, axis=-1, keepdims=True)
    spread = jnp.mean(center * center, axis=-1, keepdims=True)
    scale = lax.rsqrt(spread + EPSILON)
    return center * scale, scale


def normed_back(n, scale, dn):
    return scale * (
        dn - jnp.mean(dn, axis=-1, keepdims=True) - n * jnp.mean(dn * n, axis=-1, keepdims=True)
    )


def head_mask(h, dtype):
    lane = lax.broadcasted_iota(jnp.int32, (1, LANES), 1)
    return jnp.where((lane // HEAD) == h, 1.0, 0.0).astype(dtype)


def bias_kernel(rows, x_ref, g_ref, wp_ref, g2_ref, wm_ref, bp_ref, bm_ref):
    hp, hm = wp_ref.shape[0], wm_ref.shape[0]
    w = cat([wp_ref[...] * g_ref[...], wm_ref[...] * g2_ref[...]], 0)
    wcat = cat(left6(split3(w)), 1)
    for j in range(rows):
        n, _ = normed(x_ref[j])
        res = nt(wcat, cat(right6(split3(n)), 1))
        for h in range(hp):
            bp_ref[h * rows + j : h * rows + j + 1, :] = res[h : h + 1]
        for h in range(hm):
            bm_ref[h * rows + j : h * rows + j + 1, :] = res[hp + h : hp + h + 1]


def pair_project_kernel(
    x_ref, adj_ref, g_ref, wq_ref, wk_ref, wv_ref, wg_ref, wo_ref, gl_ref, wp_ref, gl2_ref, wm_ref,
    q_ref, k_ref, v_ref, m_ref, kt_ref, vt_ref, dout_ref, sig_ref, n_ref, scale_ref, wj_ref,
):
    rows, length, feats = x_ref.shape
    g = g_ref[...]
    wq = wq_ref[...] * g * (1.0 / math.sqrt(HEAD))
    wk = wk_ref[...] * g
    wv = wv_ref[...] * g
    wg = wg_ref[...] * g
    w6 = cat(right6(split3(cat([wq, wk], 1))), 0)
    w3 = cat(right3(split2(cat([wv, wg], 1))), 0)
    wo3 = cat(right3(split2(wo_ref[...])), 1)
    for i in range(rows):
        n, scale = normed(x_ref[i])
        n_ref[i] = n
        scale_ref[i] = jnp.broadcast_to(scale, n.shape)
        parts = split3(n)
        qk = nn(cat(left6(parts), 1), w6)
        vg = nn(cat(left3(parts), 1), w3)
        d_out = nt(cat(left3(split2(adj_ref[i])), 1), wo3)
        sig = jax.nn.sigmoid(vg[:, feats:])
        dout_ref[i] = d_out
        sig_ref[i] = sig
        q, k, v = qk[:, :feats], qk[:, feats:], vg[:, :feats]
        q_ref[i] = cat(split3(q), 1)
        k_ref[i] = cat(split3(k), 1)
        v_ref[i] = cat(split2(v), 1)
        m_ref[i] = cat(split2(d_out * sig), 1)
        kt_ref[i] = cat(split2(k.T), 0)
        vt_ref[i] = cat(split2(v.T), 0)
    hp, hm = wp_ref.shape[0], wm_ref.shape[0]
    w = cat([wp_ref[...] * gl_ref[...], wm_ref[...] * gl2_ref[...]], 0)
    lines = [jnp.broadcast_to(w[h : h + 1], (rows, feats)) for h in range(hp + hm)]
    lines += [jnp.zeros((LANES - rows * (hp + hm), feats), F32)]
    spread = cat(lines, 0)
    at = lax.broadcasted_iota(jnp.int32, (LANES, 1), 0)
    for j in range(rows):
        mine = jnp.where(lax.rem(at, rows) == j, spread, 0.0)
        wj_ref[:, j * feats : (j + 1) * feats] = cat(right3(split2(mine)), 0)


def gather_chips(natural, refs, core, chip):
    half = len(refs) // 2
    for t in range(half):
        at = lax.bitwise_xor(chip, t) * 2
        natural[at + core] = refs[t][...]
        natural[at + 1 - core] = refs[half + t][...]


def pair_kernel(
    dims,
    q_ref, k_ref, v_ref, m_ref, kt_ref, vt_ref,
    b0_ref, b1_ref, b2_ref, b3_ref, b4_ref, b5_ref, b6_ref, b7_ref,
    ot_ref, dqt_ref, dk_ref, dv_ref, near_ref, far_ref,
    bt, dbt, stack, natural,
):
    rows, heads, seq_n, res_n = dims
    step = pl.program_id(0)
    seq, res = lax.axis_index("seq"), lax.axis_index("res")
    core, chip = lax.rem(seq, 2), lax.div(seq, 2)
    n_keys = q_ref.shape[1]

    @pl.when(step == 0)
    def _():
        blocks = (b0_ref, b1_ref, b2_ref, b3_ref, b4_ref, b5_ref, b6_ref, b7_ref)
        gather_chips(natural, blocks, core, chip)
        for z in range(res_n):
            zi = lax.bitwise_xor(res, z)
            for s in range(seq_n):
                block = natural[s, zi]
                d = z * seq_n + s
                for h in range(heads):
                    at = h * n_keys + d * rows
                    stack[at : at + rows, :] = block[h * rows : (h + 1) * rows]
        bt[...] = stack[...].T
        dbt[...] = jnp.zeros_like(dbt)

    def pieces(ref, count):
        return [ref[0, :, t * LANES : (t + 1) * LANES] for t in range(count)]

    masks = [head_mask(h, BF16) for h in range(heads)]
    qs = [cat([a * mask for mask in masks], 0) for a in pieces(q_ref, 3)]
    ms = [cat([a * mask for mask in masks], 0) for a in pieces(m_ref, 2)]
    kcat = cat(left6(pieces(k_ref, 3)), 1)
    vcat = cat(left3(pieces(v_ref, 2)), 1)
    kt1, kt2 = kt_ref[0, :LANES], kt_ref[0, LANES:]
    vt1, vt2 = vt_ref[0, :LANES], vt_ref[0, LANES:]
    dk = jnp.zeros((n_keys, LANES), F32)
    dv = jnp.zeros((n_keys, LANES), F32)
    for c in range(heads * n_keys // TILE):
        cols = slice(c * TILE, (c + 1) * TILE)
        first, last = c * TILE // n_keys, ((c + 1) * TILE - 1) // n_keys
        band = slice(first * HEAD, (last + 1) * HEAD)
        lane = lax.broadcasted_iota(jnp.int32, (1, TILE), 1) + c * TILE

        def of_heads(top, low, a1, a2):
            both = nn(cat([top[band], low[band]], 0), a1)
            half = both.shape[0] // 2
            total = both[:half] + both[half:] + nn(top[band], a2)
            picked = total[:HEAD]
            for h in range(first + 1, last + 1):
                rest = total[(h - first) * HEAD : (h - first + 1) * HEAD]
                picked = jnp.where(lane >= h * n_keys, rest, picked)
            return picked

        qc = [a[cols] for a in qs]
        mc = [a[cols] for a in ms]
        s = nt(kcat, cat(right6(qc), 1)) + bt[:, cols]
        dp = nt(vcat, cat(right3(mc), 1))
        e = jnp.exp(s - jnp.max(s, axis=0, keepdims=True))
        p = e * (1.0 / jnp.sum(e, axis=0, keepdims=True))
        p1, p2 = split2(p)
        ot_ref[0, :, cols] = of_heads(vt1, vt2, p1, p2)
        ds = p * (dp - jnp.sum(p * dp, axis=0, keepdims=True))
        dbt[:, cols] = dbt[:, cols] + ds
        s1, s2 = split2(ds)
        dqt_ref[0, :, cols] = of_heads(kt1, kt2, s1, s2)
        both = nn(s1, cat(qc[:2], 1))
        dk = dk + both[:, :LANES] + both[:, LANES:] + nn(s2, qc[0])
        both = nn(p1, cat(mc, 1))
        dv = dv + both[:, :LANES] + both[:, LANES:] + nn(p2, mc[0])
    dk_ref[0] = dk
    dv_ref[0] = dv

    @pl.when(step == rows - 1)
    def _():
        stack[...] = dbt[...].T
        for z in range(res_n):
            zi = lax.bitwise_xor(res, z)
            for s in range(seq_n):
                ci = lax.bitwise_xor(chip, s // 2)
                d = z * seq_n + s
                at = [h * n_keys + d * rows for h in range(heads)]
                block = cat([stack[a : a + rows, :] for a in at], 0)

                @pl.when(core == s % 2)
                def _():
                    near_ref[ci, zi] = block

                @pl.when(core != s % 2)
                def _():
                    far_ref[ci, zi] = block


def pair_back_kernel(
    ot_ref, dqt_ref, dk_ref, dv_ref, dout_ref, sig_ref,
    g_ref, wq_ref, wk_ref, wv_ref, wg_ref, dn_ref,
):
    rows, length, feats = dk_ref.shape
    g = g_ref[...]
    wq = wq_ref[...] * g * (1.0 / math.sqrt(HEAD))
    w1, w2 = split2(cat([wq, wk_ref[...] * g, wv_ref[...] * g, wg_ref[...] * g], 1))

    def lines(flat):
        heads = flat.shape[1] // length
        return cat([flat[:, h * length : (h + 1) * length] for h in range(heads)], 0).T

    for i in range(rows):
        o, sig = lines(ot_ref[i]), sig_ref[i]
        d_gate = dout_ref[i] * o * sig * (1.0 - sig)
        t1, t2 = split2(cat([lines(dqt_ref[i]), dk_ref[i], dv_ref[i], d_gate], 1))
        dn_ref[i] = nt(t1, w1) + nt(t1, w2) + nt(t2, w1)


def msa_project_kernel(
    y0_ref, y1_ref, y2_ref, y3_ref, adj_ref,
    g_ref, wq_ref, wk_ref, wv_ref, wg_ref, wo_ref,
    q_ref, m_ref, dout_ref, sig_ref, k_ref, v_ref,
    yall,
):
    res = lax.axis_index("res")
    n_seqs, own, feats = y0_ref.shape
    n_keys = yall.shape[1]
    g = g_ref[...]
    for t, ref in enumerate((y0_ref, y1_ref, y2_ref, y3_ref)):
        at = pl.multiple_of(lax.bitwise_xor(res, t) * own, own)
        for b in range(n_seqs):
            yall[b, pl.ds(at, own), :] = ref[b]
    n_own, _ = normed(y0_ref[...].reshape(n_seqs * own, feats))
    n_all, _ = normed(yall[...].reshape(n_seqs * n_keys, feats))
    own_parts, all_parts = split3(n_own), split3(n_all)
    wq = wq_ref[...] * g * (1.0 / math.sqrt(HEAD))
    q = nn(cat(left6(own_parts), 1), cat(right6(split3(wq)), 0))
    gate = nn(cat(left3(own_parts), 1), cat(right3(split2(wg_ref[...] * g)), 0))
    k = nn(cat(left6(all_parts), 1), cat(right6(split3(wk_ref[...] * g)), 0))
    v = nn(cat(left3(all_parts), 1), cat(right3(split2(wv_ref[...] * g)), 0))
    adj = adj_ref[...].reshape(n_seqs * own, feats)
    d_out = nt(cat(left3(split2(adj)), 1), cat(right3(split2(wo_ref[...])), 1))
    sig = jax.nn.sigmoid(gate)
    q_ref[...] = q
    m_ref[...] = d_out * sig
    dout_ref[...] = d_out
    sig_ref[...] = sig
    k_ref[...] = k
    v_ref[...] = v


def msa_kernel(
    dims,
    q_ref, m_ref, k_ref, v_ref,
    b0_ref, b1_ref, b2_ref, b3_ref, b4_ref, b5_ref, b6_ref, b7_ref,
    g_ref, wk_ref, wv_ref, after_ref,
    o_ref, dq_ref, r0_ref, r1_ref, r2_ref, r3_ref, near_ref, far_ref,
    bias, dbias, dyall, natural,
):
    rows, heads, seq_n, res_n = dims
    seq, res = lax.axis_index("seq"), lax.axis_index("res")
    core, chip = lax.rem(seq, 2), lax.div(seq, 2)
    n_seqs, own, feats = r0_ref.shape
    n_keys = own * res_n
    tiles, group = feats // LANES, LANES // HEAD
    blocks = (b0_ref, b1_ref, b2_ref, b3_ref, b4_ref, b5_ref, b6_ref, b7_ref)
    gather_chips(natural, blocks, core, chip)
    for s in range(seq_n):
        block = cat([natural[s, res_n], natural[s, res_n + 1]], 0)
        for h in range(heads):
            at = h * own + s * rows
            bias[at : at + rows, :] = block[h * rows : (h + 1) * rows]
    masks = [head_mask(u, BF16) for u in range(group)]
    fmasks = [head_mask(u, F32) for u in range(group)]

    def stacked(a, by):
        return cat([a * mask for mask in by], 0)

    def own_rows(full):
        total = fmasks[0] * full[:own]
        for u in range(1, group):
            total = total + fmasks[u] * full[u * own : (u + 1) * own]
        return total

    b1, b2 = split2(cat([wk_ref[...] * g_ref[...], wv_ref[...] * g_ref[...]], 1))
    for b in range(n_seqs):
        near = slice(b * own, (b + 1) * own)
        wide = slice(b * n_keys, (b + 1) * n_keys)
        dkt, dvt = [], []
        for t in range(tiles):
            cols = slice(t * LANES, (t + 1) * LANES)
            lines = slice(t * group * own, (t + 1) * group * own)
            q_t, m_t = q_ref[near, cols], m_ref[near, cols]
            qs = [stacked(a, masks) for a in split3(q_t)]
            ms = [stacked(a, masks) for a in split2(m_t)]
            qt1, qt2 = split2(stacked(q_t, fmasks).T)
            mt1, mt2 = split2(stacked(m_t, fmasks).T)
            kp = split3(k_ref[wide, cols])
            vp = split2(v_ref[wide, cols])
            s = nt(cat(left6(qs), 1), cat(right6(kp), 1)) + bias[lines]
            dp = nt(cat(left3(ms), 1), cat(right3(vp), 1))
            e = jnp.exp(s - jnp.max(s, axis=1, keepdims=True))
            p = e * (1.0 / jnp.sum(e, axis=1, keepdims=True))
            p1, p2 = split2(p)
            both = nn(p1, cat(vp, 1))
            o_ref[near, cols] = own_rows(both[:, :LANES] + both[:, LANES:] + nn(p2, vp[0]))
            ds = p * (dp - jnp.sum(p * dp, axis=1, keepdims=True))
            dbias[lines] = ds if b == 0 else dbias[lines] + ds
            s1, s2 = split2(ds)
            both = nn(s1, cat(kp[:2], 1))
            dq_ref[near, cols] = own_rows(both[:, :LANES] + both[:, LANES:] + nn(s2, kp[0]))
            both = nn(cat([qt1, qt2], 0), s1)
            dkt.append(both[:LANES] + both[LANES:] + nn(qt1, s2))
            both = nn(cat([mt1, mt2], 0), p1)
            dvt.append(both[:LANES] + both[LANES:] + nn(mt1, p2))
        t1, t2 = split2(cat([a.T for a in dkt + dvt], 1))
        dyall[b] = nt(t1, b1) + nt(t1, b2) + nt(t2, b1)
    for t, ref in enumerate((r0_ref, r1_ref, r2_ref, r3_ref)):
        at = pl.multiple_of(lax.bitwise_xor(res, t) * own, own)
        for b in range(n_seqs):
            ref[b] = dyall[b, pl.ds(at, own), :]
    for s in range(seq_n):
        ci = lax.bitwise_xor(chip, s // 2)
        at = [h * own + s * rows for h in range(heads)]
        block = cat([dbias[a : a + rows, :] for a in at], 0)

        @pl.when(core == s % 2)
        def _():
            near_ref[ci] = block

        @pl.when(core != s % 2)
        def _():
            far_ref[ci] = block


def aligned_back_kernel(
    o_ref, dq_ref, dout_ref, sig_ref, g_ref, wq_ref, wg_ref, r0_ref, dy_ref
):
    n_seqs, own, feats = r0_ref.shape
    sig = sig_ref[...]
    d_gate = dout_ref[...] * o_ref[...] * sig * (1.0 - sig)
    t1, t2 = split2(cat([dq_ref[...], d_gate], 1))
    wq = wq_ref[...] * g_ref[...] * (1.0 / math.sqrt(HEAD))
    b1, b2 = split2(cat([wq, wg_ref[...] * g_ref[...]], 1))
    dy = nt(t1, b1) + nt(t1, b2) + nt(t2, b1)
    dy_ref[...] = dy.reshape(n_seqs, own, feats) + r0_ref[...]


def aligned_end_kernel(y_ref, dy_ref, r1_ref, r2_ref, r3_ref, out_ref):
    n, scale = normed(y_ref[...])
    out_ref[...] = normed_back(n, scale, dy_ref[...] + r1_ref[...] + r2_ref[...] + r3_ref[...])


def stack_kernel(p0_ref, p1_ref, p2_ref, p3_ref, m_ref, after_ref, out_ref):
    lines = p0_ref.shape[0]
    for t, ref in enumerate((p0_ref, p1_ref, p2_ref, p3_ref)):
        out_ref[t] = ref[...]
    out_ref[4] = m_ref[:lines]
    out_ref[5] = m_ref[lines:]


def core_sum_kernel(p0_ref, p1_ref, m0_ref, m1_ref, after_ref, s0_ref, s1_ref, s2_ref, s3_ref):
    res_n, lines = p0_ref.shape[1:3]
    for t, ref in enumerate((s0_ref, s1_ref, s2_ref, s3_ref)):
        ref[:res_n] = p0_ref[t] + p1_ref[t]
        ref[res_n] = m0_ref[t, :lines] + m1_ref[t, :lines]
        ref[res_n + 1] = m0_ref[t, lines:] + m1_ref[t, lines:]


def chip_sum_kernel(
    s0_ref, s1_ref, s2_ref, s3_ref, after_ref, c0_ref, c1_ref, c2_ref, c3_ref, m_ref
):
    lines = c0_ref.shape[0]
    for t, ref in enumerate((c0_ref, c1_ref, c2_ref, c3_ref)):
        ref[...] = s0_ref[t] + s1_ref[t] + s2_ref[t] + s3_ref[t]
    for t in range(2):
        total = s0_ref[4 + t] + s1_ref[4 + t] + s2_ref[4 + t] + s3_ref[4 + t]
        m_ref[t * lines : (t + 1) * lines] = total


def pair_end_kernel(
    n_ref, scale_ref, dn_ref, p0_ref, p1_ref, p2_ref, p3_ref, m_ref, wj_ref, out_ref
):
    rows, length, feats = n_ref.shape
    pair = p0_ref[...] + p1_ref[...] + p2_ref[...] + p3_ref[...]
    msa = m_ref[...]
    pad = jnp.zeros((LANES - pair.shape[0] - msa.shape[0], length), F32)
    b = cat([pair, msa, pad], 0).T
    more = nn(cat(left3(split2(b)), 1), wj_ref[...])
    for j in range(rows):
        dn = dn_ref[j] + more[:, j * feats : (j + 1) * feats]
        out_ref[j] = normed_back(n_ref[j], scale_ref[j], dn)


MIB = 1 << 20


def params(mib, **more):
    return pltpu.CompilerParams(vmem_limit_bytes=mib * MIB, **more)


def swap(values, axis, size, offset):
    return lax.ppermute(values, axis, [(i, i ^ offset) for i in range(size)])


def fused_on_device(
    seq_n,
    res_n,
    coupled_embedding,
    aligned_embedding,
    coupled_change_adjoint,
    aligned_change_adjoint,
    coupled_scaler,
    coupled_asking_matrix,
    coupled_lookup_matrix,
    coupled_content_matrix,
    coupled_sigmoid_matrix,
    coupled_offset_matrix,
    coupled_result_matrix,
    aligned_scaler,
    coupled_scaler_for_offset,
    aligned_asking_matrix,
    aligned_lookup_matrix,
    aligned_content_matrix,
    aligned_sigmoid_matrix,
    aligned_offset_matrix,
    aligned_result_matrix,
):
    rows, length, feats = coupled_embedding.shape
    n_seqs, own, wide = aligned_embedding.shape
    hp, hm = HP, ALIGNED_SPLITS
    chips = seq_n // 2
    shape = lambda *s: jax.ShapeDtypeStruct(s, F32)
    wp_t, wm_t = coupled_offset_matrix.T, aligned_offset_matrix.T
    gain = coupled_scaler.reshape(1, feats)
    gain2 = coupled_scaler_for_offset.reshape(1, feats)

    others = [swap(aligned_embedding, "res", res_n, t) for t in range(1, res_n)]
    pair_rows, msa_rows = pl.pallas_call(
        functools.partial(bias_kernel, rows),
        out_shape=(shape(hp * rows, length), shape(hm * rows, length)),
        compiler_params=params(16),
        name="bias_rows",
    )(coupled_embedding, gain, wp_t, gain2, wm_t)
    bf = lambda *s: jax.ShapeDtypeStruct(s, BF16)
    gain_in = coupled_scaler.reshape(feats, 1)
    q, k, v, m, kt, vt, d_out, sig, n, scale, wj = pl.pallas_call(
        pair_project_kernel,
        out_shape=(
            bf(rows, length, 3 * feats), bf(rows, length, 3 * feats),
            bf(rows, length, 2 * feats), bf(rows, length, 2 * feats),
            bf(rows, 2 * feats, length), bf(rows, 2 * feats, length),
        ) + (shape(rows, length, feats),) * 4 + (bf(3 * LANES, rows * feats),),
        compiler_params=params(63),
        name="pair_project",
        cost_estimate=pl.CostEstimate(flops=2 * 10**9, bytes_accessed=10**7, transcendentals=0),
    )(
        coupled_embedding, coupled_change_adjoint, gain_in, coupled_asking_matrix,
        coupled_lookup_matrix, coupled_content_matrix, coupled_sigmoid_matrix,
        coupled_result_matrix, gain, wp_t, gain2, wm_t,
    )

    lines = hp * rows
    joint = (res_n + 2, lines, length)
    vmem = lambda count: [pl.BlockSpec(memory_space=pltpu.VMEM)] * count
    after = [pl.BlockSpec(memory_space=pl.ANY)]
    first = pl.pallas_call(
        stack_kernel,
        in_specs=vmem(5) + after,
        out_shape=shape(*joint),
        compiler_params=params(16),
        name="stack_rows",
    )(pair_rows, *[swap(pair_rows, "res", res_n, t) for t in range(1, res_n)], msa_rows, n)
    blocks = [first] + [swap(first, "seq", seq_n, 2 * t) for t in range(1, chips)]
    blocks = blocks + [swap(a, "seq", seq_n, 1) for a in blocks]

    wide_gain = aligned_scaler.reshape(wide, 1)
    flat = lambda count: shape(n_seqs * count, wide)
    mq, mm, m_out, m_sig, mk, mv = pl.pallas_call(
        msa_project_kernel,
        out_shape=(flat(own),) * 4 + (flat(length),) * 2,
        scratch_shapes=[pltpu.VMEM((n_seqs, length, wide), F32)],
        compiler_params=params(63),
        name="msa_project",
        cost_estimate=pl.CostEstimate(flops=10**9, bytes_accessed=10**7, transcendentals=0),
    )(
        aligned_embedding, *others, aligned_change_adjoint, wide_gain, aligned_asking_matrix,
        aligned_lookup_matrix, aligned_content_matrix, aligned_sigmoid_matrix,
        aligned_result_matrix,
    )

    piece = lambda *s: pl.BlockSpec((1,) + s, lambda i: (i, 0, 0))
    whole = lambda *s: pl.BlockSpec(s, lambda i: (0,) * len(s))
    quarter = (chips, res_n, lines, length)
    ot, dqt, dk, dv, near, far = pl.pallas_call(
        functools.partial(pair_kernel, (rows, hp, seq_n, res_n)),
        grid=(rows,),
        in_specs=[
            piece(length, 3 * feats), piece(length, 3 * feats),
            piece(length, 2 * feats), piece(length, 2 * feats),
            piece(2 * feats, length), piece(2 * feats, length),
        ] + [whole(*joint)] * seq_n,
        out_specs=(
            piece(HEAD, hp * length), piece(HEAD, hp * length),
            piece(length, feats), piece(length, feats), whole(*quarter), whole(*quarter),
        ),
        out_shape=(
            shape(rows, HEAD, hp * length), shape(rows, HEAD, hp * length),
            shape(rows, length, feats), shape(rows, length, feats),
            shape(*quarter), shape(*quarter),
        ),
        scratch_shapes=[
            pltpu.VMEM((length, hp * length), F32),
            pltpu.VMEM((length, hp * length), F32),
            pltpu.VMEM((hp * length, length), F32),
            pltpu.VMEM((seq_n,) + joint, F32),
        ],
        compiler_params=params(48),
        name="pair_attention",
        cost_estimate=pl.CostEstimate(flops=10**10, bytes_accessed=10**7, transcendentals=0),
    )(q, k, v, m, kt, vt, *blocks)
    far_pair = swap(far, "seq", seq_n, 1)
    dn = pl.pallas_call(
        pair_back_kernel,
        out_shape=shape(rows, length, feats),
        compiler_params=params(32),
        name="pair_back",
        cost_estimate=pl.CostEstimate(flops=10**9, bytes_accessed=10**7, transcendentals=0),
    )(
        ot, dqt, dk, dv, d_out, sig, gain_in, coupled_asking_matrix,
        coupled_lookup_matrix, coupled_content_matrix, coupled_sigmoid_matrix,
    )
    stretch = pltpu.VMEM((hm * own, length), F32)
    o, dq, kept, r1, r2, r3, msa_near, msa_far = pl.pallas_call(
        functools.partial(msa_kernel, (rows, hm, seq_n, res_n)),
        out_shape=(flat(own),) * 2 + (shape(n_seqs, own, wide),) * 4
        + (shape(chips, hm * rows, length),) * 2,
        in_specs=vmem(15) + after,
        scratch_shapes=[
            stretch, stretch, pltpu.VMEM((n_seqs, length, wide), F32),
            pltpu.VMEM((seq_n,) + joint, F32),
        ],
        compiler_params=params(48),
        name="msa_attention",
        cost_estimate=pl.CostEstimate(flops=4 * 10**9, bytes_accessed=10**7, transcendentals=0),
    )(
        mq, mm, mk, mv, *blocks, wide_gain,
        aligned_lookup_matrix, aligned_content_matrix, near,
    )
    far_msa = swap(msa_far, "seq", seq_n, 1)
    arrived = [swap(a, "res", res_n, t + 1) for t, a in enumerate((r1, r2, r3))]
    sums = pl.pallas_call(
        core_sum_kernel,
        in_specs=vmem(4) + after,
        out_shape=(shape(*joint),) * chips,
        compiler_params=params(16),
        name="core_sum",
    )(near, far_pair, msa_near, far_msa, dn)
    dy = pl.pallas_call(
        aligned_back_kernel,
        out_shape=shape(n_seqs, own, wide),
        compiler_params=params(16),
        name="aligned_back",
        cost_estimate=pl.CostEstimate(flops=10**9, bytes_accessed=10**6, transcendentals=0),
    )(o, dq, m_out, m_sig, wide_gain, aligned_asking_matrix, aligned_sigmoid_matrix, kept)
    *column, msa_sum = pl.pallas_call(
        chip_sum_kernel,
        in_specs=vmem(4) + after,
        out_shape=(shape(lines, length),) * res_n + (shape(hm * rows, length),),
        compiler_params=params(16),
        name="chip_sum",
    )(sums[0], *[swap(sums[t], "seq", seq_n, 2 * t) for t in range(1, chips)], dy)
    parts = [column[0]] + [swap(column[t], "res", res_n, t) for t in range(1, res_n)]

    aligned_out = pl.pallas_call(
        aligned_end_kernel,
        out_shape=shape(n_seqs, own, wide),
        compiler_params=params(16),
        name="aligned_end",
    )(aligned_embedding, dy, *arrived)
    coupled_out = pl.pallas_call(
        pair_end_kernel,
        out_shape=shape(rows, length, feats),
        compiler_params=params(16),
        name="pair_end",
    )(n, scale, dn, *parts, msa_sum, wj)
    return coupled_out, aligned_out


def on_device(seq_n, res_n, *arrays):
    length = arrays[0].shape[1]
    rows = arrays[0].shape[0]
    narrow = length <= 2 * LANES and HP * length % TILE == 0
    narrow = narrow and rows * (HP + ALIGNED_SPLITS) <= LANES
    narrow = narrow and ALIGNED_SPLITS == 2 * HP
    if narrow and seq_n == 8 and res_n == 4:
        return fused_on_device(seq_n, res_n, *arrays)
    return scanned_on_device(*arrays)


def solution(mesh):
    in_specs = (
        P(("res", "seq"), None, None),
        P("seq", "res", None),
        P(("res", "seq"), None, None),
        P("seq", "res", None),
        P(),
        P(),
        P(),
        P(),
        P(),
        P(),
        P(),
        P(),
        P(),
        P(),
        P(),
        P(),
        P(),
        P(),
        P(),
    )
    out_specs = (P(("res", "seq"), None, None), P("seq", "res", None))
    return jax.shard_map(
        functools.partial(on_device, mesh.shape["seq"], mesh.shape["res"]),
        mesh=mesh, in_specs=in_specs, out_specs=out_specs, check_vma=False
    )
```

```python
import functools
import math

import jax
import jax.numpy as jnp
from jax import lax
from jax.experimental import pallas as pl
from jax.experimental.pallas import tpu as pltpu
from jax.sharding import PartitionSpec as P

HP = 4
ALIGNED_SPLITS = 8


EXACT_MATMUL = lax.Precision.HIGHEST
EPSILON = 1e-05


def standardize_features(values, norm_gain):
    center = values - jnp.mean(values, axis=-1, keepdims=True)
    spread = jnp.mean(center * center, axis=-1, keepdims=True)
    return center * lax.rsqrt(spread + EPSILON) * norm_gain


def affine_map(values, weight):
    return jnp.einsum("...c,ce->...e", values, weight, precision=EXACT_MATMUL)


def sigmoid_mixing(query_vectors, key_rows, value_rows, gate_preact, softmax_offset, head_count):
    query_shape = query_vectors.shape
    head_width = query_shape[-1] // head_count
    query_heads = query_vectors.reshape(query_shape[:-1] + (head_count, head_width))
    key_heads = key_rows.reshape(key_rows.shape[:-1] + (head_count, head_width))
    value_heads = value_rows.reshape(value_rows.shape[:-1] + (head_count, head_width))
    logits = (
        jnp.einsum("...qhd,...khd->...qhk", query_heads, key_heads, precision=EXACT_MATMUL)
        / math.sqrt(head_width)
        + softmax_offset
    )
    largest = lax.stop_gradient(jnp.max(logits, axis=-1, keepdims=True))
    weights = jnp.exp(logits - largest)
    weights = weights / jnp.sum(weights, axis=-1, keepdims=True)
    mixed_contents = jnp.einsum(
        "...qhk,...khd->...qhd", weights, value_heads, precision=EXACT_MATMUL
    )
    return mixed_contents.reshape(query_shape) * jax.nn.sigmoid(gate_preact)


def scanned_on_device(
    coupled_embedding,
    aligned_embedding,
    coupled_change_adjoint,
    aligned_change_adjoint,
    coupled_scaler,
    coupled_asking_matrix,
    coupled_lookup_matrix,
    coupled_content_matrix,
    coupled_sigmoid_matrix,
    coupled_offset_matrix,
    coupled_result_matrix,
    aligned_scaler,
    coupled_scaler_for_offset,
    aligned_asking_matrix,
    aligned_lookup_matrix,
    aligned_content_matrix,
    aligned_sigmoid_matrix,
    aligned_offset_matrix,
    aligned_result_matrix,
):

    def pair_local(entering_lines):
        standardized_source = standardize_features(entering_lines, coupled_scaler)
        return (
            affine_map(standardized_source, coupled_asking_matrix),
            affine_map(standardized_source, coupled_lookup_matrix),
            affine_map(standardized_source, coupled_content_matrix),
            affine_map(standardized_source, coupled_sigmoid_matrix),
            jnp.einsum(
                "jkc,ch->jhk", standardized_source, coupled_offset_matrix, precision=EXACT_MATMUL
            ),
        )

    (row_queries, row_keys, row_values, row_gates, bias_rows), pair_back = jax.vjp(
        pair_local, coupled_embedding
    )
    by_seq = lax.all_gather(bias_rows, "seq", axis=0, tiled=True)
    full_bias = lax.all_gather(by_seq, "res", axis=0, tiled=True)

    def row_output(one_query, one_key, one_value, one_gate, softmax_offset):
        return affine_map(
            sigmoid_mixing(one_query, one_key, one_value, one_gate, softmax_offset, HP),
            coupled_result_matrix,
        )

    def row_step(bias_sum, row_items):
        one_query, one_key, one_value, one_gate, one_cotan = row_items
        discarded_entry, row_back = jax.vjp(
            row_output, one_query, one_key, one_value, one_gate, full_bias
        )
        grad_query, grad_key, grad_value, grad_gate, grad_bias = row_back(one_cotan)
        return (bias_sum + grad_bias, (grad_query, grad_key, grad_value, grad_gate))

    bias_total, row_grads = lax.scan(
        row_step,
        jnp.zeros_like(full_bias),
        (row_queries, row_keys, row_values, row_gates, coupled_change_adjoint),
    )
    by_res = lax.psum_scatter(bias_total, "res", scatter_dimension=0, tiled=True)
    bias_grad_rows = lax.psum_scatter(by_res, "seq", scatter_dimension=0, tiled=True)
    (mixed_result_sensitivity,) = pair_back(row_grads + (bias_grad_rows,))

    def aligned_offset_portion(entering_lines):
        return jnp.einsum(
            "gys,sj->gjy",
            standardize_features(entering_lines, coupled_scaler_for_offset),
            aligned_offset_matrix,
            precision=EXACT_MATMUL,
        )

    aligned_offset_part, aligned_offset_reverse = jax.vjp(aligned_offset_portion, coupled_embedding)
    tile_softmax_offset = lax.all_gather(aligned_offset_part, "seq", axis=0, tiled=True)

    def sequence_output(query_vectors, full_key_rows, full_value_rows, gate_preact, softmax_offset):
        return affine_map(
            sigmoid_mixing(
                query_vectors,
                full_key_rows,
                full_value_rows,
                gate_preact,
                softmax_offset,
                ALIGNED_SPLITS,
            ),
            aligned_result_matrix,
        )

    state_all = lax.all_gather(aligned_embedding, "res", axis=1, tiled=True)

    def near_local(carry_pile):
        standardized_source = standardize_features(carry_pile, aligned_scaler)
        return (
            affine_map(standardized_source, aligned_asking_matrix),
            affine_map(standardized_source, aligned_sigmoid_matrix),
        )

    def keys_local(carry_pile):
        standardized_source = standardize_features(carry_pile, aligned_scaler)
        return (
            affine_map(standardized_source, aligned_lookup_matrix),
            affine_map(standardized_source, aligned_content_matrix),
        )

    (aligned_asking_lines, aligned_sigmoid_factors), near_back = jax.vjp(
        near_local, aligned_embedding
    )
    (full_key_rows, full_value_rows), keys_back = jax.vjp(keys_local, state_all)
    discarded_entry, sigmoid_mixing_reverse = jax.vjp(
        sequence_output,
        aligned_asking_lines,
        full_key_rows,
        full_value_rows,
        aligned_sigmoid_factors,
        tile_softmax_offset,
    )
    query_gradient, full_key_gradient, full_value_gradient, gate_gradient, block_bias_gradient = (
        sigmoid_mixing_reverse(aligned_change_adjoint)
    )
    (state_term,) = keys_back((full_key_gradient, full_value_gradient))
    spread_grad = lax.psum_scatter(state_term, "res", scatter_dimension=1, tiled=True)
    (near_grad,) = near_back((query_gradient, gate_gradient))
    aligned_embedding_sensitivity = near_grad + spread_grad
    offset_line_sensitivity = lax.psum_scatter(
        block_bias_gradient, "seq", scatter_dimension=0, tiled=True
    )
    (coupled_sensitivity_via_offset,) = aligned_offset_reverse(offset_line_sensitivity)
    return (
        mixed_result_sensitivity + coupled_sensitivity_via_offset,
        aligned_embedding_sensitivity,
    )


F32 = jnp.float32
BF16 = jnp.bfloat16
HEAD = 32
LANES = 128
TILE = 256


def split2(a):
    top = a.astype(BF16)
    return top, (a - top.astype(F32)).astype(BF16)


def split3(a):
    top = a.astype(BF16)
    rest = a - top.astype(F32)
    mid = rest.astype(BF16)
    return top, mid, (rest - mid.astype(F32)).astype(BF16)


def left6(parts):
    a, b, c = parts
    return [a, a, b, b, a, c]


def right6(parts):
    a, b, c = parts
    return [a, b, a, b, c, a]


def left3(parts):
    return [parts[0], parts[0], parts[1]]


def right3(parts):
    return [parts[0], parts[1], parts[0]]


def nn(a, b):
    return lax.dot_general(a, b, (((1,), (0,)), ((), ())), preferred_element_type=F32)


def nt(a, b):
    return lax.dot_general(a, b, (((1,), (1,)), ((), ())), preferred_element_type=F32)


def cat(parts, axis):
    return jnp.concatenate(parts, axis=axis)


def normed(v):
    center = v - jnp.mean(v, axis=-1, keepdims=True)
    spread = jnp.mean(center * center, axis=-1, keepdims=True)
    scale = lax.rsqrt(spread + EPSILON)
    return center * scale, scale


def normed_back(n, scale, dn):
    return scale * (
        dn - jnp.mean(dn, axis=-1, keepdims=True) - n * jnp.mean(dn * n, axis=-1, keepdims=True)
    )


def head_mask(h, dtype):
    lane = lax.broadcasted_iota(jnp.int32, (1, LANES), 1)
    return jnp.where((lane // HEAD) == h, 1.0, 0.0).astype(dtype)


def fetch(pairs, sem):
    copies = [pltpu.make_async_copy(a, b, sem.at[t]) for t, (a, b) in enumerate(pairs)]
    for copy in copies:
        copy.start()
    return copies


def bias_kernel(rows, x_ref, y_ref, g_ref, wp_ref, g2_ref, wm_ref, joint_ref, bm_ref):
    length = x_ref.shape[1]
    base, wide = y_ref.shape
    joint_ref[:base] = y_ref[...]
    if length < wide:
        joint_ref[base:, length:] = jnp.zeros((wp_ref.shape[0] * rows, wide - length), F32)
    hp, hm = wp_ref.shape[0], wm_ref.shape[0]
    w = cat([wp_ref[...] * g_ref[...], wm_ref[...] * g2_ref[...]], 0)
    wcat = cat(left6(split3(w)), 1)
    for j in range(rows):
        n, _ = normed(x_ref[j])
        res = nt(wcat, cat(right6(split3(n)), 1))
        for h in range(hp):
            at = base + h * rows + j
            joint_ref[at : at + 1, :length] = res[h : h + 1]
        for h in range(hm):
            bm_ref[h * rows + j : h * rows + j + 1, :] = res[hp + h : hp + h + 1]


def pair_project_kernel(
    x_hbm, adj_hbm, g_ref, wq_hbm, wk_hbm, wv_hbm, wg_hbm, wo_hbm, wp_ref, g2_ref, wm_ref,
    q_ref, k_ref, v_ref, m_ref, kt_ref, vt_ref, dout_ref, sig_ref, n_ref, scale_ref, wj_ref, wb_ref,
    x_ref, adj_ref, wq_ref, wk_ref, wv_ref, wg_ref, wo_ref, sem,
):
    rows, length, feats = x_ref.shape
    g = g_ref[...]
    copies = fetch(
        [
            (wq_hbm, wq_ref), (wk_hbm, wk_ref), (wv_hbm, wv_ref), (wg_hbm, wg_ref),
            (wo_hbm, wo_ref), (x_hbm, x_ref), (adj_hbm, adj_ref),
        ],
        sem,
    )
    for copy in copies:
        copy.wait()
    top, low = split2(cat([wq_ref[...], wk_ref[...], wv_ref[...], wg_ref[...]], 1))
    wb_ref[0] = top
    wb_ref[1] = low
    w6 = cat(right6(split3(cat([wq_ref[...], wk_ref[...]], 1))), 0)
    w3 = cat(right3(split2(cat([wv_ref[...], wg_ref[...]], 1))), 0)
    wo3 = cat(right3(split2(wo_ref[...])), 1)
    for i in range(rows):
        n, scale = normed(x_ref[i])
        n_ref[i] = n
        scale_ref[i] = jnp.broadcast_to(scale, n.shape)
        parts = split3(n * g)
        qk = nn(cat(left6(parts), 1), w6)
        vg = nn(cat(left3(parts), 1), w3)
        d_out = nt(cat(left3(split2(adj_ref[i])), 1), wo3)
        sig = jax.nn.sigmoid(vg[:, feats:])
        dout_ref[i] = d_out
        sig_ref[i] = sig
        q, k, v = qk[:, :feats] * (1.0 / math.sqrt(HEAD)), qk[:, feats:], vg[:, :feats]
        q_ref[i] = cat(split3(q), 1)
        k_ref[i] = cat(split3(k), 1)
        v_ref[i] = cat(split2(v), 1)
        m_ref[i] = cat(split2(d_out * sig), 1)
        kt_ref[i] = cat(split2(k.T), 0)
        vt_ref[i] = cat(split2(v.T), 0)
    hp, hm = wp_ref.shape[0], wm_ref.shape[0]
    w = cat([wp_ref[...] * g, wm_ref[...] * g2_ref[...]], 0)
    lines = [jnp.broadcast_to(w[h : h + 1], (rows, feats)) for h in range(hp + hm)]
    lines += [jnp.zeros((LANES - rows * (hp + hm), feats), F32)]
    spread = cat(lines, 0)
    at = lax.broadcasted_iota(jnp.int32, (LANES, 1), 0)
    for j in range(rows):
        mine = jnp.where(lax.rem(at, rows) == j, spread, 0.0)
        wj_ref[:, j * feats : (j + 1) * feats] = cat(right3(split2(mine)), 0)


def pack(block_of, count, lines, out_ref):
    half = count // 2
    for t in range(half):
        first, second = block_of(t), block_of(t + half)
        out_ref[t * lines : (t + 1) * lines] = first[:, :LANES]
        out_ref[(t + half) * lines : (t + half + 1) * lines] = second[:, :LANES]
        rest = cat([first[:, LANES:], second[:, LANES:]], 1)
        out_ref[(t + count) * lines : (t + count + 1) * lines] = rest


def unpack(dense, count, lines):
    half = count // 2
    blocks = []
    for t in range(count):
        rest = dense[(count + t % half) * lines : (count + t % half + 1) * lines]
        rest = rest[:, : LANES // 2] if t < half else rest[:, LANES // 2 :]
        blocks.append(cat([dense[t * lines : (t + 1) * lines], rest], 1))
    return blocks


def gather_chips(natural, refs, core, chip):
    _, count, lines, _ = natural.shape
    for (own_ref, others_ref), side in zip((refs[:2], refs[2:]), (core, 1 - core)):
        for t in range(others_ref.shape[0] + 1):
            at = lax.bitwise_xor(chip, t) * 2 + side
            dense = others_ref[t - 1] if t > 0 else own_ref[...]
            for i, block in enumerate(unpack(dense, count, lines)):
                natural[at, i] = block


def pair_kernel(
    dims,
    q_ref, k_ref, v_ref, m_ref, kt_ref, vt_ref,
    b0_ref, b1_ref, b2_ref, b3_ref,
    after_ref,
    ot_ref, dqt_ref, dk_ref, dv_ref, near_ref, far_ref,
    bt, dbt, stack, natural,
):
    rows, heads, seq_n, res_n = dims
    step = pl.program_id(0)
    seq, res = lax.axis_index("seq"), lax.axis_index("res")
    core, chip = lax.rem(seq, 2), lax.div(seq, 2)
    n_keys = q_ref.shape[1]

    @pl.when(step == 0)
    def _():
        blocks = (b0_ref, b1_ref, b2_ref, b3_ref)
        gather_chips(natural, blocks, core, chip)
        for z in range(res_n):
            zi = lax.bitwise_xor(res, z)
            for s in range(seq_n):
                block = natural[s, zi]
                d = z * seq_n + s
                for h in range(heads):
                    at = h * n_keys + d * rows
                    stack[at : at + rows, :] = block[h * rows : (h + 1) * rows]
        bt[...] = stack[...].T
        dbt[...] = jnp.zeros_like(dbt)

    def pieces(ref, count):
        return [ref[0, :, t * LANES : (t + 1) * LANES] for t in range(count)]

    masks = [head_mask(h, BF16) for h in range(heads)]
    qs = [cat([a * mask for mask in masks], 0) for a in pieces(q_ref, 3)]
    ms = [cat([a * mask for mask in masks], 0) for a in pieces(m_ref, 2)]
    kcat = cat(left6(pieces(k_ref, 3)), 1)
    vcat = cat(left3(pieces(v_ref, 2)), 1)
    kt1, kt2 = kt_ref[0, :LANES], kt_ref[0, LANES:]
    vt1, vt2 = vt_ref[0, :LANES], vt_ref[0, LANES:]
    dk = jnp.zeros((n_keys, LANES), F32)
    dv = jnp.zeros((n_keys, LANES), F32)
    for c in range(heads * n_keys // TILE):
        cols = slice(c * TILE, (c + 1) * TILE)
        first, last = c * TILE // n_keys, ((c + 1) * TILE - 1) // n_keys
        band = slice(first * HEAD, (last + 1) * HEAD)
        lane = lax.broadcasted_iota(jnp.int32, (1, TILE), 1) + c * TILE

        def of_heads(top, low, a1, a2):
            both = nn(cat([top[band], low[band]], 0), a1)
            half = both.shape[0] // 2
            total = both[:half] + both[half:] + nn(top[band], a2)
            picked = total[:HEAD]
            for h in range(first + 1, last + 1):
                rest = total[(h - first) * HEAD : (h - first + 1) * HEAD]
                picked = jnp.where(lane >= h * n_keys, rest, picked)
            return picked

        qc = [a[cols] for a in qs]
        mc = [a[cols] for a in ms]
        s = nt(kcat, cat(right6(qc), 1)) + bt[:, cols]
        dp = nt(vcat, cat(right3(mc), 1))
        e = jnp.exp(s - jnp.max(s, axis=0, keepdims=True))
        p = e * (1.0 / jnp.sum(e, axis=0, keepdims=True))
        p1, p2 = split2(p)
        ot_ref[0, :, cols] = of_heads(vt1, vt2, p1, p2)
        ds = p * (dp - jnp.sum(p * dp, axis=0, keepdims=True))
        dbt[:, cols] = dbt[:, cols] + ds
        s1, s2 = split2(ds)
        dqt_ref[0, :, cols] = of_heads(kt1, kt2, s1, s2)
        both = nn(s1, cat(qc[:2], 1))
        dk = dk + both[:, :LANES] + both[:, LANES:] + nn(s2, qc[0])
        both = nn(p1, cat(mc, 1))
        dv = dv + both[:, :LANES] + both[:, LANES:] + nn(p2, mc[0])
    dk_ref[0] = dk
    dv_ref[0] = dv

    @pl.when(step == rows - 1)
    def _():
        stack[...] = dbt[...].T
        for z in range(res_n):
            zi = lax.bitwise_xor(res, z)
            for s in range(seq_n):
                ci = lax.bitwise_xor(chip, s // 2)
                d = z * seq_n + s
                at = [h * n_keys + d * rows for h in range(heads)]
                block = cat([stack[a : a + rows, :] for a in at], 0)

                @pl.when(core == s % 2)
                def _():
                    near_ref[ci, zi] = block

                @pl.when(core != s % 2)
                def _():
                    far_ref[ci, zi] = block


def pair_back_kernel(
    ot_ref, dqt_ref, dk_ref, dv_ref, dout_ref, sig_ref,
    g_ref, wb_ref, dn_ref,
):
    rows, length, feats = dk_ref.shape
    g = g_ref[...]
    w1, w2 = wb_ref[0], wb_ref[1]

    def lines(flat):
        heads = flat.shape[1] // length
        return cat([flat[:, h * length : (h + 1) * length] for h in range(heads)], 0).T

    for i in range(rows):
        o, sig = lines(ot_ref[i]), sig_ref[i]
        d_gate = dout_ref[i] * o * sig * (1.0 - sig)
        dq = lines(dqt_ref[i]) * (1.0 / math.sqrt(HEAD))
        t1, t2 = split2(cat([dq, dk_ref[i], dv_ref[i], d_gate], 1))
        dn_ref[i] = g * (nt(t1, w1) + nt(t1, w2) + nt(t2, w1))


def msa_project_kernel(
    y0_ref, y1_ref, y2_ref, y3_ref, adj_hbm,
    g_ref, wq_hbm, wk_hbm, wv_hbm, wg_hbm, wo_hbm,
    q_ref, m_ref, dout_ref, sig_ref, k_ref, v_ref, wkv_ref, wqg_ref,
    yall, adj_ref, wq_ref, wk_ref, wv_ref, wg_ref, wo_ref, sem,
):
    res = lax.axis_index("res")
    n_seqs, own, feats = adj_ref.shape
    n_keys = yall.shape[1]
    g = g_ref[...]
    copies = fetch(
        [
            (wk_hbm, wk_ref), (wv_hbm, wv_ref), (wq_hbm, wq_ref), (wg_hbm, wg_ref),
            (wo_hbm, wo_ref), (adj_hbm, adj_ref),
        ],
        sem,
    )
    for t, ref in enumerate((y0_ref, y1_ref, y2_ref, y3_ref)):
        at = pl.multiple_of(lax.bitwise_xor(res, t) * own, own)
        for b in range(n_seqs):
            yall[b, pl.ds(at, own), :] = ref[b * own : (b + 1) * own, :]
    n_own, _ = normed(y0_ref[: n_seqs * own])
    n_all, _ = normed(yall[...].reshape(n_seqs * n_keys, feats))
    own_parts, all_parts = split3(n_own * g), split3(n_all * g)
    for copy in copies:
        copy.wait()
    for ref, pair in ((wkv_ref, (wk_ref, wv_ref)), (wqg_ref, (wq_ref, wg_ref))):
        top, low = split2(cat([pair[0][...], pair[1][...]], 1))
        ref[0] = top
        ref[1] = low
    q = nn(cat(left6(own_parts), 1), cat(right6(split3(wq_ref[...])), 0))
    gate = nn(cat(left3(own_parts), 1), cat(right3(split2(wg_ref[...])), 0))
    k = nn(cat(left6(all_parts), 1), cat(right6(split3(wk_ref[...])), 0))
    v = nn(cat(left3(all_parts), 1), cat(right3(split2(wv_ref[...])), 0))
    adj = adj_ref[...].reshape(n_seqs * own, feats)
    d_out = nt(cat(left3(split2(adj)), 1), cat(right3(split2(wo_ref[...])), 1))
    sig = jax.nn.sigmoid(gate)
    q_ref[...] = q * (1.0 / math.sqrt(HEAD))
    m_ref[...] = d_out * sig
    dout_ref[...] = d_out
    sig_ref[...] = sig
    k_ref[...] = k
    v_ref[...] = v


def msa_kernel(
    dims,
    q_ref, m_ref, k_ref, v_ref,
    b0_ref, b1_ref, b2_ref, b3_ref,
    wkv_ref,
    o_ref, dq_ref, r0_ref, r1_ref, r23_ref, near_ref, far_ref,
    bias, dbias, dyall, natural,
):
    rows, heads, seq_n, res_n = dims
    seq, res = lax.axis_index("seq"), lax.axis_index("res")
    core, chip = lax.rem(seq, 2), lax.div(seq, 2)
    n_seqs, n_keys, feats = dyall.shape
    own = n_keys // res_n
    tiles, group = feats // LANES, LANES // HEAD
    blocks = (b0_ref, b1_ref, b2_ref, b3_ref)
    gather_chips(natural, blocks, core, chip)
    for s in range(seq_n):
        block = cat([natural[s, res_n], natural[s, res_n + 1]], 0)
        for h in range(heads):
            at = h * own + s * rows
            bias[at : at + rows, :] = block[h * rows : (h + 1) * rows]
    masks = [head_mask(u, BF16) for u in range(group)]
    fmasks = [head_mask(u, F32) for u in range(group)]

    def stacked(a, by):
        return cat([a * mask for mask in by], 0)

    def own_rows(full):
        total = fmasks[0] * full[:own]
        for u in range(1, group):
            total = total + fmasks[u] * full[u * own : (u + 1) * own]
        return total

    b1, b2 = wkv_ref[0], wkv_ref[1]
    for b in range(n_seqs):
        near = slice(b * own, (b + 1) * own)
        wide = slice(b * n_keys, (b + 1) * n_keys)
        dkt, dvt = [], []
        for t in range(tiles):
            cols = slice(t * LANES, (t + 1) * LANES)
            lines = slice(t * group * own, (t + 1) * group * own)
            q_t, m_t = q_ref[near, cols], m_ref[near, cols]
            qs = [stacked(a, masks) for a in split3(q_t)]
            ms = [stacked(a, masks) for a in split2(m_t)]
            qt1, qt2 = split2(stacked(q_t, fmasks).T)
            mt1, mt2 = split2(stacked(m_t, fmasks).T)
            kp = split3(k_ref[wide, cols])
            vp = split2(v_ref[wide, cols])
            s = nt(cat(left6(qs), 1), cat(right6(kp), 1)) + bias[lines]
            dp = nt(cat(left3(ms), 1), cat(right3(vp), 1))
            e = jnp.exp(s - jnp.max(s, axis=1, keepdims=True))
            p = e * (1.0 / jnp.sum(e, axis=1, keepdims=True))
            p1, p2 = split2(p)
            both = nn(p1, cat(vp, 1))
            o_ref[near, cols] = own_rows(both[:, :LANES] + both[:, LANES:] + nn(p2, vp[0]))
            ds = p * (dp - jnp.sum(p * dp, axis=1, keepdims=True))
            dbias[lines] = ds if b == 0 else dbias[lines] + ds
            s1, s2 = split2(ds)
            both = nn(s1, cat(kp[:2], 1))
            dq_ref[near, cols] = own_rows(both[:, :LANES] + both[:, LANES:] + nn(s2, kp[0]))
            both = nn(cat([qt1, qt2], 0), s1)
            dkt.append(both[:LANES] + both[LANES:] + nn(qt1, s2))
            both = nn(cat([mt1, mt2], 0), p1)
            dvt.append(both[:LANES] + both[LANES:] + nn(mt1, p2))
        t1, t2 = split2(cat([a.T for a in dkt + dvt], 1))
        dyall[b] = nt(t1, b1) + nt(t1, b2) + nt(t2, b1)
    for t, (ref, base) in enumerate(((r0_ref, 0), (r1_ref, 0), (r23_ref, 0), (r23_ref, n_seqs))):
        at = pl.multiple_of(lax.bitwise_xor(res, t) * own, own)
        for b in range(n_seqs):
            to = (base + b) * own
            ref[to : to + own, :] = dyall[b, pl.ds(at, own), :]
    for s in range(seq_n):
        ci = lax.bitwise_xor(chip, s // 2)
        at = [h * own + s * rows for h in range(heads)]
        block = cat([dbias[a : a + rows, :] for a in at], 0)

        @pl.when(core == s % 2)
        def _():
            near_ref[ci] = block

        @pl.when(core != s % 2)
        def _():
            far_ref[ci] = block


def aligned_back_kernel(o_ref, dq_ref, dout_ref, sig_ref, wqg_ref, r0_ref, dy_ref):
    sig = sig_ref[...]
    d_gate = dout_ref[...] * o_ref[...] * sig * (1.0 - sig)
    t1, t2 = split2(cat([dq_ref[...] * (1.0 / math.sqrt(HEAD)), d_gate], 1))
    b1, b2 = wqg_ref[0], wqg_ref[1]
    dy_ref[...] = nt(t1, b1) + nt(t1, b2) + nt(t2, b1) + r0_ref[...]


def aligned_end_kernel(y_ref, g_ref, dy_ref, r23_ref, r1_ref, out_ref):
    n_seqs, own, _ = out_ref.shape
    g = g_ref[...]
    for b in range(n_seqs):
        at = slice(b * own, (b + 1) * own)
        n, scale = normed(y_ref[at])
        out_ref[b] = normed_back(n, scale, g * (dy_ref[at] + r23_ref[at] + r1_ref[at]))


def stack_kernel(length, p0_ref, p1_ref, p2_ref, p3_ref, m_ref, after_ref, out_ref):
    lines = m_ref.shape[0] // 2
    blocks = [ref[ref.shape[0] - lines :, :length] for ref in (p0_ref, p1_ref, p2_ref, p3_ref)]
    blocks += [m_ref[:lines], m_ref[lines:]]
    pack(lambda t: blocks[t], len(blocks), lines, out_ref)


def chip_stack_kernel(b1_ref, b2_ref, b3_ref, after_ref, out_ref):
    for t, ref in enumerate((b1_ref, b2_ref, b3_ref)):
        out_ref[t] = ref[...]


def core_sum_kernel(p0_ref, p1_ref, m0_ref, m1_ref, after_ref, s0_ref, s1_ref, s2_ref, s3_ref):
    res_n, lines = p0_ref.shape[1:3]
    for t, ref in enumerate((s0_ref, s1_ref, s2_ref, s3_ref)):
        pair = p0_ref[t] + p1_ref[t]
        msa = m0_ref[t] + m1_ref[t]
        blocks = [pair[z] for z in range(res_n)] + [msa[:lines], msa[lines:]]
        pack(lambda i: blocks[i], len(blocks), lines, ref)


def chip_sum_kernel(
    s0_ref, s1_ref, s2_ref, s3_ref, r1_ref, r23_ref, after_ref,
    c0_ref, joint_ref, c2_ref, c3_ref, m_ref,
):
    lines, length = c0_ref.shape
    base = r1_ref.shape[0]
    joint_ref[:base] = r1_ref[...] + r23_ref[base:]
    if length < joint_ref.shape[1]:
        joint_ref[base:, length:] = jnp.zeros((lines, joint_ref.shape[1] - length), F32)
    total = s0_ref[...] + s1_ref[...] + s2_ref[...] + s3_ref[...]
    blocks = unpack(total, 2 * total.shape[0] // (3 * lines), lines)
    for t, ref in enumerate((c0_ref, joint_ref, c2_ref, c3_ref)):
        if t == 1:
            ref[base:, :length] = blocks[t]
        else:
            ref[...] = blocks[t]
    m_ref[:lines] = blocks[-2]
    m_ref[lines:] = blocks[-1]


def pair_end_kernel(
    n_ref, scale_ref, dn_ref, p0_ref, p1_ref, p2_ref, p3_ref, m_ref, wj_ref, out_ref
):
    rows, length, feats = n_ref.shape
    lines = p0_ref.shape[0]
    pair = p0_ref[...] + p2_ref[...] + p3_ref[...]
    pair = pair + p1_ref[p1_ref.shape[0] - lines :, :length]
    msa = m_ref[...]
    pad = jnp.zeros((LANES - pair.shape[0] - msa.shape[0], length), F32)
    b = cat([pair, msa, pad], 0).T
    more = nn(cat(left3(split2(b)), 1), wj_ref[...])
    for j in range(rows):
        dn = dn_ref[j] + more[:, j * feats : (j + 1) * feats]
        out_ref[j] = normed_back(n_ref[j], scale_ref[j], dn)


MIB = 1 << 20


def params(mib, **more):
    return pltpu.CompilerParams(vmem_limit_bytes=mib * MIB, **more)


def hbm(count):
    return [pl.BlockSpec(memory_space=pltpu.HBM)] * count


def vmem(count):
    return [pl.BlockSpec(memory_space=pltpu.VMEM)] * count


def swap(values, axis, size, offset):
    return lax.ppermute(values, axis, [(i, i ^ offset) for i in range(size)])


def fused_on_device(
    seq_n,
    res_n,
    coupled_embedding,
    aligned_embedding,
    coupled_change_adjoint,
    aligned_change_adjoint,
    coupled_scaler,
    coupled_asking_matrix,
    coupled_lookup_matrix,
    coupled_content_matrix,
    coupled_sigmoid_matrix,
    coupled_offset_matrix,
    coupled_result_matrix,
    aligned_scaler,
    coupled_scaler_for_offset,
    aligned_asking_matrix,
    aligned_lookup_matrix,
    aligned_content_matrix,
    aligned_sigmoid_matrix,
    aligned_offset_matrix,
    aligned_result_matrix,
):
    rows, length, feats = coupled_embedding.shape
    n_seqs, own, wide = aligned_embedding.shape
    hp, hm = HP, ALIGNED_SPLITS
    chips = seq_n // 2
    shape = lambda *s: jax.ShapeDtypeStruct(s, F32)
    wp_t, wm_t = coupled_offset_matrix.T, aligned_offset_matrix.T
    gain = coupled_scaler.reshape(1, feats)
    gain2 = coupled_scaler_for_offset.reshape(1, feats)

    lines, base = hp * rows, n_seqs * own
    mixed_rows, msa_rows = pl.pallas_call(
        functools.partial(bias_kernel, rows),
        out_shape=(shape(base + lines, wide), shape(hm * rows, length)),
        compiler_params=params(63),
        name="bias_rows",
    )(
        coupled_embedding, aligned_embedding.reshape(base, wide), gain, wp_t, gain2, wm_t
    )
    columns = [mixed_rows] + [swap(mixed_rows, "res", res_n, t) for t in range(1, res_n)]

    bf = lambda *s: jax.ShapeDtypeStruct(s, BF16)
    q, k, v, m, kt, vt, d_out, sig, n, scale, wj, wb = pl.pallas_call(
        pair_project_kernel,
        in_specs=hbm(2) + vmem(1) + hbm(5) + vmem(3),
        scratch_shapes=[pltpu.VMEM((rows, length, feats), F32)] * 2
        + [pltpu.VMEM((feats, feats), F32)] * 5 + [pltpu.SemaphoreType.DMA((7,))],
        out_shape=(
            bf(rows, length, 3 * feats), bf(rows, length, 3 * feats),
            bf(rows, length, 2 * feats), bf(rows, length, 2 * feats),
            bf(rows, 2 * feats, length), bf(rows, 2 * feats, length),
        ) + (shape(rows, length, feats),) * 4
        + (bf(3 * LANES, rows * feats), bf(2, feats, 4 * feats)),
        compiler_params=params(32),
        name="pair_project",
        cost_estimate=pl.CostEstimate(flops=2 * 10**9, bytes_accessed=10**7, transcendentals=0),
    )(
        coupled_embedding, coupled_change_adjoint, gain, coupled_asking_matrix,
        coupled_lookup_matrix, coupled_content_matrix, coupled_sigmoid_matrix,
        coupled_result_matrix, wp_t, gain2, wm_t,
    )

    joint = (3 * (res_n + 2) * lines // 2, LANES)
    spread = pltpu.VMEM((seq_n, res_n + 2, lines, length), F32)
    after = [pl.BlockSpec(memory_space=pl.ANY)]
    first = pl.pallas_call(
        functools.partial(stack_kernel, length),
        in_specs=vmem(5) + after,
        out_shape=shape(*joint),
        compiler_params=params(16),
        name="stack_rows",
    )(*columns, msa_rows, n)

    wide_gain = aligned_scaler.reshape(1, wide)
    flat = lambda count: shape(n_seqs * count, wide)
    mq, mm, m_out, m_sig, mk, mv, wkv, wqg = pl.pallas_call(
        msa_project_kernel,
        in_specs=vmem(4) + hbm(1) + vmem(1) + hbm(5),
        out_shape=(flat(own),) * 4 + (flat(length),) * 2 + (bf(2, wide, 2 * wide),) * 2,
        scratch_shapes=[
            pltpu.VMEM((n_seqs, length, wide), F32), pltpu.VMEM((n_seqs, own, wide), F32),
        ] + [pltpu.VMEM((wide, wide), F32)] * 5 + [pltpu.SemaphoreType.DMA((6,))],
        compiler_params=params(32),
        name="msa_project",
        cost_estimate=pl.CostEstimate(flops=10**9, bytes_accessed=10**7, transcendentals=0),
    )(
        *columns, aligned_change_adjoint, wide_gain, aligned_asking_matrix,
        aligned_lookup_matrix, aligned_content_matrix, aligned_sigmoid_matrix,
        aligned_result_matrix,
    )

    rest = pl.pallas_call(
        chip_stack_kernel,
        in_specs=vmem(3) + after,
        out_shape=shape(chips - 1, *joint),
        compiler_params=params(16),
        name="stack_chips",
    )(*[swap(first, "seq", seq_n, 2 * t) for t in range(1, chips)], mq)
    blocks = [first, rest, swap(first, "seq", seq_n, 1), swap(rest, "seq", seq_n, 1)]

    stretch = pltpu.VMEM((hm * own, length), F32)
    o, dq, kept, r1, r23, msa_near, msa_far = pl.pallas_call(
        functools.partial(msa_kernel, (rows, hm, seq_n, res_n)),
        out_shape=(flat(own),) * 4 + (shape(2 * base, wide),)
        + (shape(chips, hm * rows, length),) * 2,
        scratch_shapes=[
            stretch, stretch, pltpu.VMEM((n_seqs, length, wide), F32),
            spread,
        ],
        compiler_params=params(32),
        name="msa_attention",
        cost_estimate=pl.CostEstimate(flops=4 * 10**9, bytes_accessed=10**7, transcendentals=0),
    )(
        mq, mm, mk, mv, *blocks, wkv,
    )
    far_msa = swap(msa_far, "seq", seq_n, 1)
    r23 = swap(r23, "res", res_n, 2)

    piece = lambda *s: pl.BlockSpec((1,) + s, lambda i: (i, 0, 0))
    whole = lambda *s: pl.BlockSpec(s, lambda i: (0,) * len(s))
    quarter = (chips, res_n, lines, length)
    ot, dqt, dk, dv, near, far = pl.pallas_call(
        functools.partial(pair_kernel, (rows, hp, seq_n, res_n)),
        grid=(rows,),
        in_specs=[
            piece(length, 3 * feats), piece(length, 3 * feats),
            piece(length, 2 * feats), piece(length, 2 * feats),
            piece(2 * feats, length), piece(2 * feats, length),
        ] + [whole(*joint), whole(chips - 1, *joint)] * 2 + after,
        out_specs=(
            piece(HEAD, hp * length), piece(HEAD, hp * length),
            piece(length, feats), piece(length, feats), whole(*quarter), whole(*quarter),
        ),
        out_shape=(
            shape(rows, HEAD, hp * length), shape(rows, HEAD, hp * length),
            shape(rows, length, feats), shape(rows, length, feats),
            shape(*quarter), shape(*quarter),
        ),
        scratch_shapes=[
            pltpu.VMEM((length, hp * length), F32),
            pltpu.VMEM((length, hp * length), F32),
            pltpu.VMEM((hp * length, length), F32),
            spread,
        ],
        compiler_params=params(32),
        name="pair_attention",
        cost_estimate=pl.CostEstimate(flops=10**10, bytes_accessed=10**7, transcendentals=0),
    )(q, k, v, m, kt, vt, *blocks, kept)
    far_pair = swap(far, "seq", seq_n, 1)
    dn = pl.pallas_call(
        pair_back_kernel,
        out_shape=shape(rows, length, feats),
        compiler_params=params(32),
        name="pair_back",
        cost_estimate=pl.CostEstimate(flops=10**9, bytes_accessed=10**7, transcendentals=0),
    )(
        ot, dqt, dk, dv, d_out, sig, gain, wb,
    )
    sums = pl.pallas_call(
        core_sum_kernel,
        in_specs=vmem(4) + after,
        out_shape=(shape(*joint),) * chips,
        compiler_params=params(16),
        name="core_sum",
    )(near, far_pair, msa_near, far_msa, dn)
    dy = pl.pallas_call(
        aligned_back_kernel,
        out_shape=flat(own),
        compiler_params=params(16),
        name="aligned_back",
        cost_estimate=pl.CostEstimate(flops=10**9, bytes_accessed=10**6, transcendentals=0),
    )(o, dq, m_out, m_sig, wqg, kept)
    c0, mixed_sum, c2, c3, msa_sum = pl.pallas_call(
        chip_sum_kernel,
        in_specs=vmem(6) + after,
        out_shape=(
            shape(lines, length), shape(base + lines, wide), shape(lines, length),
            shape(lines, length), shape(hm * rows, length),
        ),
        compiler_params=params(16),
        name="chip_sum",
    )(sums[0], *[swap(sums[t], "seq", seq_n, 2 * t) for t in range(1, chips)], r1, r23, dy)
    mixed_sum, c2, c3 = [swap(a, "res", res_n, t) for a, t in ((mixed_sum, 1), (c2, 2), (c3, 3))]

    aligned_out = pl.pallas_call(
        aligned_end_kernel,
        out_shape=shape(n_seqs, own, wide),
        compiler_params=params(16),
        name="aligned_end",
    )(mixed_rows, wide_gain, dy, r23, mixed_sum)
    coupled_out = pl.pallas_call(
        pair_end_kernel,
        out_shape=shape(rows, length, feats),
        compiler_params=params(16),
        name="pair_end",
    )(n, scale, dn, c0, mixed_sum, c2, c3, msa_sum, wj)
    return coupled_out, aligned_out


def on_device(seq_n, res_n, *arrays):
    length = arrays[0].shape[1]
    rows = arrays[0].shape[0]
    narrow = length <= arrays[1].shape[2] and HP * length % TILE == 0
    narrow = narrow and rows * (HP + ALIGNED_SPLITS) <= LANES
    narrow = narrow and ALIGNED_SPLITS == 2 * HP and 2 * (length - LANES) == LANES
    if narrow and seq_n == 8 and res_n == 4:
        return fused_on_device(seq_n, res_n, *arrays)
    return scanned_on_device(*arrays)


def solution(mesh):
    in_specs = (
        P(("res", "seq"), None, None),
        P("seq", "res", None),
        P(("res", "seq"), None, None),
        P("seq", "res", None),
        P(),
        P(),
        P(),
        P(),
        P(),
        P(),
        P(),
        P(),
        P(),
        P(),
        P(),
        P(),
        P(),
        P(),
        P(),
    )
    out_specs = (P(("res", "seq"), None, None), P("seq", "res", None))
    return jax.shard_map(
        functools.partial(on_device, mesh.shape["seq"], mesh.shape["res"]),
        mesh=mesh, in_specs=in_specs, out_specs=out_specs, check_vma=False
    )
```

```python
import functools
import math

import jax
import jax.numpy as jnp
from jax import lax
from jax.experimental import pallas as pl
from jax.experimental.pallas import tpu as pltpu
from jax.sharding import PartitionSpec as P

HP = 4
ALIGNED_SPLITS = 8


EXACT_MATMUL = lax.Precision.HIGHEST
EPSILON = 1e-05


def standardize_features(values, norm_gain):
    center = values - jnp.mean(values, axis=-1, keepdims=True)
    spread = jnp.mean(center * center, axis=-1, keepdims=True)
    return center * lax.rsqrt(spread + EPSILON) * norm_gain


def affine_map(values, weight):
    return jnp.einsum("...c,ce->...e", values, weight, precision=EXACT_MATMUL)


def sigmoid_mixing(query_vectors, key_rows, value_rows, gate_preact, softmax_offset, head_count):
    query_shape = query_vectors.shape
    head_width = query_shape[-1] // head_count
    query_heads = query_vectors.reshape(query_shape[:-1] + (head_count, head_width))
    key_heads = key_rows.reshape(key_rows.shape[:-1] + (head_count, head_width))
    value_heads = value_rows.reshape(value_rows.shape[:-1] + (head_count, head_width))
    logits = (
        jnp.einsum("...qhd,...khd->...qhk", query_heads, key_heads, precision=EXACT_MATMUL)
        / math.sqrt(head_width)
        + softmax_offset
    )
    largest = lax.stop_gradient(jnp.max(logits, axis=-1, keepdims=True))
    weights = jnp.exp(logits - largest)
    weights = weights / jnp.sum(weights, axis=-1, keepdims=True)
    mixed_contents = jnp.einsum(
        "...qhk,...khd->...qhd", weights, value_heads, precision=EXACT_MATMUL
    )
    return mixed_contents.reshape(query_shape) * jax.nn.sigmoid(gate_preact)


def scanned_on_device(
    coupled_embedding,
    aligned_embedding,
    coupled_change_adjoint,
    aligned_change_adjoint,
    coupled_scaler,
    coupled_asking_matrix,
    coupled_lookup_matrix,
    coupled_content_matrix,
    coupled_sigmoid_matrix,
    coupled_offset_matrix,
    coupled_result_matrix,
    aligned_scaler,
    coupled_scaler_for_offset,
    aligned_asking_matrix,
    aligned_lookup_matrix,
    aligned_content_matrix,
    aligned_sigmoid_matrix,
    aligned_offset_matrix,
    aligned_result_matrix,
):

    def pair_local(entering_lines):
        standardized_source = standardize_features(entering_lines, coupled_scaler)
        return (
            affine_map(standardized_source, coupled_asking_matrix),
            affine_map(standardized_source, coupled_lookup_matrix),
            affine_map(standardized_source, coupled_content_matrix),
            affine_map(standardized_source, coupled_sigmoid_matrix),
            jnp.einsum(
                "jkc,ch->jhk", standardized_source, coupled_offset_matrix, precision=EXACT_MATMUL
            ),
        )

    (row_queries, row_keys, row_values, row_gates, bias_rows), pair_back = jax.vjp(
        pair_local, coupled_embedding
    )
    by_seq = lax.all_gather(bias_rows, "seq", axis=0, tiled=True)
    full_bias = lax.all_gather(by_seq, "res", axis=0, tiled=True)

    def row_output(one_query, one_key, one_value, one_gate, softmax_offset):
        return affine_map(
            sigmoid_mixing(one_query, one_key, one_value, one_gate, softmax_offset, HP),
            coupled_result_matrix,
        )

    def row_step(bias_sum, row_items):
        one_query, one_key, one_value, one_gate, one_cotan = row_items
        discarded_entry, row_back = jax.vjp(
            row_output, one_query, one_key, one_value, one_gate, full_bias
        )
        grad_query, grad_key, grad_value, grad_gate, grad_bias = row_back(one_cotan)
        return (bias_sum + grad_bias, (grad_query, grad_key, grad_value, grad_gate))

    bias_total, row_grads = lax.scan(
        row_step,
        jnp.zeros_like(full_bias),
        (row_queries, row_keys, row_values, row_gates, coupled_change_adjoint),
    )
    by_res = lax.psum_scatter(bias_total, "res", scatter_dimension=0, tiled=True)
    bias_grad_rows = lax.psum_scatter(by_res, "seq", scatter_dimension=0, tiled=True)
    (mixed_result_sensitivity,) = pair_back(row_grads + (bias_grad_rows,))

    def aligned_offset_portion(entering_lines):
        return jnp.einsum(
            "gys,sj->gjy",
            standardize_features(entering_lines, coupled_scaler_for_offset),
            aligned_offset_matrix,
            precision=EXACT_MATMUL,
        )

    aligned_offset_part, aligned_offset_reverse = jax.vjp(aligned_offset_portion, coupled_embedding)
    tile_softmax_offset = lax.all_gather(aligned_offset_part, "seq", axis=0, tiled=True)

    def sequence_output(query_vectors, full_key_rows, full_value_rows, gate_preact, softmax_offset):
        return affine_map(
            sigmoid_mixing(
                query_vectors,
                full_key_rows,
                full_value_rows,
                gate_preact,
                softmax_offset,
                ALIGNED_SPLITS,
            ),
            aligned_result_matrix,
        )

    state_all = lax.all_gather(aligned_embedding, "res", axis=1, tiled=True)

    def near_local(carry_pile):
        standardized_source = standardize_features(carry_pile, aligned_scaler)
        return (
            affine_map(standardized_source, aligned_asking_matrix),
            affine_map(standardized_source, aligned_sigmoid_matrix),
        )

    def keys_local(carry_pile):
        standardized_source = standardize_features(carry_pile, aligned_scaler)
        return (
            affine_map(standardized_source, aligned_lookup_matrix),
            affine_map(standardized_source, aligned_content_matrix),
        )

    (aligned_asking_lines, aligned_sigmoid_factors), near_back = jax.vjp(
        near_local, aligned_embedding
    )
    (full_key_rows, full_value_rows), keys_back = jax.vjp(keys_local, state_all)
    discarded_entry, sigmoid_mixing_reverse = jax.vjp(
        sequence_output,
        aligned_asking_lines,
        full_key_rows,
        full_value_rows,
        aligned_sigmoid_factors,
        tile_softmax_offset,
    )
    query_gradient, full_key_gradient, full_value_gradient, gate_gradient, block_bias_gradient = (
        sigmoid_mixing_reverse(aligned_change_adjoint)
    )
    (state_term,) = keys_back((full_key_gradient, full_value_gradient))
    spread_grad = lax.psum_scatter(state_term, "res", scatter_dimension=1, tiled=True)
    (near_grad,) = near_back((query_gradient, gate_gradient))
    aligned_embedding_sensitivity = near_grad + spread_grad
    offset_line_sensitivity = lax.psum_scatter(
        block_bias_gradient, "seq", scatter_dimension=0, tiled=True
    )
    (coupled_sensitivity_via_offset,) = aligned_offset_reverse(offset_line_sensitivity)
    return (
        mixed_result_sensitivity + coupled_sensitivity_via_offset,
        aligned_embedding_sensitivity,
    )


F32 = jnp.float32
BF16 = jnp.bfloat16
HEAD = 32
LANES = 128
TILE = 256


def split2(a):
    top = a.astype(BF16)
    return top, (a - top.astype(F32)).astype(BF16)


def split3(a):
    top = a.astype(BF16)
    rest = a - top.astype(F32)
    mid = rest.astype(BF16)
    return top, mid, (rest - mid.astype(F32)).astype(BF16)


def left6(parts):
    a, b, c = parts
    return [a, a, b, b, a, c]


def right6(parts):
    a, b, c = parts
    return [a, b, a, b, c, a]


def left3(parts):
    return [parts[0], parts[0], parts[1]]


def right3(parts):
    return [parts[0], parts[1], parts[0]]


def nn(a, b):
    return lax.dot_general(a, b, (((1,), (0,)), ((), ())), preferred_element_type=F32)


def nt(a, b):
    return lax.dot_general(a, b, (((1,), (1,)), ((), ())), preferred_element_type=F32)


def cat(parts, axis):
    return jnp.concatenate(parts, axis=axis)


def normed(v):
    center = v - jnp.mean(v, axis=-1, keepdims=True)
    spread = jnp.mean(center * center, axis=-1, keepdims=True)
    scale = lax.rsqrt(spread + EPSILON)
    return center * scale, scale


def normed_back(n, scale, dn):
    return scale * (
        dn - jnp.mean(dn, axis=-1, keepdims=True) - n * jnp.mean(dn * n, axis=-1, keepdims=True)
    )


def head_mask(h, dtype):
    lane = lax.broadcasted_iota(jnp.int32, (1, LANES), 1)
    return jnp.where((lane // HEAD) == h, 1.0, 0.0).astype(dtype)


def pack(block_of, count, lines, out_ref):
    half = count // 2
    for t in range(half):
        first, second = block_of(t), block_of(t + half)
        out_ref[t * lines : (t + 1) * lines] = first[:, :LANES]
        out_ref[(t + half) * lines : (t + half + 1) * lines] = second[:, :LANES]
        rest = cat([first[:, LANES:], second[:, LANES:]], 1)
        out_ref[(t + count) * lines : (t + count + 1) * lines] = rest


def unpack(dense, count, lines):
    half = count // 2
    blocks = []
    for t in range(count):
        rest = dense[(count + t % half) * lines : (count + t % half + 1) * lines]
        rest = rest[:, : LANES // 2] if t < half else rest[:, LANES // 2 :]
        blocks.append(cat([dense[t * lines : (t + 1) * lines], rest], 1))
    return blocks


def bias_kernel(rows, x_ref, y_ref, g_ref, wp_ref, g2_ref, wm_ref, joint_ref, packed_ref, bm_ref):
    length = x_ref.shape[1]
    base, wide = y_ref.shape
    joint_ref[:base] = y_ref[...]
    if length < wide:
        joint_ref[base:, length:] = jnp.zeros((wp_ref.shape[0] * rows, wide - length), F32)
    hp, hm = wp_ref.shape[0], wm_ref.shape[0]
    w = cat([wp_ref[...] * g_ref[...], wm_ref[...] * g2_ref[...]], 0)
    wcat = cat(left6(split3(w)), 1)
    for j in range(rows):
        n, _ = normed(x_ref[j])
        res = nt(wcat, cat(right6(split3(n)), 1))
        for h in range(hp):
            at = base + h * rows + j
            joint_ref[at : at + 1, :length] = res[h : h + 1]
        for h in range(hm):
            bm_ref[h * rows + j : h * rows + j + 1, :] = res[hp + h : hp + h + 1]
    lines = hp * rows
    pack(lambda t: bm_ref[t * lines : (t + 1) * lines], hm // hp, lines, packed_ref)


def pair_project_kernel(
    x_ref, adj_ref, g_ref, wq_ref, wk_ref, wv_ref, wg_ref, wo_ref, wp_ref, g2_ref, wm_ref,
    q_ref, k_ref, v_ref, m_ref, kt_ref, vt_ref, dout_ref, sig_ref, n_ref, scale_ref, wj_ref, wb_ref,
):
    rows, length, feats = x_ref.shape
    g = g_ref[...]
    top, low = split2(cat([wq_ref[...], wk_ref[...], wv_ref[...], wg_ref[...]], 1))
    wb_ref[0] = top
    wb_ref[1] = low
    w6 = cat(right6(split3(cat([wq_ref[...], wk_ref[...]], 1))), 0)
    w3 = cat(right3(split2(cat([wv_ref[...], wg_ref[...]], 1))), 0)
    wo3 = cat(right3(split2(wo_ref[...])), 1)
    for i in range(rows):
        n, scale = normed(x_ref[i])
        n_ref[i] = n
        scale_ref[i] = jnp.broadcast_to(scale, n.shape)
        parts = split3(n * g)
        qk = nn(cat(left6(parts), 1), w6)
        vg = nn(cat(left3(parts), 1), w3)
        d_out = nt(cat(left3(split2(adj_ref[i])), 1), wo3)
        sig = jax.nn.sigmoid(vg[:, feats:])
        dout_ref[i] = d_out
        sig_ref[i] = sig
        q, k, v = qk[:, :feats] * (1.0 / math.sqrt(HEAD)), qk[:, feats:], vg[:, :feats]
        q_ref[i] = cat(split3(q), 1)
        k_ref[i] = cat(split3(k), 1)
        v_ref[i] = cat(split2(v), 1)
        m_ref[i] = cat(split2(d_out * sig), 1)
        kt_ref[i] = cat(split2(k.T), 0)
        vt_ref[i] = cat(split2(v.T), 0)
    hp, hm = wp_ref.shape[0], wm_ref.shape[0]
    w = cat([wp_ref[...] * g, wm_ref[...] * g2_ref[...]], 0)
    lines = [jnp.broadcast_to(w[h : h + 1], (rows, feats)) for h in range(hp + hm)]
    lines += [jnp.zeros((LANES - rows * (hp + hm), feats), F32)]
    spread = cat(lines, 0)
    at = lax.broadcasted_iota(jnp.int32, (LANES, 1), 0)
    for j in range(rows):
        mine = jnp.where(lax.rem(at, rows) == j, spread, 0.0)
        wj_ref[:, j * feats : (j + 1) * feats] = cat(right3(split2(mine)), 0)


def gather_chips(natural, refs, core, chip):
    _, count, lines, _ = natural.shape
    for (own_ref, others_ref), side in zip((refs[:2], refs[2:]), (core, 1 - core)):
        for t in range(others_ref.shape[0] + 1):
            at = lax.bitwise_xor(chip, t) * 2 + side
            dense = others_ref[t - 1] if t > 0 else own_ref[...]
            for i, block in enumerate(unpack(dense, count, lines)):
                natural[at, i] = block


def pair_kernel(
    dims,
    q_ref, k_ref, v_ref, m_ref, kt_ref, vt_ref,
    b0_ref, b1_ref, b2_ref, b3_ref,
    after_ref,
    ot_ref, dqt_ref, dk_ref, dv_ref, near_ref, far_ref,
    bt, dbt, stack, natural,
):
    rows, heads, seq_n, res_n = dims
    step = pl.program_id(0)
    seq, res = lax.axis_index("seq"), lax.axis_index("res")
    core, chip = lax.rem(seq, 2), lax.div(seq, 2)
    n_keys = q_ref.shape[1]

    @pl.when(step == 0)
    def _():
        blocks = (b0_ref, b1_ref, b2_ref, b3_ref)
        gather_chips(natural, blocks, core, chip)
        for z in range(res_n):
            zi = lax.bitwise_xor(res, z)
            for s in range(seq_n):
                block = natural[s, zi]
                d = z * seq_n + s
                for h in range(heads):
                    at = h * n_keys + d * rows
                    stack[at : at + rows, :] = block[h * rows : (h + 1) * rows]
        bt[...] = stack[...].T
        dbt[...] = jnp.zeros_like(dbt)

    def pieces(ref, count):
        return [ref[0, :, t * LANES : (t + 1) * LANES] for t in range(count)]

    masks = [head_mask(h, BF16) for h in range(heads)]
    qs = [cat([a * mask for mask in masks], 0) for a in pieces(q_ref, 3)]
    ms = [cat([a * mask for mask in masks], 0) for a in pieces(m_ref, 2)]
    kcat = cat(left6(pieces(k_ref, 3)), 1)
    vcat = cat(left3(pieces(v_ref, 2)), 1)
    kt1, kt2 = kt_ref[0, :LANES], kt_ref[0, LANES:]
    vt1, vt2 = vt_ref[0, :LANES], vt_ref[0, LANES:]
    dk = jnp.zeros((n_keys, LANES), F32)
    dv = jnp.zeros((n_keys, LANES), F32)
    for c in range(heads * n_keys // TILE):
        cols = slice(c * TILE, (c + 1) * TILE)
        first, last = c * TILE // n_keys, ((c + 1) * TILE - 1) // n_keys
        band = slice(first * HEAD, (last + 1) * HEAD)
        lane = lax.broadcasted_iota(jnp.int32, (1, TILE), 1) + c * TILE

        def of_heads(top, low, a1, a2):
            both = nn(cat([top[band], low[band]], 0), a1)
            half = both.shape[0] // 2
            total = both[:half] + both[half:] + nn(top[band], a2)
            picked = total[:HEAD]
            for h in range(first + 1, last + 1):
                rest = total[(h - first) * HEAD : (h - first + 1) * HEAD]
                picked = jnp.where(lane >= h * n_keys, rest, picked)
            return picked

        qc = [a[cols] for a in qs]
        mc = [a[cols] for a in ms]
        s = nt(kcat, cat(right6(qc), 1)) + bt[:, cols]
        dp = nt(vcat, cat(right3(mc), 1))
        e = jnp.exp(s - jnp.max(s, axis=0, keepdims=True))
        p = e * (1.0 / jnp.sum(e, axis=0, keepdims=True))
        p1, p2 = split2(p)
        ot_ref[0, :, cols] = of_heads(vt1, vt2, p1, p2)
        ds = p * (dp - jnp.sum(p * dp, axis=0, keepdims=True))
        dbt[:, cols] = dbt[:, cols] + ds
        s1, s2 = split2(ds)
        dqt_ref[0, :, cols] = of_heads(kt1, kt2, s1, s2)
        both = nn(s1, cat(qc[:2], 1))
        dk = dk + both[:, :LANES] + both[:, LANES:] + nn(s2, qc[0])
        both = nn(p1, cat(mc, 1))
        dv = dv + both[:, :LANES] + both[:, LANES:] + nn(p2, mc[0])
    dk_ref[0] = dk
    dv_ref[0] = dv

    @pl.when(step == rows - 1)
    def _():
        stack[...] = dbt[...].T
        for z in range(res_n):
            zi = lax.bitwise_xor(res, z)
            for s in range(seq_n):
                ci = lax.bitwise_xor(chip, s // 2)
                d = z * seq_n + s
                at = [h * n_keys + d * rows for h in range(heads)]
                block = cat([stack[a : a + rows, :] for a in at], 0)

                @pl.when(core == s % 2)
                def _():
                    near_ref[ci, zi] = block

                @pl.when(core != s % 2)
                def _():
                    far_ref[ci, zi] = block


def pair_back_kernel(
    ot_ref, dqt_ref, dk_ref, dv_ref, dout_ref, sig_ref,
    g_ref, wb_ref, after1_ref, after2_ref, dn_ref,
):
    rows, length, feats = dk_ref.shape
    g = g_ref[...]
    w1, w2 = wb_ref[0], wb_ref[1]

    def lines(flat):
        heads = flat.shape[1] // length
        return cat([flat[:, h * length : (h + 1) * length] for h in range(heads)], 0).T

    for i in range(rows):
        o, sig = lines(ot_ref[i]), sig_ref[i]
        d_gate = dout_ref[i] * o * sig * (1.0 - sig)
        dq = lines(dqt_ref[i]) * (1.0 / math.sqrt(HEAD))
        t1, t2 = split2(cat([dq, dk_ref[i], dv_ref[i], d_gate], 1))
        dn_ref[i] = g * (nt(t1, w1) + nt(t1, w2) + nt(t2, w1))


def msa_project_kernel(
    y0_ref, y1_ref, y2_ref, y3_ref, adj_ref,
    g_ref, wq_ref, wk_ref, wv_ref, wg_ref, wo_ref,
    q_ref, m_ref, dout_ref, sig_ref, k_ref, v_ref, wkv_ref, wqg_ref,
    yall,
):
    res = lax.axis_index("res")
    n_seqs, own, feats = adj_ref.shape
    n_keys = yall.shape[1]
    g = g_ref[...]
    for t, ref in enumerate((y0_ref, y1_ref, y2_ref, y3_ref)):
        at = pl.multiple_of(lax.bitwise_xor(res, t) * own, own)
        for b in range(n_seqs):
            yall[b, pl.ds(at, own), :] = ref[b * own : (b + 1) * own, :]
    n_own, _ = normed(y0_ref[: n_seqs * own])
    n_all, _ = normed(yall[...].reshape(n_seqs * n_keys, feats))
    own_parts, all_parts = split3(n_own * g), split3(n_all * g)
    for ref, pair in ((wkv_ref, (wk_ref, wv_ref)), (wqg_ref, (wq_ref, wg_ref))):
        top, low = split2(cat([pair[0][...], pair[1][...]], 1))
        ref[0] = top
        ref[1] = low
    q = nn(cat(left6(own_parts), 1), cat(right6(split3(wq_ref[...])), 0))
    gate = nn(cat(left3(own_parts), 1), cat(right3(split2(wg_ref[...])), 0))
    k = nn(cat(left6(all_parts), 1), cat(right6(split3(wk_ref[...])), 0))
    v = nn(cat(left3(all_parts), 1), cat(right3(split2(wv_ref[...])), 0))
    adj = adj_ref[...].reshape(n_seqs * own, feats)
    d_out = nt(cat(left3(split2(adj)), 1), cat(right3(split2(wo_ref[...])), 1))
    sig = jax.nn.sigmoid(gate)
    q_ref[...] = q * (1.0 / math.sqrt(HEAD))
    m_ref[...] = d_out * sig
    dout_ref[...] = d_out
    sig_ref[...] = sig
    k_ref[...] = k
    v_ref[...] = v


def msa_kernel(
    dims,
    q_ref, m_ref, k_ref, v_ref,
    b0_ref, b1_ref, b2_ref, b3_ref,
    wkv_ref,
    o_ref, dq_ref, r0_ref, r1_ref, r23_ref, near_ref, far_ref,
    bias, dbias, dyall, natural,
):
    rows, heads, seq_n, res_n = dims
    seq, res = lax.axis_index("seq"), lax.axis_index("res")
    core, chip = lax.rem(seq, 2), lax.div(seq, 2)
    n_seqs, n_keys, feats = dyall.shape
    own = n_keys // res_n
    tiles, group = feats // LANES, LANES // HEAD
    blocks = (b0_ref, b1_ref, b2_ref, b3_ref)
    gather_chips(natural, blocks, core, chip)
    for s in range(seq_n):
        block = cat([natural[s, 0], natural[s, 1]], 0)
        for h in range(heads):
            at = h * own + s * rows
            bias[at : at + rows, :] = block[h * rows : (h + 1) * rows]
    masks = [head_mask(u, BF16) for u in range(group)]
    fmasks = [head_mask(u, F32) for u in range(group)]

    def stacked(a, by):
        return cat([a * mask for mask in by], 0)

    def own_rows(full):
        total = fmasks[0] * full[:own]
        for u in range(1, group):
            total = total + fmasks[u] * full[u * own : (u + 1) * own]
        return total

    b1, b2 = wkv_ref[0], wkv_ref[1]
    for b in range(n_seqs):
        near = slice(b * own, (b + 1) * own)
        wide = slice(b * n_keys, (b + 1) * n_keys)
        dkt, dvt = [], []
        for t in range(tiles):
            cols = slice(t * LANES, (t + 1) * LANES)
            lines = slice(t * group * own, (t + 1) * group * own)
            q_t, m_t = q_ref[near, cols], m_ref[near, cols]
            qs = [stacked(a, masks) for a in split3(q_t)]
            ms = [stacked(a, masks) for a in split2(m_t)]
            qt1, qt2 = split2(stacked(q_t, fmasks).T)
            mt1, mt2 = split2(stacked(m_t, fmasks).T)
            kp = split3(k_ref[wide, cols])
            vp = split2(v_ref[wide, cols])
            s = nt(cat(left6(qs), 1), cat(right6(kp), 1)) + bias[lines]
            dp = nt(cat(left3(ms), 1), cat(right3(vp), 1))
            e = jnp.exp(s - jnp.max(s, axis=1, keepdims=True))
            p = e * (1.0 / jnp.sum(e, axis=1, keepdims=True))
            p1, p2 = split2(p)
            both = nn(p1, cat(vp, 1))
            o_ref[near, cols] = own_rows(both[:, :LANES] + both[:, LANES:] + nn(p2, vp[0]))
            ds = p * (dp - jnp.sum(p * dp, axis=1, keepdims=True))
            dbias[lines] = ds if b == 0 else dbias[lines] + ds
            s1, s2 = split2(ds)
            both = nn(s1, cat(kp[:2], 1))
            dq_ref[near, cols] = own_rows(both[:, :LANES] + both[:, LANES:] + nn(s2, kp[0]))
            both = nn(cat([qt1, qt2], 0), s1)
            dkt.append(both[:LANES] + both[LANES:] + nn(qt1, s2))
            both = nn(cat([mt1, mt2], 0), p1)
            dvt.append(both[:LANES] + both[LANES:] + nn(mt1, p2))
        t1, t2 = split2(cat([a.T for a in dkt + dvt], 1))
        dyall[b] = nt(t1, b1) + nt(t1, b2) + nt(t2, b1)
    for t, (ref, base) in enumerate(((r0_ref, 0), (r1_ref, 0), (r23_ref, 0), (r23_ref, n_seqs))):
        at = pl.multiple_of(lax.bitwise_xor(res, t) * own, own)
        for b in range(n_seqs):
            to = (base + b) * own
            ref[to : to + own, :] = dyall[b, pl.ds(at, own), :]
    for s in range(seq_n):
        ci = lax.bitwise_xor(chip, s // 2)
        at = [h * own + s * rows for h in range(heads)]
        block = cat([dbias[a : a + rows, :] for a in at], 0)

        @pl.when(core == s % 2)
        def _():
            near_ref[ci] = block

        @pl.when(core != s % 2)
        def _():
            far_ref[ci] = block


def aligned_back_kernel(o_ref, dq_ref, dout_ref, sig_ref, wqg_ref, r0_ref, dy_ref):
    sig = sig_ref[...]
    d_gate = dout_ref[...] * o_ref[...] * sig * (1.0 - sig)
    t1, t2 = split2(cat([dq_ref[...] * (1.0 / math.sqrt(HEAD)), d_gate], 1))
    b1, b2 = wqg_ref[0], wqg_ref[1]
    dy_ref[...] = nt(t1, b1) + nt(t1, b2) + nt(t2, b1) + r0_ref[...]


def aligned_end_kernel(y_ref, g_ref, dy_ref, r23_ref, r1_ref, out_ref):
    n_seqs, own, _ = out_ref.shape
    g = g_ref[...]
    for b in range(n_seqs):
        at = slice(b * own, (b + 1) * own)
        n, scale = normed(y_ref[at])
        out_ref[b] = normed_back(n, scale, g * (dy_ref[at] + r23_ref[at] + r1_ref[at]))


def stack_kernel(length, lines, p0_ref, p1_ref, p2_ref, p3_ref, after_ref, out_ref):
    blocks = [ref[ref.shape[0] - lines :, :length] for ref in (p0_ref, p1_ref, p2_ref, p3_ref)]
    pack(lambda t: blocks[t], len(blocks), lines, out_ref)


def chip_stack_kernel(b1_ref, b2_ref, b3_ref, after_ref, out_ref):
    for t, ref in enumerate((b1_ref, b2_ref, b3_ref)):
        out_ref[t] = ref[...]


def core_sum_kernel(p0_ref, p1_ref, m0_ref, m1_ref, after_ref, s0_ref, s1_ref, s2_ref, s3_ref):
    res_n, lines = p0_ref.shape[1:3]
    for t, ref in enumerate((s0_ref, s1_ref, s2_ref, s3_ref)):
        pair = p0_ref[t] + p1_ref[t]
        msa = m0_ref[t] + m1_ref[t]
        blocks = [pair[z] for z in range(res_n)] + [msa[:lines], msa[lines:]]
        pack(lambda i: blocks[i], len(blocks), lines, ref)


def chip_sum_kernel(
    s0_ref, s1_ref, s2_ref, s3_ref, r1_ref, r23_ref, after_ref,
    c0_ref, joint_ref, c2_ref, c3_ref, m_ref,
):
    lines, length = c0_ref.shape
    base = r1_ref.shape[0]
    joint_ref[:base] = r1_ref[...] + r23_ref[base:]
    if length < joint_ref.shape[1]:
        joint_ref[base:, length:] = jnp.zeros((lines, joint_ref.shape[1] - length), F32)
    total = s0_ref[...] + s1_ref[...] + s2_ref[...] + s3_ref[...]
    blocks = unpack(total, 2 * total.shape[0] // (3 * lines), lines)
    for t, ref in enumerate((c0_ref, joint_ref, c2_ref, c3_ref)):
        if t == 1:
            ref[base:, :length] = blocks[t]
        else:
            ref[...] = blocks[t]
    m_ref[:lines] = blocks[-2]
    m_ref[lines:] = blocks[-1]


def pair_end_kernel(
    n_ref, scale_ref, dn_ref, p0_ref, p1_ref, p2_ref, p3_ref, m_ref, wj_ref, out_ref
):
    rows, length, feats = n_ref.shape
    lines = p0_ref.shape[0]
    pair = p0_ref[...] + p2_ref[...] + p3_ref[...]
    pair = pair + p1_ref[p1_ref.shape[0] - lines :, :length]
    msa = m_ref[...]
    pad = jnp.zeros((LANES - pair.shape[0] - msa.shape[0], length), F32)
    b = cat([pair, msa, pad], 0).T
    more = nn(cat(left3(split2(b)), 1), wj_ref[...])
    for j in range(rows):
        dn = dn_ref[j] + more[:, j * feats : (j + 1) * feats]
        out_ref[j] = normed_back(n_ref[j], scale_ref[j], dn)


MIB = 1 << 20


def params(mib, **more):
    return pltpu.CompilerParams(vmem_limit_bytes=mib * MIB, **more)


def vmem(count):
    return [pl.BlockSpec(memory_space=pltpu.VMEM)] * count


def swap(values, axis, size, offset):
    return lax.ppermute(values, axis, [(i, i ^ offset) for i in range(size)])


def fused_on_device(
    seq_n,
    res_n,
    coupled_embedding,
    aligned_embedding,
    coupled_change_adjoint,
    aligned_change_adjoint,
    coupled_scaler,
    coupled_asking_matrix,
    coupled_lookup_matrix,
    coupled_content_matrix,
    coupled_sigmoid_matrix,
    coupled_offset_matrix,
    coupled_result_matrix,
    aligned_scaler,
    coupled_scaler_for_offset,
    aligned_asking_matrix,
    aligned_lookup_matrix,
    aligned_content_matrix,
    aligned_sigmoid_matrix,
    aligned_offset_matrix,
    aligned_result_matrix,
):
    rows, length, feats = coupled_embedding.shape
    n_seqs, own, wide = aligned_embedding.shape
    hp, hm = HP, ALIGNED_SPLITS
    chips = seq_n // 2
    shape = lambda *s: jax.ShapeDtypeStruct(s, F32)
    wp_t, wm_t = coupled_offset_matrix.T, aligned_offset_matrix.T
    gain = coupled_scaler.reshape(1, feats)
    gain2 = coupled_scaler_for_offset.reshape(1, feats)

    lines, base = hp * rows, n_seqs * own
    after = [pl.BlockSpec(memory_space=pl.ANY)]
    packed = lambda count: (3 * count * lines // 2, LANES)
    spread = lambda count: pltpu.VMEM((seq_n, count, lines, length), F32)
    mixed_rows, msa_rows = pl.pallas_call(
        functools.partial(bias_kernel, rows),
        out_shape=(shape(base + lines, wide), shape(*packed(2))),
        scratch_shapes=[pltpu.VMEM((hm * rows, length), F32)],
        compiler_params=params(63),
        name="bias_rows",
    )(
        coupled_embedding, aligned_embedding.reshape(base, wide), gain, wp_t, gain2, wm_t
    )

    def over_chips(first, *behind):
        return pl.pallas_call(
            chip_stack_kernel,
            in_specs=vmem(3) + after * len(behind),
            out_shape=shape(chips - 1, *first.shape),
            compiler_params=params(16),
            name="stack_chips",
        )(*[swap(first, "seq", seq_n, 2 * t) for t in range(1, chips)], *behind)

    def over_cores(first, rest):
        return [first, rest, swap(first, "seq", seq_n, 1), swap(rest, "seq", seq_n, 1)]

    columns = [mixed_rows] + [swap(mixed_rows, "res", res_n, t) for t in range(1, res_n)]

    bf = lambda *s: jax.ShapeDtypeStruct(s, BF16)
    q, k, v, m, kt, vt, d_out, sig, n, scale, wj, wb = pl.pallas_call(
        pair_project_kernel,
        out_shape=(
            bf(rows, length, 3 * feats), bf(rows, length, 3 * feats),
            bf(rows, length, 2 * feats), bf(rows, length, 2 * feats),
            bf(rows, 2 * feats, length), bf(rows, 2 * feats, length),
        ) + (shape(rows, length, feats),) * 4
        + (bf(3 * LANES, rows * feats), bf(2, feats, 4 * feats)),
        compiler_params=params(32),
        name="pair_project",
        cost_estimate=pl.CostEstimate(flops=2 * 10**9, bytes_accessed=10**7, transcendentals=0),
    )(
        coupled_embedding, coupled_change_adjoint, gain, coupled_asking_matrix,
        coupled_lookup_matrix, coupled_content_matrix, coupled_sigmoid_matrix,
        coupled_result_matrix, wp_t, gain2, wm_t,
    )

    msa_rest = over_chips(msa_rows, n)
    msa_blocks = over_cores(msa_rows, msa_rest)
    joint = packed(res_n + 2)
    first = pl.pallas_call(
        functools.partial(stack_kernel, length, lines),
        in_specs=vmem(4) + after,
        out_shape=shape(*packed(res_n)),
        compiler_params=params(16),
        name="stack_rows",
    )(*columns, msa_rest)

    wide_gain = aligned_scaler.reshape(1, wide)
    flat = lambda count: shape(n_seqs * count, wide)
    mq, mm, m_out, m_sig, mk, mv, wkv, wqg = pl.pallas_call(
        msa_project_kernel,
        out_shape=(flat(own),) * 4 + (flat(length),) * 2 + (bf(2, wide, 2 * wide),) * 2,
        scratch_shapes=[pltpu.VMEM((n_seqs, length, wide), F32)],
        compiler_params=params(32),
        name="msa_project",
        cost_estimate=pl.CostEstimate(flops=10**9, bytes_accessed=10**7, transcendentals=0),
    )(
        *columns, aligned_change_adjoint, wide_gain, aligned_asking_matrix,
        aligned_lookup_matrix, aligned_content_matrix, aligned_sigmoid_matrix,
        aligned_result_matrix,
    )

    stretch = pltpu.VMEM((hm * own, length), F32)
    o, dq, kept, r1, r23, msa_near, msa_far = pl.pallas_call(
        functools.partial(msa_kernel, (rows, hm, seq_n, res_n)),
        out_shape=(flat(own),) * 4 + (shape(2 * base, wide),)
        + (shape(chips, hm * rows, length),) * 2,
        scratch_shapes=[
            stretch, stretch, pltpu.VMEM((n_seqs, length, wide), F32),
            spread(hm // hp),
        ],
        compiler_params=params(32),
        name="msa_attention",
        cost_estimate=pl.CostEstimate(flops=4 * 10**9, bytes_accessed=10**7, transcendentals=0),
    )(
        mq, mm, mk, mv, *msa_blocks, wkv,
    )
    far_msa = swap(msa_far, "seq", seq_n, 1)
    r23 = swap(r23, "res", res_n, 2)

    blocks = over_cores(first, over_chips(first, kept))

    piece = lambda *s: pl.BlockSpec((1,) + s, lambda i: (i, 0, 0))
    whole = lambda *s: pl.BlockSpec(s, lambda i: (0,) * len(s))
    quarter = (chips, res_n, lines, length)
    ot, dqt, dk, dv, near, far = pl.pallas_call(
        functools.partial(pair_kernel, (rows, hp, seq_n, res_n)),
        grid=(rows,),
        in_specs=[
            piece(length, 3 * feats), piece(length, 3 * feats),
            piece(length, 2 * feats), piece(length, 2 * feats),
            piece(2 * feats, length), piece(2 * feats, length),
        ] + [whole(*packed(res_n)), whole(chips - 1, *packed(res_n))] * 2 + after,
        out_specs=(
            piece(HEAD, hp * length), piece(HEAD, hp * length),
            piece(length, feats), piece(length, feats), whole(*quarter), whole(*quarter),
        ),
        out_shape=(
            shape(rows, HEAD, hp * length), shape(rows, HEAD, hp * length),
            shape(rows, length, feats), shape(rows, length, feats),
            shape(*quarter), shape(*quarter),
        ),
        scratch_shapes=[
            pltpu.VMEM((length, hp * length), F32),
            pltpu.VMEM((length, hp * length), F32),
            pltpu.VMEM((hp * length, length), F32),
            spread(res_n),
        ],
        compiler_params=params(32),
        name="pair_attention",
        cost_estimate=pl.CostEstimate(flops=10**10, bytes_accessed=10**7, transcendentals=0),
    )(q, k, v, m, kt, vt, *blocks, kept)
    far_pair = swap(far, "seq", seq_n, 1)
    dn = pl.pallas_call(
        pair_back_kernel,
        in_specs=vmem(8) + after * 2,
        out_shape=shape(rows, length, feats),
        compiler_params=params(32),
        name="pair_back",
        cost_estimate=pl.CostEstimate(flops=10**11, bytes_accessed=10**8, transcendentals=0),
    )(
        ot, dqt, dk, dv, d_out, sig, gain, wb, r23, far_msa,
    )
    sums = pl.pallas_call(
        core_sum_kernel,
        in_specs=vmem(4) + after,
        out_shape=(shape(*joint),) * chips,
        compiler_params=params(16),
        name="core_sum",
    )(near, far_pair, msa_near, far_msa, dn)
    dy = pl.pallas_call(
        aligned_back_kernel,
        out_shape=flat(own),
        compiler_params=params(16),
        name="aligned_back",
        cost_estimate=pl.CostEstimate(flops=10**9, bytes_accessed=10**6, transcendentals=0),
    )(o, dq, m_out, m_sig, wqg, kept)
    c0, mixed_sum, c2, c3, msa_sum = pl.pallas_call(
        chip_sum_kernel,
        in_specs=vmem(6) + after,
        out_shape=(
            shape(lines, length), shape(base + lines, wide), shape(lines, length),
            shape(lines, length), shape(hm * rows, length),
        ),
        compiler_params=params(16),
        name="chip_sum",
    )(sums[0], *[swap(sums[t], "seq", seq_n, 2 * t) for t in range(1, chips)], r1, r23, dy)
    mixed_sum, c2, c3 = [swap(a, "res", res_n, t) for a, t in ((mixed_sum, 1), (c2, 2), (c3, 3))]

    aligned_out = pl.pallas_call(
        aligned_end_kernel,
        out_shape=shape(n_seqs, own, wide),
        compiler_params=params(16),
        name="aligned_end",
    )(mixed_rows, wide_gain, dy, r23, mixed_sum)
    coupled_out = pl.pallas_call(
        pair_end_kernel,
        out_shape=shape(rows, length, feats),
        compiler_params=params(16),
        name="pair_end",
    )(n, scale, dn, c0, mixed_sum, c2, c3, msa_sum, wj)
    return coupled_out, aligned_out


def on_device(seq_n, res_n, *arrays):
    length = arrays[0].shape[1]
    rows = arrays[0].shape[0]
    narrow = length <= arrays[1].shape[2] and HP * length % TILE == 0
    narrow = narrow and rows * (HP + ALIGNED_SPLITS) <= LANES
    narrow = narrow and ALIGNED_SPLITS == 2 * HP and 2 * (length - LANES) == LANES
    if narrow and seq_n == 8 and res_n == 4:
        return fused_on_device(seq_n, res_n, *arrays)
    return scanned_on_device(*arrays)


def solution(mesh):
    in_specs = (
        P(("res", "seq"), None, None),
        P("seq", "res", None),
        P(("res", "seq"), None, None),
        P("seq", "res", None),
        P(),
        P(),
        P(),
        P(),
        P(),
        P(),
        P(),
        P(),
        P(),
        P(),
        P(),
        P(),
        P(),
        P(),
        P(),
    )
    out_specs = (P(("res", "seq"), None, None), P("seq", "res", None))
    return jax.shard_map(
        functools.partial(on_device, mesh.shape["seq"], mesh.shape["res"]),
        mesh=mesh, in_specs=in_specs, out_specs=out_specs, check_vma=False
    )
```

```python
import functools
import math

import jax
import jax.numpy as jnp
from jax import lax
from jax.experimental import pallas as pl
from jax.experimental.pallas import tpu as pltpu
from jax.sharding import PartitionSpec as P

HP = 4
ALIGNED_SPLITS = 8


EXACT_MATMUL = lax.Precision.HIGHEST
EPSILON = 1e-05


def standardize_features(values, norm_gain):
    center = values - jnp.mean(values, axis=-1, keepdims=True)
    spread = jnp.mean(center * center, axis=-1, keepdims=True)
    return center * lax.rsqrt(spread + EPSILON) * norm_gain


def affine_map(values, weight):
    return jnp.einsum("...c,ce->...e", values, weight, precision=EXACT_MATMUL)


def sigmoid_mixing(query_vectors, key_rows, value_rows, gate_preact, softmax_offset, head_count):
    query_shape = query_vectors.shape
    head_width = query_shape[-1] // head_count
    query_heads = query_vectors.reshape(query_shape[:-1] + (head_count, head_width))
    key_heads = key_rows.reshape(key_rows.shape[:-1] + (head_count, head_width))
    value_heads = value_rows.reshape(value_rows.shape[:-1] + (head_count, head_width))
    logits = (
        jnp.einsum("...qhd,...khd->...qhk", query_heads, key_heads, precision=EXACT_MATMUL)
        / math.sqrt(head_width)
        + softmax_offset
    )
    largest = lax.stop_gradient(jnp.max(logits, axis=-1, keepdims=True))
    weights = jnp.exp(logits - largest)
    weights = weights / jnp.sum(weights, axis=-1, keepdims=True)
    mixed_contents = jnp.einsum(
        "...qhk,...khd->...qhd", weights, value_heads, precision=EXACT_MATMUL
    )
    return mixed_contents.reshape(query_shape) * jax.nn.sigmoid(gate_preact)


def scanned_on_device(
    coupled_embedding,
    aligned_embedding,
    coupled_change_adjoint,
    aligned_change_adjoint,
    coupled_scaler,
    coupled_asking_matrix,
    coupled_lookup_matrix,
    coupled_content_matrix,
    coupled_sigmoid_matrix,
    coupled_offset_matrix,
    coupled_result_matrix,
    aligned_scaler,
    coupled_scaler_for_offset,
    aligned_asking_matrix,
    aligned_lookup_matrix,
    aligned_content_matrix,
    aligned_sigmoid_matrix,
    aligned_offset_matrix,
    aligned_result_matrix,
):

    def pair_local(entering_lines):
        standardized_source = standardize_features(entering_lines, coupled_scaler)
        return (
            affine_map(standardized_source, coupled_asking_matrix),
            affine_map(standardized_source, coupled_lookup_matrix),
            affine_map(standardized_source, coupled_content_matrix),
            affine_map(standardized_source, coupled_sigmoid_matrix),
            jnp.einsum(
                "jkc,ch->jhk", standardized_source, coupled_offset_matrix, precision=EXACT_MATMUL
            ),
        )

    (row_queries, row_keys, row_values, row_gates, bias_rows), pair_back = jax.vjp(
        pair_local, coupled_embedding
    )
    by_seq = lax.all_gather(bias_rows, "seq", axis=0, tiled=True)
    full_bias = lax.all_gather(by_seq, "res", axis=0, tiled=True)

    def row_output(one_query, one_key, one_value, one_gate, softmax_offset):
        return affine_map(
            sigmoid_mixing(one_query, one_key, one_value, one_gate, softmax_offset, HP),
            coupled_result_matrix,
        )

    def row_step(bias_sum, row_items):
        one_query, one_key, one_value, one_gate, one_cotan = row_items
        discarded_entry, row_back = jax.vjp(
            row_output, one_query, one_key, one_value, one_gate, full_bias
        )
        grad_query, grad_key, grad_value, grad_gate, grad_bias = row_back(one_cotan)
        return (bias_sum + grad_bias, (grad_query, grad_key, grad_value, grad_gate))

    bias_total, row_grads = lax.scan(
        row_step,
        jnp.zeros_like(full_bias),
        (row_queries, row_keys, row_values, row_gates, coupled_change_adjoint),
    )
    by_res = lax.psum_scatter(bias_total, "res", scatter_dimension=0, tiled=True)
    bias_grad_rows = lax.psum_scatter(by_res, "seq", scatter_dimension=0, tiled=True)
    (mixed_result_sensitivity,) = pair_back(row_grads + (bias_grad_rows,))

    def aligned_offset_portion(entering_lines):
        return jnp.einsum(
            "gys,sj->gjy",
            standardize_features(entering_lines, coupled_scaler_for_offset),
            aligned_offset_matrix,
            precision=EXACT_MATMUL,
        )

    aligned_offset_part, aligned_offset_reverse = jax.vjp(aligned_offset_portion, coupled_embedding)
    tile_softmax_offset = lax.all_gather(aligned_offset_part, "seq", axis=0, tiled=True)

    def sequence_output(query_vectors, full_key_rows, full_value_rows, gate_preact, softmax_offset):
        return affine_map(
            sigmoid_mixing(
                query_vectors,
                full_key_rows,
                full_value_rows,
                gate_preact,
                softmax_offset,
                ALIGNED_SPLITS,
            ),
            aligned_result_matrix,
        )

    state_all = lax.all_gather(aligned_embedding, "res", axis=1, tiled=True)

    def near_local(carry_pile):
        standardized_source = standardize_features(carry_pile, aligned_scaler)
        return (
            affine_map(standardized_source, aligned_asking_matrix),
            affine_map(standardized_source, aligned_sigmoid_matrix),
        )

    def keys_local(carry_pile):
        standardized_source = standardize_features(carry_pile, aligned_scaler)
        return (
            affine_map(standardized_source, aligned_lookup_matrix),
            affine_map(standardized_source, aligned_content_matrix),
        )

    (aligned_asking_lines, aligned_sigmoid_factors), near_back = jax.vjp(
        near_local, aligned_embedding
    )
    (full_key_rows, full_value_rows), keys_back = jax.vjp(keys_local, state_all)
    discarded_entry, sigmoid_mixing_reverse = jax.vjp(
        sequence_output,
        aligned_asking_lines,
        full_key_rows,
        full_value_rows,
        aligned_sigmoid_factors,
        tile_softmax_offset,
    )
    query_gradient, full_key_gradient, full_value_gradient, gate_gradient, block_bias_gradient = (
        sigmoid_mixing_reverse(aligned_change_adjoint)
    )
    (state_term,) = keys_back((full_key_gradient, full_value_gradient))
    spread_grad = lax.psum_scatter(state_term, "res", scatter_dimension=1, tiled=True)
    (near_grad,) = near_back((query_gradient, gate_gradient))
    aligned_embedding_sensitivity = near_grad + spread_grad
    offset_line_sensitivity = lax.psum_scatter(
        block_bias_gradient, "seq", scatter_dimension=0, tiled=True
    )
    (coupled_sensitivity_via_offset,) = aligned_offset_reverse(offset_line_sensitivity)
    return (
        mixed_result_sensitivity + coupled_sensitivity_via_offset,
        aligned_embedding_sensitivity,
    )


F32 = jnp.float32
BF16 = jnp.bfloat16
HEAD = 32
LANES = 128
TILE = 256


def split2(a):
    top = a.astype(BF16)
    return top, (a - top.astype(F32)).astype(BF16)


def split3(a):
    top = a.astype(BF16)
    rest = a - top.astype(F32)
    mid = rest.astype(BF16)
    return top, mid, (rest - mid.astype(F32)).astype(BF16)


def left6(parts):
    a, b, c = parts
    return [a, a, b, b, a, c]


def right6(parts):
    a, b, c = parts
    return [a, b, a, b, c, a]


def left3(parts):
    return [parts[0], parts[0], parts[1]]


def right3(parts):
    return [parts[0], parts[1], parts[0]]


def nn(a, b):
    return lax.dot_general(a, b, (((1,), (0,)), ((), ())), preferred_element_type=F32)


def nt(a, b):
    return lax.dot_general(a, b, (((1,), (1,)), ((), ())), preferred_element_type=F32)


def cat(parts, axis):
    return jnp.concatenate(parts, axis=axis)


def normed(v):
    center = v - jnp.mean(v, axis=-1, keepdims=True)
    spread = jnp.mean(center * center, axis=-1, keepdims=True)
    scale = lax.rsqrt(spread + EPSILON)
    return center * scale, scale


def normed_back(n, scale, dn):
    return scale * (
        dn - jnp.mean(dn, axis=-1, keepdims=True) - n * jnp.mean(dn * n, axis=-1, keepdims=True)
    )


def head_mask(h, dtype):
    lane = lax.broadcasted_iota(jnp.int32, (1, LANES), 1)
    return jnp.where((lane // HEAD) == h, 1.0, 0.0).astype(dtype)


def pack(block_of, count, lines, out_ref):
    half = count // 2
    for t in range(half):
        first, second = block_of(t), block_of(t + half)
        out_ref[t * lines : (t + 1) * lines] = first[:, :LANES]
        out_ref[(t + half) * lines : (t + half + 1) * lines] = second[:, :LANES]
        rest = cat([first[:, LANES:], second[:, LANES:]], 1)
        out_ref[(t + count) * lines : (t + count + 1) * lines] = rest


def unpack(dense, count, lines):
    half = count // 2
    blocks = []
    for t in range(count):
        rest = dense[(count + t % half) * lines : (count + t % half + 1) * lines]
        rest = rest[:, : LANES // 2] if t < half else rest[:, LANES // 2 :]
        blocks.append(cat([dense[t * lines : (t + 1) * lines], rest], 1))
    return blocks


def bias_kernel(rows, x_ref, y_ref, g_ref, wp_ref, g2_ref, wm_ref, joint_ref, packed_ref, bm_ref):
    length = x_ref.shape[1]
    base, wide = y_ref.shape
    joint_ref[:base] = y_ref[...]
    if length < wide:
        joint_ref[base:, length:] = jnp.zeros((wp_ref.shape[0] * rows, wide - length), F32)
    hp, hm = wp_ref.shape[0], wm_ref.shape[0]
    w = cat([wp_ref[...] * g_ref[...], wm_ref[...] * g2_ref[...]], 0)
    wcat = cat(left6(split3(w)), 1)
    for j in range(rows):
        n, _ = normed(x_ref[j])
        res = nt(wcat, cat(right6(split3(n)), 1))
        for h in range(hp):
            at = base + h * rows + j
            joint_ref[at : at + 1, :length] = res[h : h + 1]
        for h in range(hm):
            bm_ref[h * rows + j : h * rows + j + 1, :] = res[hp + h : hp + h + 1]
    lines = hp * rows
    pack(lambda t: bm_ref[t * lines : (t + 1) * lines], hm // hp, lines, packed_ref)


def pair_project_kernel(
    x_ref, adj_ref, g_ref, wq_ref, wk_ref, wv_ref, wg_ref, wo_ref, wp_ref, g2_ref, wm_ref,
    q_ref, k_ref, v_ref, m_ref, kt_ref, vt_ref, dout_ref, sig_ref, n_ref, scale_ref, wj_ref, wb_ref,
):
    rows, length, feats = x_ref.shape
    g = g_ref[...]
    top, low = split2(cat([wq_ref[...], wk_ref[...], wv_ref[...], wg_ref[...]], 1))
    wb_ref[0] = top
    wb_ref[1] = low
    w6 = cat(right6(split3(cat([wq_ref[...], wk_ref[...]], 1))), 0)
    w3 = cat(right3(split2(cat([wv_ref[...], wg_ref[...]], 1))), 0)
    wo3 = cat(right3(split2(wo_ref[...])), 1)
    for i in range(rows):
        n, scale = normed(x_ref[i])
        n_ref[i] = n
        scale_ref[i] = jnp.broadcast_to(scale, n.shape)
        parts = split3(n * g)
        qk = nn(cat(left6(parts), 1), w6)
        vg = nn(cat(left3(parts), 1), w3)
        d_out = nt(cat(left3(split2(adj_ref[i])), 1), wo3)
        sig = jax.nn.sigmoid(vg[:, feats:])
        dout_ref[i] = d_out
        sig_ref[i] = sig
        q, k, v = qk[:, :feats] * (1.0 / math.sqrt(HEAD)), qk[:, feats:], vg[:, :feats]
        q_ref[i] = cat(split3(q), 1)
        k_ref[i] = cat(split3(k), 1)
        v_ref[i] = cat(split2(v), 1)
        m_ref[i] = cat(split2(d_out * sig), 1)
        kt_ref[i] = cat(split2(k.T), 0)
        vt_ref[i] = cat(split2(v.T), 0)
    hp, hm = wp_ref.shape[0], wm_ref.shape[0]
    w = cat([wp_ref[...] * g, wm_ref[...] * g2_ref[...]], 0)
    lines = [jnp.broadcast_to(w[h : h + 1], (rows, feats)) for h in range(hp + hm)]
    lines += [jnp.zeros((LANES - rows * (hp + hm), feats), F32)]
    spread = cat(lines, 0)
    at = lax.broadcasted_iota(jnp.int32, (LANES, 1), 0)
    for j in range(rows):
        mine = jnp.where(lax.rem(at, rows) == j, spread, 0.0)
        wj_ref[:, j * feats : (j + 1) * feats] = cat(right3(split2(mine)), 0)


def gather_chips(natural, refs, core, chip):
    _, count, lines, _ = natural.shape
    for (own_ref, others_ref), side in zip((refs[:2], refs[2:]), (core, 1 - core)):
        for t in range(others_ref.shape[0] + 1):
            at = lax.bitwise_xor(chip, t) * 2 + side
            dense = others_ref[t - 1] if t > 0 else own_ref[...]
            for i, block in enumerate(unpack(dense, count, lines)):
                natural[at, i] = block


def pair_kernel(
    dims,
    q_ref, k_ref, v_ref, m_ref, kt_ref, vt_ref,
    b0_ref, b1_ref, b2_ref, b3_ref,
    after_ref,
    ot_ref, dqt_ref, dk_ref, dv_ref, near_ref, far_ref,
    bt, dbt, stack, natural,
):
    rows, heads, seq_n, res_n = dims
    step = pl.program_id(0)
    seq, res = lax.axis_index("seq"), lax.axis_index("res")
    core, chip = lax.rem(seq, 2), lax.div(seq, 2)
    n_keys = q_ref.shape[1]

    @pl.when(step == 0)
    def _():
        blocks = (b0_ref, b1_ref, b2_ref, b3_ref)
        gather_chips(natural, blocks, core, chip)
        for z in range(res_n):
            zi = lax.bitwise_xor(res, z)
            for s in range(seq_n):
                block = natural[s, zi]
                d = z * seq_n + s
                for h in range(heads):
                    at = h * n_keys + d * rows
                    stack[at : at + rows, :] = block[h * rows : (h + 1) * rows]
        bt[...] = stack[...].T
        dbt[...] = jnp.zeros_like(dbt)

    def pieces(ref, u, count):
        return [ref[u, :, t * LANES : (t + 1) * LANES] for t in range(count)]

    masks = [head_mask(h, BF16) for h in range(heads)]
    tiles = heads * n_keys // TILE
    batch = q_ref.shape[0]

    def operands(u):
        qs = [cat([a * mask for mask in masks], 0) for a in pieces(q_ref, u, 3)]
        ms = [cat([a * mask for mask in masks], 0) for a in pieces(m_ref, u, 2)]
        kcat = cat(left6(pieces(k_ref, u, 3)), 1)
        vcat = cat(left3(pieces(v_ref, u, 2)), 1)
        return qs, ms, kcat, vcat

    rows_in = {}

    def logits(item):
        u, c = divmod(item, tiles)
        if u not in rows_in:
            rows_in[u] = operands(u)
        qs, ms, kcat, vcat = rows_in[u]
        cols = slice(c * TILE, (c + 1) * TILE)
        qc, mc = [a[cols] for a in qs], [a[cols] for a in ms]
        s = nt(kcat, cat(right6(qc), 1)) + bt[:, cols]
        return s, nt(vcat, cat(right3(mc), 1)), qc, mc

    def weights(item, s, dp):
        c = item % tiles
        cols = slice(c * TILE, (c + 1) * TILE)
        e = jnp.exp(s - jnp.max(s, axis=0, keepdims=True))
        p = e * (1.0 / jnp.sum(e, axis=0, keepdims=True))
        ds = p * (dp - jnp.sum(p * dp, axis=0, keepdims=True))
        dbt[:, cols] = dbt[:, cols] + ds
        return split2(p) + split2(ds)

    sums = {}

    def products(item, p1, p2, s1, s2, qc, mc):
        u, c = divmod(item, tiles)
        cols = slice(c * TILE, (c + 1) * TILE)
        first, last = c * TILE // n_keys, ((c + 1) * TILE - 1) // n_keys
        lane = lax.broadcasted_iota(jnp.int32, (1, TILE), 1) + c * TILE

        def of_heads(ref, a1, a2):
            top = ref[u, first * HEAD : (last + 1) * HEAD]
            low = ref[u, LANES + first * HEAD : LANES + (last + 1) * HEAD]
            both = nn(cat([top, low], 0), a1)
            half = both.shape[0] // 2
            total = both[:half] + both[half:] + nn(top, a2)
            picked = total[:HEAD]
            for h in range(first + 1, last + 1):
                rest = total[(h - first) * HEAD : (h - first + 1) * HEAD]
                picked = jnp.where(lane >= h * n_keys, rest, picked)
            return picked

        ot_ref[u, :, cols] = of_heads(vt_ref, p1, p2)
        dqt_ref[u, :, cols] = of_heads(kt_ref, s1, s2)
        both = nn(s1, cat(qc[:2], 1))
        dk = both[:, :LANES] + both[:, LANES:] + nn(s2, qc[0])
        both = nn(p1, cat(mc, 1))
        dv = both[:, :LANES] + both[:, LANES:] + nn(p2, mc[0])
        if c > 0:
            dk, dv = sums[u][0] + dk, sums[u][1] + dv
        sums[u] = (dk, dv)
        if c == tiles - 1:
            dk_ref[u] = dk
            dv_ref[u] = dv

    count = batch * tiles
    ready, waiting = {}, {}
    for item in range(-1, count + 1):
        if 0 <= item + 1 < count:
            ready[item + 1] = logits(item + 1)
        if 0 <= item < count:
            s, dp, qc, mc = ready.pop(item)
            waiting[item] = weights(item, s, dp) + (qc, mc)
        if 0 <= item - 1 < count:
            products(item - 1, *waiting.pop(item - 1))

    @pl.when(step == pl.num_programs(0) - 1)
    def _():
        stack[...] = dbt[...].T
        for z in range(res_n):
            zi = lax.bitwise_xor(res, z)
            for s in range(seq_n):
                ci = lax.bitwise_xor(chip, s // 2)
                d = z * seq_n + s
                at = [h * n_keys + d * rows for h in range(heads)]
                block = cat([stack[a : a + rows, :] for a in at], 0)

                @pl.when(core == s % 2)
                def _():
                    near_ref[ci, zi] = block

                @pl.when(core != s % 2)
                def _():
                    far_ref[ci, zi] = block


def pair_back_kernel(
    ot_ref, dqt_ref, dk_ref, dv_ref, dout_ref, sig_ref,
    g_ref, wb_ref, dn_ref,
):
    rows, length, feats = dk_ref.shape
    g = g_ref[...]
    w1, w2 = wb_ref[0], wb_ref[1]

    def lines(flat):
        heads = flat.shape[1] // length
        return cat([flat[:, h * length : (h + 1) * length] for h in range(heads)], 0).T

    for i in range(rows):
        o, sig = lines(ot_ref[i]), sig_ref[i]
        d_gate = dout_ref[i] * o * sig * (1.0 - sig)
        dq = lines(dqt_ref[i]) * (1.0 / math.sqrt(HEAD))
        t1, t2 = split2(cat([dq, dk_ref[i], dv_ref[i], d_gate], 1))
        dn_ref[i] = g * (nt(t1, w1) + nt(t1, w2) + nt(t2, w1))


def msa_project_kernel(
    y0_ref, y1_ref, y2_ref, y3_ref, adj_ref,
    g_ref, wq_ref, wk_ref, wv_ref, wg_ref, wo_ref,
    q_ref, m_ref, dout_ref, sig_ref, k_ref, v_ref, wkv_ref, wqg_ref,
    yall,
):
    res = lax.axis_index("res")
    n_seqs, own, feats = adj_ref.shape
    n_keys = yall.shape[1]
    g = g_ref[...]
    for t, ref in enumerate((y0_ref, y1_ref, y2_ref, y3_ref)):
        at = pl.multiple_of(lax.bitwise_xor(res, t) * own, own)
        for b in range(n_seqs):
            yall[b, pl.ds(at, own), :] = ref[b * own : (b + 1) * own, :]
    n_own, _ = normed(y0_ref[: n_seqs * own])
    n_all, _ = normed(yall[...].reshape(n_seqs * n_keys, feats))
    own_parts, all_parts = split3(n_own * g), split3(n_all * g)
    for ref, pair in ((wkv_ref, (wk_ref, wv_ref)), (wqg_ref, (wq_ref, wg_ref))):
        top, low = split2(cat([pair[0][...], pair[1][...]], 1))
        ref[0] = top
        ref[1] = low
    q = nn(cat(left6(own_parts), 1), cat(right6(split3(wq_ref[...])), 0))
    gate = nn(cat(left3(own_parts), 1), cat(right3(split2(wg_ref[...])), 0))
    k = nn(cat(left6(all_parts), 1), cat(right6(split3(wk_ref[...])), 0))
    v = nn(cat(left3(all_parts), 1), cat(right3(split2(wv_ref[...])), 0))
    adj = adj_ref[...].reshape(n_seqs * own, feats)
    d_out = nt(cat(left3(split2(adj)), 1), cat(right3(split2(wo_ref[...])), 1))
    sig = jax.nn.sigmoid(gate)
    q_ref[...] = q * (1.0 / math.sqrt(HEAD))
    m_ref[...] = d_out * sig
    dout_ref[...] = d_out
    sig_ref[...] = sig
    k_ref[...] = k
    v_ref[...] = v


def msa_kernel(
    dims,
    q_ref, m_ref, k_ref, v_ref,
    b0_ref, b1_ref, b2_ref, b3_ref,
    wkv_ref,
    o_ref, dq_ref, r0_ref, r1_ref, r23_ref, near_ref, far_ref,
    bias, dbias, dyall, natural,
):
    rows, heads, seq_n, res_n = dims
    seq, res = lax.axis_index("seq"), lax.axis_index("res")
    core, chip = lax.rem(seq, 2), lax.div(seq, 2)
    n_seqs, n_keys, feats = dyall.shape
    own = n_keys // res_n
    tiles, group = feats // LANES, LANES // HEAD
    blocks = (b0_ref, b1_ref, b2_ref, b3_ref)
    gather_chips(natural, blocks, core, chip)
    for s in range(seq_n):
        block = cat([natural[s, 0], natural[s, 1]], 0)
        for h in range(heads):
            at = h * own + s * rows
            bias[at : at + rows, :] = block[h * rows : (h + 1) * rows]
    masks = [head_mask(u, BF16) for u in range(group)]
    fmasks = [head_mask(u, F32) for u in range(group)]

    def stacked(a, by):
        return cat([a * mask for mask in by], 0)

    def own_rows(full):
        total = fmasks[0] * full[:own]
        for u in range(1, group):
            total = total + fmasks[u] * full[u * own : (u + 1) * own]
        return total

    b1, b2 = wkv_ref[0], wkv_ref[1]

    def spans(item):
        b, t = divmod(item, tiles)
        near = slice(b * own, (b + 1) * own)
        wide = slice(b * n_keys, (b + 1) * n_keys)
        cols = slice(t * LANES, (t + 1) * LANES)
        return b, near, wide, cols, slice(t * group * own, (t + 1) * group * own)

    def logits(item):
        b, near, wide, cols, lines = spans(item)
        qs = [stacked(a, masks) for a in split3(q_ref[near, cols])]
        ms = [stacked(a, masks) for a in split2(m_ref[near, cols])]
        kp = split3(k_ref[wide, cols])
        vp = split2(v_ref[wide, cols])
        s = nt(cat(left6(qs), 1), cat(right6(kp), 1)) + bias[lines]
        return s, nt(cat(left3(ms), 1), cat(right3(vp), 1)), kp, vp

    def weights(item, s, dp):
        b, near, wide, cols, lines = spans(item)
        e = jnp.exp(s - jnp.max(s, axis=1, keepdims=True))
        p = e * (1.0 / jnp.sum(e, axis=1, keepdims=True))
        ds = p * (dp - jnp.sum(p * dp, axis=1, keepdims=True))
        dbias[lines] = ds if b == 0 else dbias[lines] + ds
        return split2(p) + split2(ds)

    turned = {}

    def products(item, p1, p2, s1, s2, kp, vp):
        b, near, wide, cols, lines = spans(item)
        qt1, qt2 = split2(stacked(q_ref[near, cols], fmasks).T)
        mt1, mt2 = split2(stacked(m_ref[near, cols], fmasks).T)
        both = nn(p1, cat(vp, 1))
        o_ref[near, cols] = own_rows(both[:, :LANES] + both[:, LANES:] + nn(p2, vp[0]))
        both = nn(s1, cat(kp[:2], 1))
        dq_ref[near, cols] = own_rows(both[:, :LANES] + both[:, LANES:] + nn(s2, kp[0]))
        both = nn(cat([qt1, qt2], 0), s1)
        dkt = both[:LANES] + both[LANES:] + nn(qt1, s2)
        both = nn(cat([mt1, mt2], 0), p1)
        dvt = both[:LANES] + both[LANES:] + nn(mt1, p2)
        turned.setdefault(b, []).append((dkt, dvt))
        if len(turned[b]) == tiles:
            flat = [a[0].T for a in turned[b]] + [a[1].T for a in turned[b]]
            t1, t2 = split2(cat(flat, 1))
            dyall[b] = nt(t1, b1) + nt(t1, b2) + nt(t2, b1)

    count = n_seqs * tiles
    ready, waiting = {}, {}
    for item in range(-1, count + 1):
        if 0 <= item + 1 < count:
            ready[item + 1] = logits(item + 1)
        if 0 <= item < count:
            s, dp, kp, vp = ready.pop(item)
            waiting[item] = weights(item, s, dp) + (kp, vp)
        if 0 <= item - 1 < count:
            products(item - 1, *waiting.pop(item - 1))
    for t, (ref, base) in enumerate(((r0_ref, 0), (r1_ref, 0), (r23_ref, 0), (r23_ref, n_seqs))):
        at = pl.multiple_of(lax.bitwise_xor(res, t) * own, own)
        for b in range(n_seqs):
            to = (base + b) * own
            ref[to : to + own, :] = dyall[b, pl.ds(at, own), :]
    for s in range(seq_n):
        ci = lax.bitwise_xor(chip, s // 2)
        at = [h * own + s * rows for h in range(heads)]
        block = cat([dbias[a : a + rows, :] for a in at], 0)

        @pl.when(core == s % 2)
        def _():
            near_ref[ci] = block

        @pl.when(core != s % 2)
        def _():
            far_ref[ci] = block


def aligned_back_kernel(o_ref, dq_ref, dout_ref, sig_ref, wqg_ref, r0_ref, dy_ref):
    sig = sig_ref[...]
    d_gate = dout_ref[...] * o_ref[...] * sig * (1.0 - sig)
    t1, t2 = split2(cat([dq_ref[...] * (1.0 / math.sqrt(HEAD)), d_gate], 1))
    b1, b2 = wqg_ref[0], wqg_ref[1]
    dy_ref[...] = nt(t1, b1) + nt(t1, b2) + nt(t2, b1) + r0_ref[...]


def aligned_end_kernel(y_ref, g_ref, dy_ref, r23_ref, r1_ref, out_ref):
    n_seqs, own, _ = out_ref.shape
    g = g_ref[...]
    for b in range(n_seqs):
        at = slice(b * own, (b + 1) * own)
        n, scale = normed(y_ref[at])
        out_ref[b] = normed_back(n, scale, g * (dy_ref[at] + r23_ref[at] + r1_ref[at]))


def stack_kernel(length, lines, p0_ref, p1_ref, p2_ref, p3_ref, after_ref, out_ref):
    blocks = [ref[ref.shape[0] - lines :, :length] for ref in (p0_ref, p1_ref, p2_ref, p3_ref)]
    pack(lambda t: blocks[t], len(blocks), lines, out_ref)


def chip_stack_kernel(b1_ref, b2_ref, b3_ref, after_ref, out_ref):
    for t, ref in enumerate((b1_ref, b2_ref, b3_ref)):
        out_ref[t] = ref[...]


def core_sum_kernel(p0_ref, p1_ref, m0_ref, m1_ref, after_ref, s0_ref, s1_ref, s2_ref, s3_ref):
    res_n, lines = p0_ref.shape[1:3]
    for t, ref in enumerate((s0_ref, s1_ref, s2_ref, s3_ref)):
        pair = p0_ref[t] + p1_ref[t]
        msa = m0_ref[t] + m1_ref[t]
        blocks = [pair[z] for z in range(res_n)] + [msa[:lines], msa[lines:]]
        pack(lambda i: blocks[i], len(blocks), lines, ref)


def chip_sum_kernel(
    s0_ref, s1_ref, s2_ref, s3_ref, r1_ref, r23_ref, after_ref,
    c0_ref, joint_ref, c2_ref, c3_ref, m_ref,
):
    lines, length = c0_ref.shape
    base = r1_ref.shape[0]
    joint_ref[:base] = r1_ref[...] + r23_ref[base:]
    if length < joint_ref.shape[1]:
        joint_ref[base:, length:] = jnp.zeros((lines, joint_ref.shape[1] - length), F32)
    total = s0_ref[...] + s1_ref[...] + s2_ref[...] + s3_ref[...]
    blocks = unpack(total, 2 * total.shape[0] // (3 * lines), lines)
    for t, ref in enumerate((c0_ref, joint_ref, c2_ref, c3_ref)):
        if t == 1:
            ref[base:, :length] = blocks[t]
        else:
            ref[...] = blocks[t]
    m_ref[:lines] = blocks[-2]
    m_ref[lines:] = blocks[-1]


def pair_end_kernel(
    n_ref, scale_ref, dn_ref, p0_ref, p1_ref, p2_ref, p3_ref, m_ref, wj_ref, out_ref
):
    rows, length, feats = n_ref.shape
    lines = p0_ref.shape[0]
    pair = p0_ref[...] + p2_ref[...] + p3_ref[...]
    pair = pair + p1_ref[p1_ref.shape[0] - lines :, :length]
    msa = m_ref[...]
    pad = jnp.zeros((LANES - pair.shape[0] - msa.shape[0], length), F32)
    b = cat([pair, msa, pad], 0).T
    more = nn(cat(left3(split2(b)), 1), wj_ref[...])
    for j in range(rows):
        dn = dn_ref[j] + more[:, j * feats : (j + 1) * feats]
        out_ref[j] = normed_back(n_ref[j], scale_ref[j], dn)


MIB = 1 << 20


def params(mib, **more):
    return pltpu.CompilerParams(vmem_limit_bytes=mib * MIB, **more)


def vmem(count):
    return [pl.BlockSpec(memory_space=pltpu.VMEM)] * count


def swap(values, axis, size, offset):
    return lax.ppermute(values, axis, [(i, i ^ offset) for i in range(size)])


def fused_on_device(
    seq_n,
    res_n,
    coupled_embedding,
    aligned_embedding,
    coupled_change_adjoint,
    aligned_change_adjoint,
    coupled_scaler,
    coupled_asking_matrix,
    coupled_lookup_matrix,
    coupled_content_matrix,
    coupled_sigmoid_matrix,
    coupled_offset_matrix,
    coupled_result_matrix,
    aligned_scaler,
    coupled_scaler_for_offset,
    aligned_asking_matrix,
    aligned_lookup_matrix,
    aligned_content_matrix,
    aligned_sigmoid_matrix,
    aligned_offset_matrix,
    aligned_result_matrix,
):
    rows, length, feats = coupled_embedding.shape
    n_seqs, own, wide = aligned_embedding.shape
    hp, hm = HP, ALIGNED_SPLITS
    chips = seq_n // 2
    shape = lambda *s: jax.ShapeDtypeStruct(s, F32)
    wp_t, wm_t = coupled_offset_matrix.T, aligned_offset_matrix.T
    gain = coupled_scaler.reshape(1, feats)
    gain2 = coupled_scaler_for_offset.reshape(1, feats)

    lines, base = hp * rows, n_seqs * own
    after = [pl.BlockSpec(memory_space=pl.ANY)]
    packed = lambda count: (3 * count * lines // 2, LANES)
    spread = lambda count: pltpu.VMEM((seq_n, count, lines, length), F32)
    mixed_rows, msa_rows = pl.pallas_call(
        functools.partial(bias_kernel, rows),
        out_shape=(shape(base + lines, wide), shape(*packed(2))),
        scratch_shapes=[pltpu.VMEM((hm * rows, length), F32)],
        compiler_params=params(63),
        name="bias_rows",
    )(
        coupled_embedding, aligned_embedding.reshape(base, wide), gain, wp_t, gain2, wm_t
    )

    def over_chips(first, *behind):
        return pl.pallas_call(
            chip_stack_kernel,
            in_specs=vmem(3) + after * len(behind),
            out_shape=shape(chips - 1, *first.shape),
            compiler_params=params(16),
            name="stack_chips",
        )(*[swap(first, "seq", seq_n, 2 * t) for t in range(1, chips)], *behind)

    def over_cores(first, rest):
        return [first, rest, swap(first, "seq", seq_n, 1), swap(rest, "seq", seq_n, 1)]

    columns = [mixed_rows] + [swap(mixed_rows, "res", res_n, t) for t in range(1, res_n)]

    bf = lambda *s: jax.ShapeDtypeStruct(s, BF16)
    q, k, v, m, kt, vt, d_out, sig, n, scale, wj, wb = pl.pallas_call(
        pair_project_kernel,
        out_shape=(
            bf(rows, length, 3 * feats), bf(rows, length, 3 * feats),
            bf(rows, length, 2 * feats), bf(rows, length, 2 * feats),
            bf(rows, 2 * feats, length), bf(rows, 2 * feats, length),
        ) + (shape(rows, length, feats),) * 4
        + (bf(3 * LANES, rows * feats), bf(2, feats, 4 * feats)),
        compiler_params=params(32),
        name="pair_project",
        cost_estimate=pl.CostEstimate(flops=2 * 10**9, bytes_accessed=10**7, transcendentals=0),
    )(
        coupled_embedding, coupled_change_adjoint, gain, coupled_asking_matrix,
        coupled_lookup_matrix, coupled_content_matrix, coupled_sigmoid_matrix,
        coupled_result_matrix, wp_t, gain2, wm_t,
    )

    msa_rest = over_chips(msa_rows, n)
    msa_blocks = over_cores(msa_rows, msa_rest)
    joint = packed(res_n + 2)
    first = pl.pallas_call(
        functools.partial(stack_kernel, length, lines),
        in_specs=vmem(4) + after,
        out_shape=shape(*packed(res_n)),
        compiler_params=params(16),
        name="stack_rows",
    )(*columns, msa_rest)

    wide_gain = aligned_scaler.reshape(1, wide)
    flat = lambda count: shape(n_seqs * count, wide)
    mq, mm, m_out, m_sig, mk, mv, wkv, wqg = pl.pallas_call(
        msa_project_kernel,
        out_shape=(flat(own),) * 4 + (flat(length),) * 2 + (bf(2, wide, 2 * wide),) * 2,
        scratch_shapes=[pltpu.VMEM((n_seqs, length, wide), F32)],
        compiler_params=params(32),
        name="msa_project",
        cost_estimate=pl.CostEstimate(flops=10**9, bytes_accessed=10**7, transcendentals=0),
    )(
        *columns, aligned_change_adjoint, wide_gain, aligned_asking_matrix,
        aligned_lookup_matrix, aligned_content_matrix, aligned_sigmoid_matrix,
        aligned_result_matrix,
    )

    stretch = pltpu.VMEM((hm * own, length), F32)
    o, dq, kept, r1, r23, msa_near, msa_far = pl.pallas_call(
        functools.partial(msa_kernel, (rows, hm, seq_n, res_n)),
        out_shape=(flat(own),) * 4 + (shape(2 * base, wide),)
        + (shape(chips, hm * rows, length),) * 2,
        scratch_shapes=[
            stretch, stretch, pltpu.VMEM((n_seqs, length, wide), F32),
            spread(hm // hp),
        ],
        compiler_params=params(32),
        name="msa_attention",
        cost_estimate=pl.CostEstimate(flops=4 * 10**9, bytes_accessed=10**7, transcendentals=0),
    )(
        mq, mm, mk, mv, *msa_blocks, wkv,
    )
    far_msa = swap(msa_far, "seq", seq_n, 1)
    r23 = swap(r23, "res", res_n, 2)

    blocks = over_cores(first, over_chips(first, kept))

    batch = 6 if rows % 6 == 0 else 1
    piece = lambda *s: pl.BlockSpec((batch,) + s, lambda i: (i, 0, 0))
    whole = lambda *s: pl.BlockSpec(s, lambda i: (0,) * len(s))
    quarter = (chips, res_n, lines, length)
    ot, dqt, dk, dv, near, far = pl.pallas_call(
        functools.partial(pair_kernel, (rows, hp, seq_n, res_n)),
        grid=(rows // batch,),
        in_specs=[
            piece(length, 3 * feats), piece(length, 3 * feats),
            piece(length, 2 * feats), piece(length, 2 * feats),
            piece(2 * feats, length), piece(2 * feats, length),
        ] + [whole(*packed(res_n)), whole(chips - 1, *packed(res_n))] * 2 + after,
        out_specs=(
            piece(HEAD, hp * length), piece(HEAD, hp * length),
            piece(length, feats), piece(length, feats), whole(*quarter), whole(*quarter),
        ),
        out_shape=(
            shape(rows, HEAD, hp * length), shape(rows, HEAD, hp * length),
            shape(rows, length, feats), shape(rows, length, feats),
            shape(*quarter), shape(*quarter),
        ),
        scratch_shapes=[
            pltpu.VMEM((length, hp * length), F32),
            pltpu.VMEM((length, hp * length), F32),
            pltpu.VMEM((hp * length, length), F32),
            spread(res_n),
        ],
        compiler_params=params(32),
        name="pair_attention",
        cost_estimate=pl.CostEstimate(flops=10**10, bytes_accessed=10**7, transcendentals=0),
    )(q, k, v, m, kt, vt, *blocks, kept)
    far_pair = swap(far, "seq", seq_n, 1)
    dn = pl.pallas_call(
        pair_back_kernel,
        out_shape=shape(rows, length, feats),
        compiler_params=params(32),
        name="pair_back",
        cost_estimate=pl.CostEstimate(flops=10**11, bytes_accessed=10**8, transcendentals=0),
    )(
        ot, dqt, dk, dv, d_out, sig, gain, wb,
    )
    sums = pl.pallas_call(
        core_sum_kernel,
        in_specs=vmem(4) + after,
        out_shape=(shape(*joint),) * chips,
        compiler_params=params(16),
        name="core_sum",
    )(near, far_pair, msa_near, far_msa, dn)
    dy = pl.pallas_call(
        aligned_back_kernel,
        out_shape=flat(own),
        compiler_params=params(16),
        name="aligned_back",
        cost_estimate=pl.CostEstimate(flops=10**9, bytes_accessed=10**6, transcendentals=0),
    )(o, dq, m_out, m_sig, wqg, kept)
    c0, mixed_sum, c2, c3, msa_sum = pl.pallas_call(
        chip_sum_kernel,
        in_specs=vmem(6) + after,
        out_shape=(
            shape(lines, length), shape(base + lines, wide), shape(lines, length),
            shape(lines, length), shape(hm * rows, length),
        ),
        compiler_params=params(16),
        name="chip_sum",
    )(sums[0], *[swap(sums[t], "seq", seq_n, 2 * t) for t in range(1, chips)], r1, r23, dy)
    mixed_sum, c2, c3 = [swap(a, "res", res_n, t) for a, t in ((mixed_sum, 1), (c2, 2), (c3, 3))]

    aligned_out = pl.pallas_call(
        aligned_end_kernel,
        out_shape=shape(n_seqs, own, wide),
        compiler_params=params(16),
        name="aligned_end",
    )(mixed_rows, wide_gain, dy, r23, mixed_sum)
    coupled_out = pl.pallas_call(
        pair_end_kernel,
        out_shape=shape(rows, length, feats),
        compiler_params=params(16),
        name="pair_end",
    )(n, scale, dn, c0, mixed_sum, c2, c3, msa_sum, wj)
    return coupled_out, aligned_out


def on_device(seq_n, res_n, *arrays):
    length = arrays[0].shape[1]
    rows = arrays[0].shape[0]
    narrow = length <= arrays[1].shape[2] and HP * length % TILE == 0
    narrow = narrow and rows * (HP + ALIGNED_SPLITS) <= LANES
    narrow = narrow and ALIGNED_SPLITS == 2 * HP and 2 * (length - LANES) == LANES
    if narrow and seq_n == 8 and res_n == 4:
        return fused_on_device(seq_n, res_n, *arrays)
    return scanned_on_device(*arrays)


def solution(mesh):
    in_specs = (
        P(("res", "seq"), None, None),
        P("seq", "res", None),
        P(("res", "seq"), None, None),
        P("seq", "res", None),
        P(),
        P(),
        P(),
        P(),
        P(),
        P(),
        P(),
        P(),
        P(),
        P(),
        P(),
        P(),
        P(),
        P(),
        P(),
    )
    out_specs = (P(("res", "seq"), None, None), P("seq", "res", None))
    return jax.shard_map(
        functools.partial(on_device, mesh.shape["seq"], mesh.shape["res"]),
        mesh=mesh, in_specs=in_specs, out_specs=out_specs, check_vma=False
    )
```

```python
import functools
import math

import jax
import jax.numpy as jnp
from jax import lax
from jax.experimental import pallas as pl
from jax.experimental.pallas import tpu as pltpu
from jax.sharding import PartitionSpec as P

HP = 4
ALIGNED_SPLITS = 8


EXACT_MATMUL = lax.Precision.HIGHEST
EPSILON = 1e-05


def standardize_features(values, norm_gain):
    center = values - jnp.mean(values, axis=-1, keepdims=True)
    spread = jnp.mean(center * center, axis=-1, keepdims=True)
    return center * lax.rsqrt(spread + EPSILON) * norm_gain


def affine_map(values, weight):
    return jnp.einsum("...c,ce->...e", values, weight, precision=EXACT_MATMUL)


def sigmoid_mixing(query_vectors, key_rows, value_rows, gate_preact, softmax_offset, head_count):
    query_shape = query_vectors.shape
    head_width = query_shape[-1] // head_count
    query_heads = query_vectors.reshape(query_shape[:-1] + (head_count, head_width))
    key_heads = key_rows.reshape(key_rows.shape[:-1] + (head_count, head_width))
    value_heads = value_rows.reshape(value_rows.shape[:-1] + (head_count, head_width))
    logits = (
        jnp.einsum("...qhd,...khd->...qhk", query_heads, key_heads, precision=EXACT_MATMUL)
        / math.sqrt(head_width)
        + softmax_offset
    )
    largest = lax.stop_gradient(jnp.max(logits, axis=-1, keepdims=True))
    weights = jnp.exp(logits - largest)
    weights = weights / jnp.sum(weights, axis=-1, keepdims=True)
    mixed_contents = jnp.einsum(
        "...qhk,...khd->...qhd", weights, value_heads, precision=EXACT_MATMUL
    )
    return mixed_contents.reshape(query_shape) * jax.nn.sigmoid(gate_preact)


def scanned_on_device(
    coupled_embedding,
    aligned_embedding,
    coupled_change_adjoint,
    aligned_change_adjoint,
    coupled_scaler,
    coupled_asking_matrix,
    coupled_lookup_matrix,
    coupled_content_matrix,
    coupled_sigmoid_matrix,
    coupled_offset_matrix,
    coupled_result_matrix,
    aligned_scaler,
    coupled_scaler_for_offset,
    aligned_asking_matrix,
    aligned_lookup_matrix,
    aligned_content_matrix,
    aligned_sigmoid_matrix,
    aligned_offset_matrix,
    aligned_result_matrix,
):

    def pair_local(entering_lines):
        standardized_source = standardize_features(entering_lines, coupled_scaler)
        return (
            affine_map(standardized_source, coupled_asking_matrix),
            affine_map(standardized_source, coupled_lookup_matrix),
            affine_map(standardized_source, coupled_content_matrix),
            affine_map(standardized_source, coupled_sigmoid_matrix),
            jnp.einsum(
                "jkc,ch->jhk", standardized_source, coupled_offset_matrix, precision=EXACT_MATMUL
            ),
        )

    (row_queries, row_keys, row_values, row_gates, bias_rows), pair_back = jax.vjp(
        pair_local, coupled_embedding
    )
    by_seq = lax.all_gather(bias_rows, "seq", axis=0, tiled=True)
    full_bias = lax.all_gather(by_seq, "res", axis=0, tiled=True)

    def row_output(one_query, one_key, one_value, one_gate, softmax_offset):
        return affine_map(
            sigmoid_mixing(one_query, one_key, one_value, one_gate, softmax_offset, HP),
            coupled_result_matrix,
        )

    def row_step(bias_sum, row_items):
        one_query, one_key, one_value, one_gate, one_cotan = row_items
        discarded_entry, row_back = jax.vjp(
            row_output, one_query, one_key, one_value, one_gate, full_bias
        )
        grad_query, grad_key, grad_value, grad_gate, grad_bias = row_back(one_cotan)
        return (bias_sum + grad_bias, (grad_query, grad_key, grad_value, grad_gate))

    bias_total, row_grads = lax.scan(
        row_step,
        jnp.zeros_like(full_bias),
        (row_queries, row_keys, row_values, row_gates, coupled_change_adjoint),
    )
    by_res = lax.psum_scatter(bias_total, "res", scatter_dimension=0, tiled=True)
    bias_grad_rows = lax.psum_scatter(by_res, "seq", scatter_dimension=0, tiled=True)
    (mixed_result_sensitivity,) = pair_back(row_grads + (bias_grad_rows,))

    def aligned_offset_portion(entering_lines):
        return jnp.einsum(
            "gys,sj->gjy",
            standardize_features(entering_lines, coupled_scaler_for_offset),
            aligned_offset_matrix,
            precision=EXACT_MATMUL,
        )

    aligned_offset_part, aligned_offset_reverse = jax.vjp(aligned_offset_portion, coupled_embedding)
    tile_softmax_offset = lax.all_gather(aligned_offset_part, "seq", axis=0, tiled=True)

    def sequence_output(query_vectors, full_key_rows, full_value_rows, gate_preact, softmax_offset):
        return affine_map(
            sigmoid_mixing(
                query_vectors,
                full_key_rows,
                full_value_rows,
                gate_preact,
                softmax_offset,
                ALIGNED_SPLITS,
            ),
            aligned_result_matrix,
        )

    state_all = lax.all_gather(aligned_embedding, "res", axis=1, tiled=True)

    def near_local(carry_pile):
        standardized_source = standardize_features(carry_pile, aligned_scaler)
        return (
            affine_map(standardized_source, aligned_asking_matrix),
            affine_map(standardized_source, aligned_sigmoid_matrix),
        )

    def keys_local(carry_pile):
        standardized_source = standardize_features(carry_pile, aligned_scaler)
        return (
            affine_map(standardized_source, aligned_lookup_matrix),
            affine_map(standardized_source, aligned_content_matrix),
        )

    (aligned_asking_lines, aligned_sigmoid_factors), near_back = jax.vjp(
        near_local, aligned_embedding
    )
    (full_key_rows, full_value_rows), keys_back = jax.vjp(keys_local, state_all)
    discarded_entry, sigmoid_mixing_reverse = jax.vjp(
        sequence_output,
        aligned_asking_lines,
        full_key_rows,
        full_value_rows,
        aligned_sigmoid_factors,
        tile_softmax_offset,
    )
    query_gradient, full_key_gradient, full_value_gradient, gate_gradient, block_bias_gradient = (
        sigmoid_mixing_reverse(aligned_change_adjoint)
    )
    (state_term,) = keys_back((full_key_gradient, full_value_gradient))
    spread_grad = lax.psum_scatter(state_term, "res", scatter_dimension=1, tiled=True)
    (near_grad,) = near_back((query_gradient, gate_gradient))
    aligned_embedding_sensitivity = near_grad + spread_grad
    offset_line_sensitivity = lax.psum_scatter(
        block_bias_gradient, "seq", scatter_dimension=0, tiled=True
    )
    (coupled_sensitivity_via_offset,) = aligned_offset_reverse(offset_line_sensitivity)
    return (
        mixed_result_sensitivity + coupled_sensitivity_via_offset,
        aligned_embedding_sensitivity,
    )


F32 = jnp.float32
BF16 = jnp.bfloat16
HEAD = 32
LANES = 128
TILE = 256


def split2(a):
    top = a.astype(BF16)
    return top, (a - top.astype(F32)).astype(BF16)


def split3(a):
    top = a.astype(BF16)
    rest = a - top.astype(F32)
    mid = rest.astype(BF16)
    return top, mid, (rest - mid.astype(F32)).astype(BF16)


def left6(parts):
    a, b, c = parts
    return [a, a, b, b, a, c]


def right6(parts):
    a, b, c = parts
    return [a, b, a, b, c, a]


def left3(parts):
    return [parts[0], parts[0], parts[1]]


def right3(parts):
    return [parts[0], parts[1], parts[0]]


def nn(a, b):
    return lax.dot_general(a, b, (((1,), (0,)), ((), ())), preferred_element_type=F32)


def nt(a, b):
    return lax.dot_general(a, b, (((1,), (1,)), ((), ())), preferred_element_type=F32)


def cat(parts, axis):
    return jnp.concatenate(parts, axis=axis)


def normed(v):
    center = v - jnp.mean(v, axis=-1, keepdims=True)
    spread = jnp.mean(center * center, axis=-1, keepdims=True)
    scale = lax.rsqrt(spread + EPSILON)
    return center * scale, scale


def normed_back(n, scale, dn):
    return scale * (
        dn - jnp.mean(dn, axis=-1, keepdims=True) - n * jnp.mean(dn * n, axis=-1, keepdims=True)
    )


def head_mask(h, dtype):
    lane = lax.broadcasted_iota(jnp.int32, (1, LANES), 1)
    return jnp.where((lane // HEAD) == h, 1.0, 0.0).astype(dtype)


def pack(block_of, count, lines, out_ref):
    half = count // 2
    for t in range(half):
        first, second = block_of(t), block_of(t + half)
        out_ref[t * lines : (t + 1) * lines] = first[:, :LANES]
        out_ref[(t + half) * lines : (t + half + 1) * lines] = second[:, :LANES]
        rest = cat([first[:, LANES:], second[:, LANES:]], 1)
        out_ref[(t + count) * lines : (t + count + 1) * lines] = rest


def unpack(dense, count, lines):
    half = count // 2
    blocks = []
    for t in range(count):
        rest = dense[(count + t % half) * lines : (count + t % half + 1) * lines]
        rest = rest[:, : LANES // 2] if t < half else rest[:, LANES // 2 :]
        blocks.append(cat([dense[t * lines : (t + 1) * lines], rest], 1))
    return blocks


def bias_kernel(rows, x_ref, y_ref, g_ref, wp_ref, g2_ref, wm_ref, joint_ref, packed_ref, bm_ref):
    length = x_ref.shape[1]
    base, wide = y_ref.shape
    joint_ref[:base] = y_ref[...]
    if length < wide:
        joint_ref[base:, length:] = jnp.zeros((wp_ref.shape[0] * rows, wide - length), F32)
    hp, hm = wp_ref.shape[0], wm_ref.shape[0]
    w = cat([wp_ref[...] * g_ref[...], wm_ref[...] * g2_ref[...]], 0)
    wcat = cat(left6(split3(w)), 1)
    for j in range(rows):
        n, _ = normed(x_ref[j])
        res = nt(wcat, cat(right6(split3(n)), 1))
        for h in range(hp):
            at = base + h * rows + j
            joint_ref[at : at + 1, :length] = res[h : h + 1]
        for h in range(hm):
            bm_ref[h * rows + j : h * rows + j + 1, :] = res[hp + h : hp + h + 1]
    lines = hp * rows
    pack(lambda t: bm_ref[t * lines : (t + 1) * lines], hm // hp, lines, packed_ref)


def pair_project_kernel(
    x_ref, adj_ref, g_ref, wq_ref, wk_ref, wv_ref, wg_ref, wo_ref, wp_ref, g2_ref, wm_ref,
    q_ref, k_ref, v_ref, m_ref, kt_ref, vt_ref, dout_ref, sig_ref, n_ref, scale_ref, wj_ref, wb_ref,
):
    rows, length, feats = x_ref.shape
    g = g_ref[...]
    top, low = split2(cat([wq_ref[...], wk_ref[...], wv_ref[...], wg_ref[...]], 1))
    wb_ref[0] = top
    wb_ref[1] = low
    w6 = cat(right6(split3(cat([wq_ref[...], wk_ref[...]], 1))), 0)
    w3 = cat(right3(split2(cat([wv_ref[...], wg_ref[...]], 1))), 0)
    wo3 = cat(right3(split2(wo_ref[...])), 1)
    for i in range(rows):
        n, scale = normed(x_ref[i])
        n_ref[i] = n
        scale_ref[i] = jnp.broadcast_to(scale, n.shape)
        parts = split3(n * g)
        qk = nn(cat(left6(parts), 1), w6)
        vg = nn(cat(left3(parts), 1), w3)
        d_out = nt(cat(left3(split2(adj_ref[i])), 1), wo3)
        sig = jax.nn.sigmoid(vg[:, feats:])
        dout_ref[i] = d_out
        sig_ref[i] = sig
        q, k, v = qk[:, :feats] * (1.0 / math.sqrt(HEAD)), qk[:, feats:], vg[:, :feats]
        q_ref[i] = cat(split3(q), 1)
        k_ref[i] = cat(split3(k), 1)
        v_ref[i] = cat(split2(v), 1)
        m_ref[i] = cat(split2(d_out * sig), 1)
        kt_ref[i] = cat(split2(k.T), 0)
        vt_ref[i] = cat(split2(v.T), 0)
    hp, hm = wp_ref.shape[0], wm_ref.shape[0]
    w = cat([wp_ref[...] * g, wm_ref[...] * g2_ref[...]], 0)
    lines = [jnp.broadcast_to(w[h : h + 1], (rows, feats)) for h in range(hp + hm)]
    lines += [jnp.zeros((LANES - rows * (hp + hm), feats), F32)]
    spread = cat(lines, 0)
    at = lax.broadcasted_iota(jnp.int32, (LANES, 1), 0)
    for j in range(rows):
        mine = jnp.where(lax.rem(at, rows) == j, spread, 0.0)
        wj_ref[:, j * feats : (j + 1) * feats] = cat(right3(split2(mine)), 0)


def gather_chips(natural, refs, core, chip):
    _, count, lines, _ = natural.shape
    for (own_ref, others_ref), side in zip((refs[:2], refs[2:]), (core, 1 - core)):
        for t in range(others_ref.shape[0] + 1):
            at = lax.bitwise_xor(chip, t) * 2 + side
            dense = others_ref[t - 1] if t > 0 else own_ref[...]
            for i, block in enumerate(unpack(dense, count, lines)):
                natural[at, i] = block


def pair_kernel(
    dims,
    q_ref, k_ref, v_ref, m_ref, kt_ref, vt_ref,
    b0_ref, b1_ref, b2_ref, b3_ref,
    after_ref,
    ot_ref, dqt_ref, dk_ref, dv_ref, near_ref, far_ref,
    bt, dbt, stack, natural,
):
    rows, heads, seq_n, res_n = dims
    step = pl.program_id(0)
    seq, res = lax.axis_index("seq"), lax.axis_index("res")
    core, chip = lax.rem(seq, 2), lax.div(seq, 2)
    n_keys = q_ref.shape[1]

    @pl.when(step == 0)
    def _():
        blocks = (b0_ref, b1_ref, b2_ref, b3_ref)
        gather_chips(natural, blocks, core, chip)
        for z in range(res_n):
            zi = lax.bitwise_xor(res, z)
            for s in range(seq_n):
                block = natural[s, zi]
                d = z * seq_n + s
                for h in range(heads):
                    at = h * n_keys + d * rows
                    stack[at : at + rows, :] = block[h * rows : (h + 1) * rows]
        bt[...] = stack[...].T
        dbt[...] = jnp.zeros_like(dbt)

    def pieces(ref, u, count):
        return [ref[u, :, t * LANES : (t + 1) * LANES] for t in range(count)]

    masks = [head_mask(h, BF16) for h in range(heads)]
    tiles = heads * n_keys // TILE
    batch = q_ref.shape[0]

    def operands(u):
        qs = [cat([a * mask for mask in masks], 0) for a in pieces(q_ref, u, 3)]
        ms = [cat([a * mask for mask in masks], 0) for a in pieces(m_ref, u, 2)]
        kcat = cat(left6(pieces(k_ref, u, 3)), 1)
        vcat = cat(left3(pieces(v_ref, u, 2)), 1)
        return qs, ms, kcat, vcat

    rows_in = {}

    def logits(item):
        u, c = divmod(item, tiles)
        if u not in rows_in:
            rows_in[u] = operands(u)
        qs, ms, kcat, vcat = rows_in[u]
        cols = slice(c * TILE, (c + 1) * TILE)
        qc, mc = [a[cols] for a in qs], [a[cols] for a in ms]
        s = nt(kcat, cat(right6(qc), 1)) + bt[:, cols]
        return s, nt(vcat, cat(right3(mc), 1)), qc, mc

    def weights(item, s, dp):
        c = item % tiles
        cols = slice(c * TILE, (c + 1) * TILE)
        e = jnp.exp(s - jnp.max(s, axis=0, keepdims=True))
        p = e * (1.0 / jnp.sum(e, axis=0, keepdims=True))
        ds = p * (dp - jnp.sum(p * dp, axis=0, keepdims=True))
        dbt[:, cols] = dbt[:, cols] + ds
        return split2(p) + split2(ds)

    sums = {}

    def products(item, p1, p2, s1, s2, qc, mc):
        u, c = divmod(item, tiles)
        cols = slice(c * TILE, (c + 1) * TILE)
        first, last = c * TILE // n_keys, ((c + 1) * TILE - 1) // n_keys
        lane = lax.broadcasted_iota(jnp.int32, (1, TILE), 1) + c * TILE

        def of_heads(ref, a1, a2):
            top = ref[u, first * HEAD : (last + 1) * HEAD]
            low = ref[u, LANES + first * HEAD : LANES + (last + 1) * HEAD]
            both = nn(cat([top, low], 0), a1)
            half = both.shape[0] // 2
            total = both[:half] + both[half:] + nn(top, a2)
            picked = total[:HEAD]
            for h in range(first + 1, last + 1):
                rest = total[(h - first) * HEAD : (h - first + 1) * HEAD]
                picked = jnp.where(lane >= h * n_keys, rest, picked)
            return picked

        ot_ref[u, :, cols] = of_heads(vt_ref, p1, p2)
        dqt_ref[u, :, cols] = of_heads(kt_ref, s1, s2)
        both = nn(s1, cat(qc[:2], 1))
        dk = both[:, :LANES] + both[:, LANES:] + nn(s2, qc[0])
        both = nn(p1, cat(mc, 1))
        dv = both[:, :LANES] + both[:, LANES:] + nn(p2, mc[0])
        if c > 0:
            dk, dv = sums[u][0] + dk, sums[u][1] + dv
        sums[u] = (dk, dv)
        if c == tiles - 1:
            dk_ref[u] = dk
            dv_ref[u] = dv

    count = batch * tiles
    ready, waiting = {}, {}
    for item in range(-1, count + 1):
        if 0 <= item + 1 < count:
            ready[item + 1] = logits(item + 1)
        if 0 <= item < count:
            s, dp, qc, mc = ready.pop(item)
            waiting[item] = weights(item, s, dp) + (qc, mc)
        if 0 <= item - 1 < count:
            products(item - 1, *waiting.pop(item - 1))

    @pl.when(step == pl.num_programs(0) - 1)
    def _():
        stack[...] = dbt[...].T
        for z in range(res_n):
            zi = lax.bitwise_xor(res, z)
            for pair in range(seq_n // 2):
                ci = lax.bitwise_xor(chip, pair)
                blocks = []
                for s in (2 * pair, 2 * pair + 1):
                    at = [h * n_keys + (z * seq_n + s) * rows for h in range(heads)]
                    blocks.append(cat([stack[a : a + rows, :] for a in at], 0))
                near_ref[ci, zi] = jnp.where(core == 0, blocks[0], blocks[1])
                far_ref[ci, zi] = jnp.where(core == 0, blocks[1], blocks[0])


def pair_back_kernel(
    ot_ref, dqt_ref, dk_ref, dv_ref, dout_ref, sig_ref,
    g_ref, wb_ref, dn_ref,
):
    rows, length, feats = dk_ref.shape
    g = g_ref[...]
    w1, w2 = wb_ref[0], wb_ref[1]

    def lines(flat):
        heads = flat.shape[1] // length
        return cat([flat[:, h * length : (h + 1) * length] for h in range(heads)], 0).T

    for i in range(rows):
        o, sig = lines(ot_ref[i]), sig_ref[i]
        d_gate = dout_ref[i] * o * sig * (1.0 - sig)
        dq = lines(dqt_ref[i]) * (1.0 / math.sqrt(HEAD))
        t1, t2 = split2(cat([dq, dk_ref[i], dv_ref[i], d_gate], 1))
        dn_ref[i] = g * (nt(t1, w1) + nt(t1, w2) + nt(t2, w1))


def msa_project_kernel(
    y0_ref, y1_ref, y2_ref, y3_ref, adj_ref,
    g_ref, wq_ref, wk_ref, wv_ref, wg_ref, wo_ref,
    q_ref, m_ref, dout_ref, sig_ref, k_ref, v_ref, wkv_ref, wqg_ref,
    yall,
):
    res = lax.axis_index("res")
    n_seqs, own, feats = adj_ref.shape
    n_keys = yall.shape[1]
    g = g_ref[...]
    for t, ref in enumerate((y0_ref, y1_ref, y2_ref, y3_ref)):
        at = pl.multiple_of(lax.bitwise_xor(res, t) * own, own)
        for b in range(n_seqs):
            yall[b, pl.ds(at, own), :] = ref[b * own : (b + 1) * own, :]
    n_own, _ = normed(y0_ref[: n_seqs * own])
    n_all, _ = normed(yall[...].reshape(n_seqs * n_keys, feats))
    own_parts, all_parts = split3(n_own * g), split3(n_all * g)
    for ref, pair in ((wkv_ref, (wk_ref, wv_ref)), (wqg_ref, (wq_ref, wg_ref))):
        top, low = split2(cat([pair[0][...], pair[1][...]], 1))
        ref[0] = top
        ref[1] = low
    q = nn(cat(left6(own_parts), 1), cat(right6(split3(wq_ref[...])), 0))
    gate = nn(cat(left3(own_parts), 1), cat(right3(split2(wg_ref[...])), 0))
    k = nn(cat(left6(all_parts), 1), cat(right6(split3(wk_ref[...])), 0))
    v = nn(cat(left3(all_parts), 1), cat(right3(split2(wv_ref[...])), 0))
    adj = adj_ref[...].reshape(n_seqs * own, feats)
    d_out = nt(cat(left3(split2(adj)), 1), cat(right3(split2(wo_ref[...])), 1))
    sig = jax.nn.sigmoid(gate)
    q_ref[...] = q * (1.0 / math.sqrt(HEAD))
    m_ref[...] = d_out * sig
    dout_ref[...] = d_out
    sig_ref[...] = sig
    k_ref[...] = k
    v_ref[...] = v


def msa_kernel(
    dims,
    q_ref, m_ref, k_ref, v_ref,
    b0_ref, b1_ref, b2_ref, b3_ref,
    wkv_ref,
    o_ref, dq_ref, r0_ref, r1_ref, r23_ref, near_ref, far_ref,
    bias, dbias, dyall, natural,
):
    rows, heads, seq_n, res_n = dims
    seq, res = lax.axis_index("seq"), lax.axis_index("res")
    core, chip = lax.rem(seq, 2), lax.div(seq, 2)
    n_seqs, n_keys, feats = dyall.shape
    own = n_keys // res_n
    tiles, group = feats // LANES, LANES // HEAD
    blocks = (b0_ref, b1_ref, b2_ref, b3_ref)
    gather_chips(natural, blocks, core, chip)
    for s in range(seq_n):
        block = cat([natural[s, 0], natural[s, 1]], 0)
        for h in range(heads):
            at = h * own + s * rows
            bias[at : at + rows, :] = block[h * rows : (h + 1) * rows]
    masks = [head_mask(u, BF16) for u in range(group)]
    fmasks = [head_mask(u, F32) for u in range(group)]

    def stacked(a, by):
        return cat([a * mask for mask in by], 0)

    def own_rows(full):
        total = fmasks[0] * full[:own]
        for u in range(1, group):
            total = total + fmasks[u] * full[u * own : (u + 1) * own]
        return total

    b1, b2 = wkv_ref[0], wkv_ref[1]

    def spans(item):
        b, t = divmod(item, tiles)
        near = slice(b * own, (b + 1) * own)
        wide = slice(b * n_keys, (b + 1) * n_keys)
        cols = slice(t * LANES, (t + 1) * LANES)
        return b, near, wide, cols, slice(t * group * own, (t + 1) * group * own)

    def logits(item):
        b, near, wide, cols, lines = spans(item)
        qs = [stacked(a, masks) for a in split3(q_ref[near, cols])]
        ms = [stacked(a, masks) for a in split2(m_ref[near, cols])]
        kp = split3(k_ref[wide, cols])
        vp = split2(v_ref[wide, cols])
        s = nt(cat(left6(qs), 1), cat(right6(kp), 1)) + bias[lines]
        return s, nt(cat(left3(ms), 1), cat(right3(vp), 1)), kp, vp

    def weights(item, s, dp):
        b, near, wide, cols, lines = spans(item)
        e = jnp.exp(s - jnp.max(s, axis=1, keepdims=True))
        p = e * (1.0 / jnp.sum(e, axis=1, keepdims=True))
        ds = p * (dp - jnp.sum(p * dp, axis=1, keepdims=True))
        dbias[lines] = ds if b == 0 else dbias[lines] + ds
        return split2(p) + split2(ds)

    turned = {}

    def products(item, p1, p2, s1, s2, kp, vp):
        b, near, wide, cols, lines = spans(item)
        qt1, qt2 = split2(stacked(q_ref[near, cols], fmasks).T)
        mt1, mt2 = split2(stacked(m_ref[near, cols], fmasks).T)
        both = nn(p1, cat(vp, 1))
        o_ref[near, cols] = own_rows(both[:, :LANES] + both[:, LANES:] + nn(p2, vp[0]))
        both = nn(s1, cat(kp[:2], 1))
        dq_ref[near, cols] = own_rows(both[:, :LANES] + both[:, LANES:] + nn(s2, kp[0]))
        both = nn(cat([qt1, qt2], 0), s1)
        dkt = both[:LANES] + both[LANES:] + nn(qt1, s2)
        both = nn(cat([mt1, mt2], 0), p1)
        dvt = both[:LANES] + both[LANES:] + nn(mt1, p2)
        turned.setdefault(b, []).append((dkt, dvt))
        if len(turned[b]) == tiles:
            flat = [a[0].T for a in turned[b]] + [a[1].T for a in turned[b]]
            t1, t2 = split2(cat(flat, 1))
            dyall[b] = nt(t1, b1) + nt(t1, b2) + nt(t2, b1)

    count = n_seqs * tiles
    ready, waiting = {}, {}
    for item in range(-1, count + 1):
        if 0 <= item + 1 < count:
            ready[item + 1] = logits(item + 1)
        if 0 <= item < count:
            s, dp, kp, vp = ready.pop(item)
            waiting[item] = weights(item, s, dp) + (kp, vp)
        if 0 <= item - 1 < count:
            products(item - 1, *waiting.pop(item - 1))
    for t, (ref, base) in enumerate(((r0_ref, 0), (r1_ref, 0), (r23_ref, 0), (r23_ref, n_seqs))):
        at = pl.multiple_of(lax.bitwise_xor(res, t) * own, own)
        for b in range(n_seqs):
            to = (base + b) * own
            ref[to : to + own, :] = dyall[b, pl.ds(at, own), :]
    for pair in range(seq_n // 2):
        ci = lax.bitwise_xor(chip, pair)
        blocks = []
        for s in (2 * pair, 2 * pair + 1):
            at = [h * own + s * rows for h in range(heads)]
            blocks.append(cat([dbias[a : a + rows, :] for a in at], 0))
        near_ref[ci] = jnp.where(core == 0, blocks[0], blocks[1])
        far_ref[ci] = jnp.where(core == 0, blocks[1], blocks[0])


def aligned_back_kernel(o_ref, dq_ref, dout_ref, sig_ref, wqg_ref, r0_ref, dy_ref):
    sig = sig_ref[...]
    d_gate = dout_ref[...] * o_ref[...] * sig * (1.0 - sig)
    t1, t2 = split2(cat([dq_ref[...] * (1.0 / math.sqrt(HEAD)), d_gate], 1))
    b1, b2 = wqg_ref[0], wqg_ref[1]
    dy_ref[...] = nt(t1, b1) + nt(t1, b2) + nt(t2, b1) + r0_ref[...]


def aligned_end_kernel(y_ref, g_ref, dy_ref, r23_ref, r1_ref, out_ref):
    n_seqs, own, _ = out_ref.shape
    g = g_ref[...]
    for b in range(n_seqs):
        at = slice(b * own, (b + 1) * own)
        n, scale = normed(y_ref[at])
        out_ref[b] = normed_back(n, scale, g * (dy_ref[at] + r23_ref[at] + r1_ref[at]))


def stack_kernel(length, lines, p0_ref, p1_ref, p2_ref, p3_ref, after_ref, out_ref):
    blocks = [ref[ref.shape[0] - lines :, :length] for ref in (p0_ref, p1_ref, p2_ref, p3_ref)]
    pack(lambda t: blocks[t], len(blocks), lines, out_ref)


def chip_stack_kernel(b1_ref, b2_ref, b3_ref, after_ref, out_ref):
    for t, ref in enumerate((b1_ref, b2_ref, b3_ref)):
        out_ref[t] = ref[...]


def core_sum_kernel(p0_ref, p1_ref, m0_ref, m1_ref, after_ref, s0_ref, s1_ref, s2_ref, s3_ref):
    res_n, lines = p0_ref.shape[1:3]
    for t, ref in enumerate((s0_ref, s1_ref, s2_ref, s3_ref)):
        pair = p0_ref[t] + p1_ref[t]
        msa = m0_ref[t] + m1_ref[t]
        blocks = [pair[z] for z in range(res_n)] + [msa[:lines], msa[lines:]]
        pack(lambda i: blocks[i], len(blocks), lines, ref)


def chip_sum_kernel(
    s0_ref, s1_ref, s2_ref, s3_ref, r1_ref, r23_ref, after_ref,
    c0_ref, joint_ref, c2_ref, c3_ref, m_ref,
):
    lines, length = c0_ref.shape
    base = r1_ref.shape[0]
    joint_ref[:base] = r1_ref[...] + r23_ref[base:]
    if length < joint_ref.shape[1]:
        joint_ref[base:, length:] = jnp.zeros((lines, joint_ref.shape[1] - length), F32)
    total = s0_ref[...] + s1_ref[...] + s2_ref[...] + s3_ref[...]
    blocks = unpack(total, 2 * total.shape[0] // (3 * lines), lines)
    for t, ref in enumerate((c0_ref, joint_ref, c2_ref, c3_ref)):
        if t == 1:
            ref[base:, :length] = blocks[t]
        else:
            ref[...] = blocks[t]
    m_ref[:lines] = blocks[-2]
    m_ref[lines:] = blocks[-1]


def pair_end_kernel(
    n_ref, scale_ref, dn_ref, p0_ref, p1_ref, p2_ref, p3_ref, m_ref, wj_ref, out_ref
):
    rows, length, feats = n_ref.shape
    lines = p0_ref.shape[0]
    pair = p0_ref[...] + p2_ref[...] + p3_ref[...]
    pair = pair + p1_ref[p1_ref.shape[0] - lines :, :length]
    msa = m_ref[...]
    pad = jnp.zeros((LANES - pair.shape[0] - msa.shape[0], length), F32)
    b = cat([pair, msa, pad], 0).T
    more = nn(cat(left3(split2(b)), 1), wj_ref[...])
    for j in range(rows):
        dn = dn_ref[j] + more[:, j * feats : (j + 1) * feats]
        out_ref[j] = normed_back(n_ref[j], scale_ref[j], dn)


MIB = 1 << 20


def params(mib, **more):
    return pltpu.CompilerParams(vmem_limit_bytes=mib * MIB, **more)


def vmem(count):
    return [pl.BlockSpec(memory_space=pltpu.VMEM)] * count


def swap(values, axis, size, offset):
    return lax.ppermute(values, axis, [(i, i ^ offset) for i in range(size)])


def fused_on_device(
    seq_n,
    res_n,
    coupled_embedding,
    aligned_embedding,
    coupled_change_adjoint,
    aligned_change_adjoint,
    coupled_scaler,
    coupled_asking_matrix,
    coupled_lookup_matrix,
    coupled_content_matrix,
    coupled_sigmoid_matrix,
    coupled_offset_matrix,
    coupled_result_matrix,
    aligned_scaler,
    coupled_scaler_for_offset,
    aligned_asking_matrix,
    aligned_lookup_matrix,
    aligned_content_matrix,
    aligned_sigmoid_matrix,
    aligned_offset_matrix,
    aligned_result_matrix,
):
    rows, length, feats = coupled_embedding.shape
    n_seqs, own, wide = aligned_embedding.shape
    hp, hm = HP, ALIGNED_SPLITS
    chips = seq_n // 2
    shape = lambda *s: jax.ShapeDtypeStruct(s, F32)
    wp_t, wm_t = coupled_offset_matrix.T, aligned_offset_matrix.T
    gain = coupled_scaler.reshape(1, feats)
    gain2 = coupled_scaler_for_offset.reshape(1, feats)

    lines, base = hp * rows, n_seqs * own
    after = [pl.BlockSpec(memory_space=pl.ANY)]
    packed = lambda count: (3 * count * lines // 2, LANES)
    spread = lambda count: pltpu.VMEM((seq_n, count, lines, length), F32)
    mixed_rows, msa_rows = pl.pallas_call(
        functools.partial(bias_kernel, rows),
        out_shape=(shape(base + lines, wide), shape(*packed(2))),
        scratch_shapes=[pltpu.VMEM((hm * rows, length), F32)],
        compiler_params=params(63),
        name="bias_rows",
    )(
        coupled_embedding, aligned_embedding.reshape(base, wide), gain, wp_t, gain2, wm_t
    )

    def over_chips(first, *behind):
        return pl.pallas_call(
            chip_stack_kernel,
            in_specs=vmem(3) + after * len(behind),
            out_shape=shape(chips - 1, *first.shape),
            compiler_params=params(16),
            name="stack_chips",
        )(*[swap(first, "seq", seq_n, 2 * t) for t in range(1, chips)], *behind)

    def over_cores(first, rest):
        return [first, rest, swap(first, "seq", seq_n, 1), swap(rest, "seq", seq_n, 1)]

    columns = [mixed_rows] + [swap(mixed_rows, "res", res_n, t) for t in range(1, res_n)]

    bf = lambda *s: jax.ShapeDtypeStruct(s, BF16)
    q, k, v, m, kt, vt, d_out, sig, n, scale, wj, wb = pl.pallas_call(
        pair_project_kernel,
        out_shape=(
            bf(rows, length, 3 * feats), bf(rows, length, 3 * feats),
            bf(rows, length, 2 * feats), bf(rows, length, 2 * feats),
            bf(rows, 2 * feats, length), bf(rows, 2 * feats, length),
        ) + (shape(rows, length, feats),) * 4
        + (bf(3 * LANES, rows * feats), bf(2, feats, 4 * feats)),
        compiler_params=params(32),
        name="pair_project",
        cost_estimate=pl.CostEstimate(flops=2 * 10**9, bytes_accessed=10**7, transcendentals=0),
    )(
        coupled_embedding, coupled_change_adjoint, gain, coupled_asking_matrix,
        coupled_lookup_matrix, coupled_content_matrix, coupled_sigmoid_matrix,
        coupled_result_matrix, wp_t, gain2, wm_t,
    )

    msa_rest = over_chips(msa_rows, n)
    msa_blocks = over_cores(msa_rows, msa_rest)
    joint = packed(res_n + 2)
    first = pl.pallas_call(
        functools.partial(stack_kernel, length, lines),
        in_specs=vmem(4) + after,
        out_shape=shape(*packed(res_n)),
        compiler_params=params(16),
        name="stack_rows",
    )(*columns, msa_rest)

    wide_gain = aligned_scaler.reshape(1, wide)
    flat = lambda count: shape(n_seqs * count, wide)
    mq, mm, m_out, m_sig, mk, mv, wkv, wqg = pl.pallas_call(
        msa_project_kernel,
        out_shape=(flat(own),) * 4 + (flat(length),) * 2 + (bf(2, wide, 2 * wide),) * 2,
        scratch_shapes=[pltpu.VMEM((n_seqs, length, wide), F32)],
        compiler_params=params(32),
        name="msa_project",
        cost_estimate=pl.CostEstimate(flops=10**9, bytes_accessed=10**7, transcendentals=0),
    )(
        *columns, aligned_change_adjoint, wide_gain, aligned_asking_matrix,
        aligned_lookup_matrix, aligned_content_matrix, aligned_sigmoid_matrix,
        aligned_result_matrix,
    )

    stretch = pltpu.VMEM((hm * own, length), F32)
    o, dq, kept, r1, r23, msa_near, msa_far = pl.pallas_call(
        functools.partial(msa_kernel, (rows, hm, seq_n, res_n)),
        out_shape=(flat(own),) * 4 + (shape(2 * base, wide),)
        + (shape(chips, hm * rows, length),) * 2,
        scratch_shapes=[
            stretch, stretch, pltpu.VMEM((n_seqs, length, wide), F32),
            spread(hm // hp),
        ],
        compiler_params=params(32),
        name="msa_attention",
        cost_estimate=pl.CostEstimate(flops=4 * 10**9, bytes_accessed=10**7, transcendentals=0),
    )(
        mq, mm, mk, mv, *msa_blocks, wkv,
    )
    far_msa = swap(msa_far, "seq", seq_n, 1)
    r23 = swap(r23, "res", res_n, 2)

    blocks = over_cores(first, over_chips(first, kept))

    batch = 6 if rows % 6 == 0 else 1
    piece = lambda *s: pl.BlockSpec((batch,) + s, lambda i: (i, 0, 0))
    whole = lambda *s: pl.BlockSpec(s, lambda i: (0,) * len(s))
    quarter = (chips, res_n, lines, length)
    ot, dqt, dk, dv, near, far = pl.pallas_call(
        functools.partial(pair_kernel, (rows, hp, seq_n, res_n)),
        grid=(rows // batch,),
        in_specs=[
            piece(length, 3 * feats), piece(length, 3 * feats),
            piece(length, 2 * feats), piece(length, 2 * feats),
            piece(2 * feats, length), piece(2 * feats, length),
        ] + [whole(*packed(res_n)), whole(chips - 1, *packed(res_n))] * 2 + after,
        out_specs=(
            piece(HEAD, hp * length), piece(HEAD, hp * length),
            piece(length, feats), piece(length, feats), whole(*quarter), whole(*quarter),
        ),
        out_shape=(
            shape(rows, HEAD, hp * length), shape(rows, HEAD, hp * length),
            shape(rows, length, feats), shape(rows, length, feats),
            shape(*quarter), shape(*quarter),
        ),
        scratch_shapes=[
            pltpu.VMEM((length, hp * length), F32),
            pltpu.VMEM((length, hp * length), F32),
            pltpu.VMEM((hp * length, length), F32),
            spread(res_n),
        ],
        compiler_params=params(32),
        name="pair_attention",
        cost_estimate=pl.CostEstimate(flops=10**10, bytes_accessed=10**7, transcendentals=0),
    )(q, k, v, m, kt, vt, *blocks, kept)
    far_pair = swap(far, "seq", seq_n, 1)
    dn = pl.pallas_call(
        pair_back_kernel,
        out_shape=shape(rows, length, feats),
        compiler_params=params(32),
        name="pair_back",
        cost_estimate=pl.CostEstimate(flops=10**11, bytes_accessed=10**8, transcendentals=0),
    )(
        ot, dqt, dk, dv, d_out, sig, gain, wb,
    )
    sums = pl.pallas_call(
        core_sum_kernel,
        in_specs=vmem(4) + after,
        out_shape=(shape(*joint),) * chips,
        compiler_params=params(16),
        name="core_sum",
    )(near, far_pair, msa_near, far_msa, dn)
    dy = pl.pallas_call(
        aligned_back_kernel,
        out_shape=flat(own),
        compiler_params=params(16),
        name="aligned_back",
        cost_estimate=pl.CostEstimate(flops=10**9, bytes_accessed=10**6, transcendentals=0),
    )(o, dq, m_out, m_sig, wqg, kept)
    c0, mixed_sum, c2, c3, msa_sum = pl.pallas_call(
        chip_sum_kernel,
        in_specs=vmem(6) + after,
        out_shape=(
            shape(lines, length), shape(base + lines, wide), shape(lines, length),
            shape(lines, length), shape(hm * rows, length),
        ),
        compiler_params=params(16),
        name="chip_sum",
    )(sums[0], *[swap(sums[t], "seq", seq_n, 2 * t) for t in range(1, chips)], r1, r23, dy)
    mixed_sum, c2, c3 = [swap(a, "res", res_n, t) for a, t in ((mixed_sum, 1), (c2, 2), (c3, 3))]

    aligned_out = pl.pallas_call(
        aligned_end_kernel,
        out_shape=shape(n_seqs, own, wide),
        compiler_params=params(16),
        name="aligned_end",
    )(mixed_rows, wide_gain, dy, r23, mixed_sum)
    coupled_out = pl.pallas_call(
        pair_end_kernel,
        out_shape=shape(rows, length, feats),
        compiler_params=params(16),
        name="pair_end",
    )(n, scale, dn, c0, mixed_sum, c2, c3, msa_sum, wj)
    return coupled_out, aligned_out


def on_device(seq_n, res_n, *arrays):
    length = arrays[0].shape[1]
    rows = arrays[0].shape[0]
    narrow = length <= arrays[1].shape[2] and HP * length % TILE == 0
    narrow = narrow and rows * (HP + ALIGNED_SPLITS) <= LANES
    narrow = narrow and ALIGNED_SPLITS == 2 * HP and 2 * (length - LANES) == LANES
    if narrow and seq_n == 8 and res_n == 4:
        return fused_on_device(seq_n, res_n, *arrays)
    return scanned_on_device(*arrays)


def solution(mesh):
    in_specs = (
        P(("res", "seq"), None, None),
        P("seq", "res", None),
        P(("res", "seq"), None, None),
        P("seq", "res", None),
        P(),
        P(),
        P(),
        P(),
        P(),
        P(),
        P(),
        P(),
        P(),
        P(),
        P(),
        P(),
        P(),
        P(),
        P(),
    )
    out_specs = (P(("res", "seq"), None, None), P("seq", "res", None))
    return jax.shard_map(
        functools.partial(on_device, mesh.shape["seq"], mesh.shape["res"]),
        mesh=mesh, in_specs=in_specs, out_specs=out_specs, check_vma=False
    )
```

```python
import functools
import math

import jax
import jax.numpy as jnp
from jax import lax
from jax.experimental import pallas as pl
from jax.experimental.pallas import tpu as pltpu
from jax.sharding import PartitionSpec as P

HP = 4
ALIGNED_SPLITS = 8


EXACT_MATMUL = lax.Precision.HIGHEST
EPSILON = 1e-05


def standardize_features(values, norm_gain):
    center = values - jnp.mean(values, axis=-1, keepdims=True)
    spread = jnp.mean(center * center, axis=-1, keepdims=True)
    return center * lax.rsqrt(spread + EPSILON) * norm_gain


def affine_map(values, weight):
    return jnp.einsum("...c,ce->...e", values, weight, precision=EXACT_MATMUL)


def sigmoid_mixing(query_vectors, key_rows, value_rows, gate_preact, softmax_offset, head_count):
    query_shape = query_vectors.shape
    head_width = query_shape[-1] // head_count
    query_heads = query_vectors.reshape(query_shape[:-1] + (head_count, head_width))
    key_heads = key_rows.reshape(key_rows.shape[:-1] + (head_count, head_width))
    value_heads = value_rows.reshape(value_rows.shape[:-1] + (head_count, head_width))
    logits = (
        jnp.einsum("...qhd,...khd->...qhk", query_heads, key_heads, precision=EXACT_MATMUL)
        / math.sqrt(head_width)
        + softmax_offset
    )
    largest = lax.stop_gradient(jnp.max(logits, axis=-1, keepdims=True))
    weights = jnp.exp(logits - largest)
    weights = weights / jnp.sum(weights, axis=-1, keepdims=True)
    mixed_contents = jnp.einsum(
        "...qhk,...khd->...qhd", weights, value_heads, precision=EXACT_MATMUL
    )
    return mixed_contents.reshape(query_shape) * jax.nn.sigmoid(gate_preact)


def scanned_on_device(
    coupled_embedding,
    aligned_embedding,
    coupled_change_adjoint,
    aligned_change_adjoint,
    coupled_scaler,
    coupled_asking_matrix,
    coupled_lookup_matrix,
    coupled_content_matrix,
    coupled_sigmoid_matrix,
    coupled_offset_matrix,
    coupled_result_matrix,
    aligned_scaler,
    coupled_scaler_for_offset,
    aligned_asking_matrix,
    aligned_lookup_matrix,
    aligned_content_matrix,
    aligned_sigmoid_matrix,
    aligned_offset_matrix,
    aligned_result_matrix,
):

    def pair_local(entering_lines):
        standardized_source = standardize_features(entering_lines, coupled_scaler)
        return (
            affine_map(standardized_source, coupled_asking_matrix),
            affine_map(standardized_source, coupled_lookup_matrix),
            affine_map(standardized_source, coupled_content_matrix),
            affine_map(standardized_source, coupled_sigmoid_matrix),
            jnp.einsum(
                "jkc,ch->jhk", standardized_source, coupled_offset_matrix, precision=EXACT_MATMUL
            ),
        )

    (row_queries, row_keys, row_values, row_gates, bias_rows), pair_back = jax.vjp(
        pair_local, coupled_embedding
    )
    by_seq = lax.all_gather(bias_rows, "seq", axis=0, tiled=True)
    full_bias = lax.all_gather(by_seq, "res", axis=0, tiled=True)

    def row_output(one_query, one_key, one_value, one_gate, softmax_offset):
        return affine_map(
            sigmoid_mixing(one_query, one_key, one_value, one_gate, softmax_offset, HP),
            coupled_result_matrix,
        )

    def row_step(bias_sum, row_items):
        one_query, one_key, one_value, one_gate, one_cotan = row_items
        discarded_entry, row_back = jax.vjp(
            row_output, one_query, one_key, one_value, one_gate, full_bias
        )
        grad_query, grad_key, grad_value, grad_gate, grad_bias = row_back(one_cotan)
        return (bias_sum + grad_bias, (grad_query, grad_key, grad_value, grad_gate))

    bias_total, row_grads = lax.scan(
        row_step,
        jnp.zeros_like(full_bias),
        (row_queries, row_keys, row_values, row_gates, coupled_change_adjoint),
    )
    by_res = lax.psum_scatter(bias_total, "res", scatter_dimension=0, tiled=True)
    bias_grad_rows = lax.psum_scatter(by_res, "seq", scatter_dimension=0, tiled=True)
    (mixed_result_sensitivity,) = pair_back(row_grads + (bias_grad_rows,))

    def aligned_offset_portion(entering_lines):
        return jnp.einsum(
            "gys,sj->gjy",
            standardize_features(entering_lines, coupled_scaler_for_offset),
            aligned_offset_matrix,
            precision=EXACT_MATMUL,
        )

    aligned_offset_part, aligned_offset_reverse = jax.vjp(aligned_offset_portion, coupled_embedding)
    tile_softmax_offset = lax.all_gather(aligned_offset_part, "seq", axis=0, tiled=True)

    def sequence_output(query_vectors, full_key_rows, full_value_rows, gate_preact, softmax_offset):
        return affine_map(
            sigmoid_mixing(
                query_vectors,
                full_key_rows,
                full_value_rows,
                gate_preact,
                softmax_offset,
                ALIGNED_SPLITS,
            ),
            aligned_result_matrix,
        )

    state_all = lax.all_gather(aligned_embedding, "res", axis=1, tiled=True)

    def near_local(carry_pile):
        standardized_source = standardize_features(carry_pile, aligned_scaler)
        return (
            affine_map(standardized_source, aligned_asking_matrix),
            affine_map(standardized_source, aligned_sigmoid_matrix),
        )

    def keys_local(carry_pile):
        standardized_source = standardize_features(carry_pile, aligned_scaler)
        return (
            affine_map(standardized_source, aligned_lookup_matrix),
            affine_map(standardized_source, aligned_content_matrix),
        )

    (aligned_asking_lines, aligned_sigmoid_factors), near_back = jax.vjp(
        near_local, aligned_embedding
    )
    (full_key_rows, full_value_rows), keys_back = jax.vjp(keys_local, state_all)
    discarded_entry, sigmoid_mixing_reverse = jax.vjp(
        sequence_output,
        aligned_asking_lines,
        full_key_rows,
        full_value_rows,
        aligned_sigmoid_factors,
        tile_softmax_offset,
    )
    query_gradient, full_key_gradient, full_value_gradient, gate_gradient, block_bias_gradient = (
        sigmoid_mixing_reverse(aligned_change_adjoint)
    )
    (state_term,) = keys_back((full_key_gradient, full_value_gradient))
    spread_grad = lax.psum_scatter(state_term, "res", scatter_dimension=1, tiled=True)
    (near_grad,) = near_back((query_gradient, gate_gradient))
    aligned_embedding_sensitivity = near_grad + spread_grad
    offset_line_sensitivity = lax.psum_scatter(
        block_bias_gradient, "seq", scatter_dimension=0, tiled=True
    )
    (coupled_sensitivity_via_offset,) = aligned_offset_reverse(offset_line_sensitivity)
    return (
        mixed_result_sensitivity + coupled_sensitivity_via_offset,
        aligned_embedding_sensitivity,
    )


F32 = jnp.float32
BF16 = jnp.bfloat16
HEAD = 32
LANES = 128
TILE = 256


def split2(a):
    top = a.astype(BF16)
    return top, (a - top.astype(F32)).astype(BF16)


def split3(a):
    top = a.astype(BF16)
    rest = a - top.astype(F32)
    mid = rest.astype(BF16)
    return top, mid, (rest - mid.astype(F32)).astype(BF16)


def left6(parts):
    a, b, c = parts
    return [a, a, b, b, a, c]


def right6(parts):
    a, b, c = parts
    return [a, b, a, b, c, a]


def left3(parts):
    return [parts[0], parts[0], parts[1]]


def right3(parts):
    return [parts[0], parts[1], parts[0]]


def nn(a, b):
    return lax.dot_general(a, b, (((1,), (0,)), ((), ())), preferred_element_type=F32)


def nt(a, b):
    return lax.dot_general(a, b, (((1,), (1,)), ((), ())), preferred_element_type=F32)


def cat(parts, axis):
    return jnp.concatenate(parts, axis=axis)


def normed(v):
    center = v - jnp.mean(v, axis=-1, keepdims=True)
    spread = jnp.mean(center * center, axis=-1, keepdims=True)
    scale = lax.rsqrt(spread + EPSILON)
    return center * scale, scale


def normed_back(n, scale, dn):
    return scale * (
        dn - jnp.mean(dn, axis=-1, keepdims=True) - n * jnp.mean(dn * n, axis=-1, keepdims=True)
    )


def head_mask(h, dtype):
    lane = lax.broadcasted_iota(jnp.int32, (1, LANES), 1)
    return jnp.where((lane // HEAD) == h, 1.0, 0.0).astype(dtype)


def pack(block_of, count, lines, out_ref):
    half = count // 2
    for t in range(half):
        first, second = block_of(t), block_of(t + half)
        out_ref[t * lines : (t + 1) * lines] = first[:, :LANES]
        out_ref[(t + half) * lines : (t + half + 1) * lines] = second[:, :LANES]
        rest = cat([first[:, LANES:], second[:, LANES:]], 1)
        out_ref[(t + count) * lines : (t + count + 1) * lines] = rest


def unpack(dense, count, lines):
    half = count // 2
    blocks = []
    for t in range(count):
        rest = dense[(count + t % half) * lines : (count + t % half + 1) * lines]
        rest = rest[:, : LANES // 2] if t < half else rest[:, LANES // 2 :]
        blocks.append(cat([dense[t * lines : (t + 1) * lines], rest], 1))
    return blocks


def bias_kernel(rows, x_ref, y_ref, g_ref, wp_ref, g2_ref, wm_ref, joint_ref, packed_ref, bm_ref):
    length = x_ref.shape[1]
    base, wide = y_ref.shape
    joint_ref[:base] = y_ref[...]
    if length < wide:
        joint_ref[base:, length:] = jnp.zeros((wp_ref.shape[0] * rows, wide - length), F32)
    hp, hm = wp_ref.shape[0], wm_ref.shape[0]
    w = cat([wp_ref[...] * g_ref[...], wm_ref[...] * g2_ref[...]], 0)
    wcat = cat(left6(split3(w)), 1)
    for j in range(rows):
        n, _ = normed(x_ref[j])
        res = nt(wcat, cat(right6(split3(n)), 1))
        for h in range(hp):
            at = base + h * rows + j
            joint_ref[at : at + 1, :length] = res[h : h + 1]
        for h in range(hm):
            bm_ref[h * rows + j : h * rows + j + 1, :] = res[hp + h : hp + h + 1]
    lines = hp * rows
    pack(lambda t: bm_ref[t * lines : (t + 1) * lines], hm // hp, lines, packed_ref)


def pair_project_kernel(
    x_ref, adj_ref, g_ref, wq_ref, wk_ref, wv_ref, wg_ref, wo_ref, wp_ref, g2_ref, wm_ref,
    q_ref, k_ref, v_ref, m_ref, kt_ref, vt_ref, dout_ref, sig_ref, n_ref, scale_ref, wj_ref, wb_ref,
):
    rows, length, feats = x_ref.shape
    g = g_ref[...]
    top, low = split2(cat([wq_ref[...], wk_ref[...], wv_ref[...], wg_ref[...]], 1))
    wb_ref[0] = top
    wb_ref[1] = low
    w6 = cat(right6(split3(cat([wq_ref[...], wk_ref[...]], 1))), 0)
    w3 = cat(right3(split2(cat([wv_ref[...], wg_ref[...]], 1))), 0)
    wo3 = cat(right3(split2(wo_ref[...])), 1)
    for i in range(rows):
        n, scale = normed(x_ref[i])
        n_ref[i] = n
        scale_ref[i] = jnp.broadcast_to(scale, n.shape)
        parts = split3(n * g)
        qk = nn(cat(left6(parts), 1), w6)
        vg = nn(cat(left3(parts), 1), w3)
        d_out = nt(cat(left3(split2(adj_ref[i])), 1), wo3)
        sig = jax.nn.sigmoid(vg[:, feats:])
        dout_ref[i] = d_out
        sig_ref[i] = sig
        q, k, v = qk[:, :feats] * (1.0 / math.sqrt(HEAD)), qk[:, feats:], vg[:, :feats]
        q_ref[i] = cat(split3(q), 1)
        k_ref[i] = cat(split3(k), 1)
        v_ref[i] = cat(split2(v), 1)
        m_ref[i] = cat(split2(d_out * sig), 1)
        kt_ref[i] = cat(split2(k.T), 0)
        vt_ref[i] = cat(split2(v.T), 0)
    hp, hm = wp_ref.shape[0], wm_ref.shape[0]
    w = cat([wp_ref[...] * g, wm_ref[...] * g2_ref[...]], 0)
    lines = [jnp.broadcast_to(w[h : h + 1], (rows, feats)) for h in range(hp + hm)]
    lines += [jnp.zeros((LANES - rows * (hp + hm), feats), F32)]
    spread = cat(lines, 0)
    at = lax.broadcasted_iota(jnp.int32, (LANES, 1), 0)
    for j in range(rows):
        mine = jnp.where(lax.rem(at, rows) == j, spread, 0.0)
        wj_ref[:, j * feats : (j + 1) * feats] = cat(right3(split2(mine)), 0)


def gather_chips(natural, refs, core, chip):
    _, count, lines, _ = natural.shape
    for (own_ref, others_ref), side in zip((refs[:2], refs[2:]), (core, 1 - core)):
        for t in range(others_ref.shape[0] + 1):
            at = lax.bitwise_xor(chip, t) * 2 + side
            dense = others_ref[t - 1] if t > 0 else own_ref[...]
            for i, block in enumerate(unpack(dense, count, lines)):
                natural[at, i] = block


def pair_kernel(
    dims,
    q_ref, k_ref, v_ref, m_ref, kt_ref, vt_ref,
    b0_ref, b1_ref, b2_ref, b3_ref,
    after_ref,
    ot_ref, dqt_ref, dk_ref, dv_ref, near_ref, far_ref,
    bt, dbt, stack, natural,
):
    rows, heads, seq_n, res_n = dims
    step = pl.program_id(0)
    seq, res = lax.axis_index("seq"), lax.axis_index("res")
    core, chip = lax.rem(seq, 2), lax.div(seq, 2)
    n_keys = q_ref.shape[1]

    @pl.when(step == 0)
    def _():
        blocks = (b0_ref, b1_ref, b2_ref, b3_ref)
        gather_chips(natural, blocks, core, chip)
        for z in range(res_n):
            zi = lax.bitwise_xor(res, z)
            for s in range(seq_n):
                block = natural[s, zi]
                d = z * seq_n + s
                for h in range(heads):
                    at = h * n_keys + d * rows
                    stack[at : at + rows, :] = block[h * rows : (h + 1) * rows]
        bt[...] = stack[...].T
        dbt[...] = jnp.zeros_like(dbt)

    def pieces(ref, u, count):
        return [ref[u, :, t * LANES : (t + 1) * LANES] for t in range(count)]

    masks = [head_mask(h, BF16) for h in range(heads)]
    tiles = heads * n_keys // TILE
    batch = q_ref.shape[0]

    def operands(u):
        qs = [cat([a * mask for mask in masks], 0) for a in pieces(q_ref, u, 3)]
        ms = [cat([a * mask for mask in masks], 0) for a in pieces(m_ref, u, 2)]
        kcat = cat(left6(pieces(k_ref, u, 3)), 1)
        vcat = cat(left3(pieces(v_ref, u, 2)), 1)
        return qs, ms, kcat, vcat

    rows_in = {}

    def logits(item):
        u, c = divmod(item, tiles)
        if u not in rows_in:
            rows_in[u] = operands(u)
        qs, ms, kcat, vcat = rows_in[u]
        cols = slice(c * TILE, (c + 1) * TILE)
        qc, mc = [a[cols] for a in qs], [a[cols] for a in ms]
        s = nt(kcat, cat(right6(qc), 1)) + bt[:, cols]
        return s, nt(vcat, cat(right3(mc), 1)), qc, mc

    def weights(item, s, dp):
        c = item % tiles
        cols = slice(c * TILE, (c + 1) * TILE)
        e = jnp.exp(s - jnp.max(s, axis=0, keepdims=True))
        p = e * (1.0 / jnp.sum(e, axis=0, keepdims=True))
        ds = p * (dp - jnp.sum(p * dp, axis=0, keepdims=True))
        dbt[:, cols] = dbt[:, cols] + ds
        return split2(p) + split2(ds)

    sums = {}

    def products(item, p1, p2, s1, s2, qc, mc):
        u, c = divmod(item, tiles)
        cols = slice(c * TILE, (c + 1) * TILE)
        first, last = c * TILE // n_keys, ((c + 1) * TILE - 1) // n_keys
        lane = lax.broadcasted_iota(jnp.int32, (1, TILE), 1) + c * TILE

        def of_heads(ref, a1, a2):
            top = ref[u, first * HEAD : (last + 1) * HEAD]
            low = ref[u, LANES + first * HEAD : LANES + (last + 1) * HEAD]
            both = nn(cat([top, low], 0), a1)
            half = both.shape[0] // 2
            total = both[:half] + both[half:] + nn(top, a2)
            picked = total[:HEAD]
            for h in range(first + 1, last + 1):
                rest = total[(h - first) * HEAD : (h - first + 1) * HEAD]
                picked = jnp.where(lane >= h * n_keys, rest, picked)
            return picked

        ot_ref[u, :, cols] = of_heads(vt_ref, p1, p2)
        dqt_ref[u, :, cols] = of_heads(kt_ref, s1, s2)
        both = nn(s1, cat(qc[:2], 1))
        dk = both[:, :LANES] + both[:, LANES:] + nn(s2, qc[0])
        both = nn(p1, cat(mc, 1))
        dv = both[:, :LANES] + both[:, LANES:] + nn(p2, mc[0])
        if c > 0:
            dk, dv = sums[u][0] + dk, sums[u][1] + dv
        sums[u] = (dk, dv)
        if c == tiles - 1:
            dk_ref[u] = dk
            dv_ref[u] = dv

    count = batch * tiles
    ready, waiting = {}, {}
    for item in range(-1, count + 1):
        if 0 <= item + 1 < count:
            ready[item + 1] = logits(item + 1)
        if 0 <= item < count:
            s, dp, qc, mc = ready.pop(item)
            waiting[item] = weights(item, s, dp) + (qc, mc)
        if 0 <= item - 1 < count:
            products(item - 1, *waiting.pop(item - 1))

    @pl.when(step == pl.num_programs(0) - 1)
    def _():
        stack[...] = dbt[...].T
        for z in range(res_n):
            zi = lax.bitwise_xor(res, z)
            for pair in range(seq_n // 2):
                ci = lax.bitwise_xor(chip, pair)
                blocks = []
                for s in (2 * pair, 2 * pair + 1):
                    at = [h * n_keys + (z * seq_n + s) * rows for h in range(heads)]
                    blocks.append(cat([stack[a : a + rows, :] for a in at], 0))
                near_ref[ci, zi] = jnp.where(core == 0, blocks[0], blocks[1])
                far_ref[ci, zi] = jnp.where(core == 0, blocks[1], blocks[0])


def pair_back_kernel(
    ot_ref, dqt_ref, dk_ref, dv_ref, dout_ref, sig_ref,
    g_ref, wb_ref, dn_ref,
):
    rows, length, feats = dk_ref.shape
    g = g_ref[...]
    w1, w2 = wb_ref[0], wb_ref[1]

    def lines(flat):
        heads = flat.shape[1] // length
        return cat([flat[:, h * length : (h + 1) * length] for h in range(heads)], 0).T

    for i in range(rows):
        o, sig = lines(ot_ref[i]), sig_ref[i]
        d_gate = dout_ref[i] * o * sig * (1.0 - sig)
        dq = lines(dqt_ref[i]) * (1.0 / math.sqrt(HEAD))
        t1, t2 = split2(cat([dq, dk_ref[i], dv_ref[i], d_gate], 1))
        dn_ref[i] = g * (nt(t1, w1) + nt(t1, w2) + nt(t2, w1))


def msa_project_kernel(
    y0_ref, y1_ref, y2_ref, y3_ref, adj_ref,
    g_ref, wq_ref, wk_ref, wv_ref, wg_ref, wo_ref,
    q_ref, m_ref, dout_ref, sig_ref, k_ref, v_ref, wkv_ref, wqg_ref,
    yall,
):
    res = lax.axis_index("res")
    n_seqs, own, feats = adj_ref.shape
    n_keys = yall.shape[1]
    g = g_ref[...]
    for t, ref in enumerate((y0_ref, y1_ref, y2_ref, y3_ref)):
        at = pl.multiple_of(lax.bitwise_xor(res, t) * own, own)
        for b in range(n_seqs):
            yall[b, pl.ds(at, own), :] = ref[b * own : (b + 1) * own, :]
    n_own, _ = normed(y0_ref[: n_seqs * own])
    n_all, _ = normed(yall[...].reshape(n_seqs * n_keys, feats))
    own_parts, all_parts = split3(n_own * g), split3(n_all * g)
    for ref, pair in ((wkv_ref, (wk_ref, wv_ref)), (wqg_ref, (wq_ref, wg_ref))):
        top, low = split2(cat([pair[0][...], pair[1][...]], 1))
        ref[0] = top
        ref[1] = low
    q = nn(cat(left6(own_parts), 1), cat(right6(split3(wq_ref[...])), 0))
    gate = nn(cat(left3(own_parts), 1), cat(right3(split2(wg_ref[...])), 0))
    k = nn(cat(left6(all_parts), 1), cat(right6(split3(wk_ref[...])), 0))
    v = nn(cat(left3(all_parts), 1), cat(right3(split2(wv_ref[...])), 0))
    adj = adj_ref[...].reshape(n_seqs * own, feats)
    d_out = nt(cat(left3(split2(adj)), 1), cat(right3(split2(wo_ref[...])), 1))
    sig = jax.nn.sigmoid(gate)
    q_ref[...] = q * (1.0 / math.sqrt(HEAD))
    m_ref[...] = d_out * sig
    dout_ref[...] = d_out
    sig_ref[...] = sig
    k_ref[...] = k
    v_ref[...] = v


def msa_kernel(
    dims,
    q_ref, m_ref, k_ref, v_ref,
    b0_ref, b1_ref, b2_ref, b3_ref,
    wkv_ref,
    o_ref, dq_ref, r0_ref, r1_ref, r23_ref, near_ref, far_ref,
    bias, dbias, dyall, natural,
):
    rows, heads, seq_n, res_n = dims
    seq, res = lax.axis_index("seq"), lax.axis_index("res")
    core, chip = lax.rem(seq, 2), lax.div(seq, 2)
    n_seqs, n_keys, feats = dyall.shape
    own = n_keys // res_n
    tiles, group = feats // LANES, LANES // HEAD
    blocks = (b0_ref, b1_ref, b2_ref, b3_ref)
    gather_chips(natural, blocks, core, chip)
    for s in range(seq_n):
        block = cat([natural[s, 0], natural[s, 1]], 0)
        for h in range(heads):
            at = h * own + s * rows
            bias[at : at + rows, :] = block[h * rows : (h + 1) * rows]
    masks = [head_mask(u, BF16) for u in range(group)]
    fmasks = [head_mask(u, F32) for u in range(group)]

    def stacked(a, by):
        return cat([a * mask for mask in by], 0)

    def own_rows(full):
        total = fmasks[0] * full[:own]
        for u in range(1, group):
            total = total + fmasks[u] * full[u * own : (u + 1) * own]
        return total

    b1, b2 = wkv_ref[0], wkv_ref[1]

    def spans(item):
        b, t = divmod(item, tiles)
        near = slice(b * own, (b + 1) * own)
        wide = slice(b * n_keys, (b + 1) * n_keys)
        cols = slice(t * LANES, (t + 1) * LANES)
        return b, near, wide, cols, slice(t * group * own, (t + 1) * group * own)

    def logits(item):
        b, near, wide, cols, lines = spans(item)
        qs = [stacked(a, masks) for a in split3(q_ref[near, cols])]
        ms = [stacked(a, masks) for a in split2(m_ref[near, cols])]
        kp = split3(k_ref[wide, cols])
        vp = split2(v_ref[wide, cols])
        s = nt(cat(left6(qs), 1), cat(right6(kp), 1)) + bias[lines]
        return s, nt(cat(left3(ms), 1), cat(right3(vp), 1)), kp, vp

    def weights(item, s, dp):
        b, near, wide, cols, lines = spans(item)
        e = jnp.exp(s - jnp.max(s, axis=1, keepdims=True))
        p = e * (1.0 / jnp.sum(e, axis=1, keepdims=True))
        ds = p * (dp - jnp.sum(p * dp, axis=1, keepdims=True))
        dbias[lines] = ds if b == 0 else dbias[lines] + ds
        return split2(p) + split2(ds)

    turned = {}

    def products(item, p1, p2, s1, s2, kp, vp):
        b, near, wide, cols, lines = spans(item)
        qt1, qt2 = split2(stacked(q_ref[near, cols], fmasks).T)
        mt1, mt2 = split2(stacked(m_ref[near, cols], fmasks).T)
        both = nn(p1, cat(vp, 1))
        o_ref[near, cols] = own_rows(both[:, :LANES] + both[:, LANES:] + nn(p2, vp[0]))
        both = nn(s1, cat(kp[:2], 1))
        dq_ref[near, cols] = own_rows(both[:, :LANES] + both[:, LANES:] + nn(s2, kp[0]))
        both = nn(cat([qt1, qt2], 0), s1)
        dkt = both[:LANES] + both[LANES:] + nn(qt1, s2)
        both = nn(cat([mt1, mt2], 0), p1)
        dvt = both[:LANES] + both[LANES:] + nn(mt1, p2)
        turned.setdefault(b, []).append((dkt, dvt))
        if len(turned[b]) == tiles:
            flat = [a[0].T for a in turned[b]] + [a[1].T for a in turned[b]]
            t1, t2 = split2(cat(flat, 1))
            dyall[b] = nt(t1, b1) + nt(t1, b2) + nt(t2, b1)

    count = n_seqs * tiles
    ready, waiting = {}, {}
    for item in range(-1, count + 1):
        if 0 <= item + 1 < count:
            ready[item + 1] = logits(item + 1)
        if 0 <= item < count:
            s, dp, kp, vp = ready.pop(item)
            waiting[item] = weights(item, s, dp) + (kp, vp)
        if 0 <= item - 1 < count:
            products(item - 1, *waiting.pop(item - 1))
    for t, (ref, base) in enumerate(((r0_ref, 0), (r1_ref, 0), (r23_ref, 0), (r23_ref, n_seqs))):
        at = pl.multiple_of(lax.bitwise_xor(res, t) * own, own)
        for b in range(n_seqs):
            to = (base + b) * own
            ref[to : to + own, :] = dyall[b, pl.ds(at, own), :]
    for pair in range(seq_n // 2):
        ci = lax.bitwise_xor(chip, pair)
        blocks = []
        for s in (2 * pair, 2 * pair + 1):
            at = [h * own + s * rows for h in range(heads)]
            blocks.append(cat([dbias[a : a + rows, :] for a in at], 0))
        near_ref[ci] = jnp.where(core == 0, blocks[0], blocks[1])
        far_ref[ci] = jnp.where(core == 0, blocks[1], blocks[0])


def aligned_back_kernel(o_ref, dq_ref, dout_ref, sig_ref, wqg_ref, r0_ref, dy_ref):
    sig = sig_ref[...]
    d_gate = dout_ref[...] * o_ref[...] * sig * (1.0 - sig)
    t1, t2 = split2(cat([dq_ref[...] * (1.0 / math.sqrt(HEAD)), d_gate], 1))
    b1, b2 = wqg_ref[0], wqg_ref[1]
    dy_ref[...] = nt(t1, b1) + nt(t1, b2) + nt(t2, b1) + r0_ref[...]


def aligned_end_kernel(y_ref, g_ref, dy_ref, r23_ref, r1_ref, out_ref):
    n_seqs, own, _ = out_ref.shape
    g = g_ref[...]
    for b in range(n_seqs):
        at = slice(b * own, (b + 1) * own)
        n, scale = normed(y_ref[at])
        out_ref[b] = normed_back(n, scale, g * (dy_ref[at] + r23_ref[at] + r1_ref[at]))


def stack_kernel(length, lines, p0_ref, p1_ref, p2_ref, p3_ref, after_ref, out_ref):
    blocks = [ref[ref.shape[0] - lines :, :length] for ref in (p0_ref, p1_ref, p2_ref, p3_ref)]
    pack(lambda t: blocks[t], len(blocks), lines, out_ref)


def chip_stack_kernel(b1_ref, b2_ref, b3_ref, after_ref, out_ref):
    for t, ref in enumerate((b1_ref, b2_ref, b3_ref)):
        out_ref[t] = ref[...]


def core_sum_kernel(p0_ref, p1_ref, m0_ref, m1_ref, after_ref, s0_ref, s1_ref, s2_ref, s3_ref):
    res_n, lines = p0_ref.shape[1:3]
    for t, ref in enumerate((s0_ref, s1_ref, s2_ref, s3_ref)):
        pair = p0_ref[t] + p1_ref[t]
        msa = m0_ref[t] + m1_ref[t]
        blocks = [pair[z] for z in range(res_n)] + [msa[:lines], msa[lines:]]
        pack(lambda i: blocks[i], len(blocks), lines, ref)


def chip_sum_kernel(
    s0_ref, s1_ref, s2_ref, s3_ref, r1_ref, r23_ref, after_ref,
    c0_ref, joint_ref, c2_ref, c3_ref, m_ref,
):
    lines, length = c0_ref.shape
    base = r1_ref.shape[0]
    joint_ref[:base] = r1_ref[...] + r23_ref[base:]
    if length < joint_ref.shape[1]:
        joint_ref[base:, length:] = jnp.zeros((lines, joint_ref.shape[1] - length), F32)
    total = s0_ref[...] + s1_ref[...] + s2_ref[...] + s3_ref[...]
    blocks = unpack(total, 2 * total.shape[0] // (3 * lines), lines)
    for t, ref in enumerate((c0_ref, joint_ref, c2_ref, c3_ref)):
        if t == 1:
            ref[base:, :length] = blocks[t]
        else:
            ref[...] = blocks[t]
    m_ref[:lines] = blocks[-2]
    m_ref[lines:] = blocks[-1]


def pair_end_kernel(
    n_ref, scale_ref, dn_ref, p0_ref, p1_ref, p2_ref, p3_ref, m_ref, wj_ref, out_hbm, out_ref, sem
):
    rows, length, feats = n_ref.shape
    lines = p0_ref.shape[0]
    pair = p0_ref[...] + p2_ref[...] + p3_ref[...]
    pair = pair + p1_ref[p1_ref.shape[0] - lines :, :length]
    msa = m_ref[...]
    pad = jnp.zeros((LANES - pair.shape[0] - msa.shape[0], length), F32)
    b = cat([pair, msa, pad], 0).T
    more = nn(cat(left3(split2(b)), 1), wj_ref[...])
    copies = []
    for j in range(rows):
        dn = dn_ref[j] + more[:, j * feats : (j + 1) * feats]
        out_ref[j] = normed_back(n_ref[j], scale_ref[j], dn)
        if j % 2 == 1 or j == rows - 1:
            span = pl.ds(j - j % 2, j % 2 + 1)
            copies.append(pltpu.make_async_copy(out_ref.at[span], out_hbm.at[span], sem.at[j // 2]))
            copies[-1].start()
    for copy in copies:
        copy.wait()


MIB = 1 << 20


def params(mib, **more):
    return pltpu.CompilerParams(vmem_limit_bytes=mib * MIB, **more)


def vmem(count):
    return [pl.BlockSpec(memory_space=pltpu.VMEM)] * count


def swap(values, axis, size, offset):
    return lax.ppermute(values, axis, [(i, i ^ offset) for i in range(size)])


def fused_on_device(
    seq_n,
    res_n,
    coupled_embedding,
    aligned_embedding,
    coupled_change_adjoint,
    aligned_change_adjoint,
    coupled_scaler,
    coupled_asking_matrix,
    coupled_lookup_matrix,
    coupled_content_matrix,
    coupled_sigmoid_matrix,
    coupled_offset_matrix,
    coupled_result_matrix,
    aligned_scaler,
    coupled_scaler_for_offset,
    aligned_asking_matrix,
    aligned_lookup_matrix,
    aligned_content_matrix,
    aligned_sigmoid_matrix,
    aligned_offset_matrix,
    aligned_result_matrix,
):
    rows, length, feats = coupled_embedding.shape
    n_seqs, own, wide = aligned_embedding.shape
    hp, hm = HP, ALIGNED_SPLITS
    chips = seq_n // 2
    shape = lambda *s: jax.ShapeDtypeStruct(s, F32)
    wp_t, wm_t = coupled_offset_matrix.T, aligned_offset_matrix.T
    gain = coupled_scaler.reshape(1, feats)
    gain2 = coupled_scaler_for_offset.reshape(1, feats)

    lines, base = hp * rows, n_seqs * own
    after = [pl.BlockSpec(memory_space=pl.ANY)]
    packed = lambda count: (3 * count * lines // 2, LANES)
    spread = lambda count: pltpu.VMEM((seq_n, count, lines, length), F32)
    mixed_rows, msa_rows = pl.pallas_call(
        functools.partial(bias_kernel, rows),
        out_shape=(shape(base + lines, wide), shape(*packed(2))),
        scratch_shapes=[pltpu.VMEM((hm * rows, length), F32)],
        compiler_params=params(63),
        name="bias_rows",
    )(
        coupled_embedding, aligned_embedding.reshape(base, wide), gain, wp_t, gain2, wm_t
    )

    def over_chips(first, *behind):
        return pl.pallas_call(
            chip_stack_kernel,
            in_specs=vmem(3) + after * len(behind),
            out_shape=shape(chips - 1, *first.shape),
            compiler_params=params(16),
            name="stack_chips",
        )(*[swap(first, "seq", seq_n, 2 * t) for t in range(1, chips)], *behind)

    def over_cores(first, rest):
        return [first, rest, swap(first, "seq", seq_n, 1), swap(rest, "seq", seq_n, 1)]

    columns = [mixed_rows] + [swap(mixed_rows, "res", res_n, t) for t in range(1, res_n)]

    bf = lambda *s: jax.ShapeDtypeStruct(s, BF16)
    q, k, v, m, kt, vt, d_out, sig, n, scale, wj, wb = pl.pallas_call(
        pair_project_kernel,
        out_shape=(
            bf(rows, length, 3 * feats), bf(rows, length, 3 * feats),
            bf(rows, length, 2 * feats), bf(rows, length, 2 * feats),
            bf(rows, 2 * feats, length), bf(rows, 2 * feats, length),
        ) + (shape(rows, length, feats),) * 4
        + (bf(3 * LANES, rows * feats), bf(2, feats, 4 * feats)),
        compiler_params=params(32),
        name="pair_project",
        cost_estimate=pl.CostEstimate(flops=2 * 10**9, bytes_accessed=10**7, transcendentals=0),
    )(
        coupled_embedding, coupled_change_adjoint, gain, coupled_asking_matrix,
        coupled_lookup_matrix, coupled_content_matrix, coupled_sigmoid_matrix,
        coupled_result_matrix, wp_t, gain2, wm_t,
    )

    msa_rest = over_chips(msa_rows, n)
    msa_blocks = over_cores(msa_rows, msa_rest)
    joint = packed(res_n + 2)
    first = pl.pallas_call(
        functools.partial(stack_kernel, length, lines),
        in_specs=vmem(4) + after,
        out_shape=shape(*packed(res_n)),
        compiler_params=params(16),
        name="stack_rows",
    )(*columns, msa_rest)

    wide_gain = aligned_scaler.reshape(1, wide)
    flat = lambda count: shape(n_seqs * count, wide)
    mq, mm, m_out, m_sig, mk, mv, wkv, wqg = pl.pallas_call(
        msa_project_kernel,
        out_shape=(flat(own),) * 4 + (flat(length),) * 2 + (bf(2, wide, 2 * wide),) * 2,
        scratch_shapes=[pltpu.VMEM((n_seqs, length, wide), F32)],
        compiler_params=params(32),
        name="msa_project",
        cost_estimate=pl.CostEstimate(flops=10**9, bytes_accessed=10**7, transcendentals=0),
    )(
        *columns, aligned_change_adjoint, wide_gain, aligned_asking_matrix,
        aligned_lookup_matrix, aligned_content_matrix, aligned_sigmoid_matrix,
        aligned_result_matrix,
    )

    stretch = pltpu.VMEM((hm * own, length), F32)
    o, dq, kept, r1, r23, msa_near, msa_far = pl.pallas_call(
        functools.partial(msa_kernel, (rows, hm, seq_n, res_n)),
        out_shape=(flat(own),) * 4 + (shape(2 * base, wide),)
        + (shape(chips, hm * rows, length),) * 2,
        scratch_shapes=[
            stretch, stretch, pltpu.VMEM((n_seqs, length, wide), F32),
            spread(hm // hp),
        ],
        compiler_params=params(32),
        name="msa_attention",
        cost_estimate=pl.CostEstimate(flops=4 * 10**9, bytes_accessed=10**7, transcendentals=0),
    )(
        mq, mm, mk, mv, *msa_blocks, wkv,
    )
    far_msa = swap(msa_far, "seq", seq_n, 1)
    r23 = swap(r23, "res", res_n, 2)

    blocks = over_cores(first, over_chips(first, kept))

    batch = 6 if rows % 6 == 0 else 1
    piece = lambda *s: pl.BlockSpec((batch,) + s, lambda i: (i, 0, 0))
    whole = lambda *s: pl.BlockSpec(s, lambda i: (0,) * len(s))
    quarter = (chips, res_n, lines, length)
    ot, dqt, dk, dv, near, far = pl.pallas_call(
        functools.partial(pair_kernel, (rows, hp, seq_n, res_n)),
        grid=(rows // batch,),
        in_specs=[
            piece(length, 3 * feats), piece(length, 3 * feats),
            piece(length, 2 * feats), piece(length, 2 * feats),
            piece(2 * feats, length), piece(2 * feats, length),
        ] + [whole(*packed(res_n)), whole(chips - 1, *packed(res_n))] * 2 + after,
        out_specs=(
            piece(HEAD, hp * length), piece(HEAD, hp * length),
            piece(length, feats), piece(length, feats), whole(*quarter), whole(*quarter),
        ),
        out_shape=(
            shape(rows, HEAD, hp * length), shape(rows, HEAD, hp * length),
            shape(rows, length, feats), shape(rows, length, feats),
            shape(*quarter), shape(*quarter),
        ),
        scratch_shapes=[
            pltpu.VMEM((length, hp * length), F32),
            pltpu.VMEM((length, hp * length), F32),
            pltpu.VMEM((hp * length, length), F32),
            spread(res_n),
        ],
        compiler_params=params(32),
        name="pair_attention",
        cost_estimate=pl.CostEstimate(flops=10**10, bytes_accessed=10**7, transcendentals=0),
    )(q, k, v, m, kt, vt, *blocks, kept)
    far_pair = swap(far, "seq", seq_n, 1)
    dn = pl.pallas_call(
        pair_back_kernel,
        out_shape=shape(rows, length, feats),
        compiler_params=params(32),
        name="pair_back",
        cost_estimate=pl.CostEstimate(flops=10**11, bytes_accessed=10**8, transcendentals=0),
    )(
        ot, dqt, dk, dv, d_out, sig, gain, wb,
    )
    sums = pl.pallas_call(
        core_sum_kernel,
        in_specs=vmem(4) + after,
        out_shape=(shape(*joint),) * chips,
        compiler_params=params(16),
        name="core_sum",
    )(near, far_pair, msa_near, far_msa, dn)
    dy = pl.pallas_call(
        aligned_back_kernel,
        out_shape=flat(own),
        compiler_params=params(16),
        name="aligned_back",
        cost_estimate=pl.CostEstimate(flops=10**9, bytes_accessed=10**6, transcendentals=0),
    )(o, dq, m_out, m_sig, wqg, kept)
    c0, mixed_sum, c2, c3, msa_sum = pl.pallas_call(
        chip_sum_kernel,
        in_specs=vmem(6) + after,
        out_shape=(
            shape(lines, length), shape(base + lines, wide), shape(lines, length),
            shape(lines, length), shape(hm * rows, length),
        ),
        compiler_params=params(16),
        name="chip_sum",
    )(sums[0], *[swap(sums[t], "seq", seq_n, 2 * t) for t in range(1, chips)], r1, r23, dy)
    mixed_sum, c2, c3 = [swap(a, "res", res_n, t) for a, t in ((mixed_sum, 1), (c2, 2), (c3, 3))]

    aligned_out = pl.pallas_call(
        aligned_end_kernel,
        out_shape=shape(n_seqs, own, wide),
        compiler_params=params(16),
        name="aligned_end",
    )(mixed_rows, wide_gain, dy, r23, mixed_sum)
    coupled_out = pl.pallas_call(
        pair_end_kernel,
        in_specs=vmem(9),
        out_specs=pl.BlockSpec(memory_space=pl.ANY),
        out_shape=shape(rows, length, feats),
        scratch_shapes=[
            pltpu.VMEM((rows, length, feats), F32), pltpu.SemaphoreType.DMA((-(-rows // 2),)),
        ],
        compiler_params=params(16),
        name="pair_end",
    )(n, scale, dn, c0, mixed_sum, c2, c3, msa_sum, wj)
    return coupled_out, aligned_out


def on_device(seq_n, res_n, *arrays):
    length = arrays[0].shape[1]
    rows = arrays[0].shape[0]
    narrow = length <= arrays[1].shape[2] and HP * length % TILE == 0
    narrow = narrow and rows * (HP + ALIGNED_SPLITS) <= LANES
    narrow = narrow and ALIGNED_SPLITS == 2 * HP and 2 * (length - LANES) == LANES
    if narrow and seq_n == 8 and res_n == 4:
        return fused_on_device(seq_n, res_n, *arrays)
    return scanned_on_device(*arrays)


def solution(mesh):
    in_specs = (
        P(("res", "seq"), None, None),
        P("seq", "res", None),
        P(("res", "seq"), None, None),
        P("seq", "res", None),
        P(),
        P(),
        P(),
        P(),
        P(),
        P(),
        P(),
        P(),
        P(),
        P(),
        P(),
        P(),
        P(),
        P(),
        P(),
    )
    out_specs = (P(("res", "seq"), None, None), P("seq", "res", None))
    return jax.shard_map(
        functools.partial(on_device, mesh.shape["seq"], mesh.shape["res"]),
        mesh=mesh, in_specs=in_specs, out_specs=out_specs, check_vma=False
    )
```
